128 devices in a mesh: dp: 4 (over x), ctx: 32 (over z, y, core).
Axes of the slice: x: 4, y: 4, z: 4, core: 2. Of those that a mesh axis runs over, the one named last changes fastest.
Arguments:
- mixer_input: bfloat16 [4, 4096, 10240], P('dp', 'ctx'), may hold values from -6 to 6
- step_raw: bfloat16 [4, 4096, 128], P('dp', 'ctx'), as said below
- out_grad: bfloat16 [4, 4096, 8192], P('dp', 'ctx'), may hold values from -0.59765625 to 0.59765625
- conv_weight: float32 [4, 10240], replicated, may hold values from -3 to 3
- conv_bias: float32 [10240], replicated, may hold values from -3 to 3
- step_bias: float32 [128], replicated, may hold values from -4 to -3
- decay_log: float32 [128], replicated, as said below
- skip_gain: float32 [128], replicated, may hold values from 0.5 to 1.5
Outputs:
- input_grad: bfloat16 [4, 4096, 10240], P('dp', 'ctx')
- step_grad: float32 [4, 4096, 128], P('dp', 'ctx')
- conv_grads: float32 [5, 10240], P(None, 'dp')
- head_grads: float32 [2, 128], P(None, 'dp')
- gain_grad: float32 [128], P('dp')
The draws below stay inside these ranges and needn't reach their ends.
Inputs may be any that keep to these rules, and one draw needn't show every extreme that they name: `step_raw`: raw step sizes of one device's positions share a per-head offset. `decay_log`: log magnitudes of the decay rates.
All inputs are finite; a program needn't handle non-finite values.
Results may differ from the reference program's by a relative error of at most 0.018.
Values may be sent and summed in bfloat16 or wider, within the bound.
A program may use at most 448 MiB of HBM per device.

```python
import math
import jax
import jax.numpy as jnp
from jax import lax

HEADS = 128
HEAD_DIM = 64
STATE = 128
GROUPS = 8
KERNEL = 4
BLOCK = 128
TOK_DEV = 128
INNER = 8192
CONV = 10240
SEQ = 4096
BATCH = 4
N_DP = 4
N_CTX = 32


def draw_step_raw(key, part):
    key = jax.random.fold_in(key, 1)
    base_key, offset_key = jax.random.split(key)
    base = 0.5 * jnp.clip(jax.random.normal(base_key, (BATCH, SEQ, HEADS), jnp.float32), -4.0, 4.0)
    offsets = jax.random.uniform(offset_key, (BATCH, SEQ // TOK_DEV, HEADS), jnp.float32, -0.7, 0.7)
    return (base + jnp.repeat(offsets, TOK_DEV, axis=1)).astype(jnp.bfloat16)


def draw_decay_log(key, part):
    key = jax.random.fold_in(key, 2)
    ranking_key, slow_key, medium_key, fast_key = jax.random.split(key, 4)
    ranking = jax.random.permutation(ranking_key, HEADS)
    slow_count = HEADS // 2
    medium_end = HEADS // 2 + HEADS // 4
    slow_rates = jnp.exp(jax.random.uniform(slow_key, (HEADS,), jnp.float32, math.log(0.3), math.log(2.0))) / (0.03 * SEQ)
    medium_rates = jnp.exp(jax.random.uniform(medium_key, (HEADS,), jnp.float32, math.log(1.0 / 50.0), math.log(1.0 / 30.0))) / 0.03
    fast_rates = jnp.exp(jax.random.uniform(fast_key, (HEADS,), jnp.float32, math.log(40.0), math.log(64.0)))
    chosen = jnp.where(ranking < slow_count, slow_rates, jnp.where(ranking < medium_end, medium_rates, fast_rates))
    return jnp.log(chosen)


def level_of(key, shape, shards, low, high):
    factor_of = 1.0
    for position, shards_of in shards:
        draws = jax.random.uniform(jax.random.fold_in(jax.random.fold_in(key, 6), position), (shards_of,), jnp.float32, low / len(shards), high / len(shards))
        factor_of = factor_of * jnp.repeat(jnp.exp(draws), shape[position] // shards_of).reshape((-1,) + (1,) * (len(shape) - 1 - position))
    return factor_of


def gaussian(rng, extent, scale, reach, cuts=(), dtype=jnp.bfloat16):
    drawn = jax.random.normal(rng, extent, jnp.float32) * scale
    if len(cuts) > 0:
        drawn = level_of(rng, extent, cuts, -0.22, 0.18) * drawn
    return jnp.clip(drawn, min=-reach, max=reach).astype(dtype)


def setup_inputs(seed: int = 0) -> dict:
    splits = jax.random.split(jax.random.key(seed), 9)
    return {
        "mixer_input": gaussian(splits[0], (BATCH, SEQ, CONV), 1.0, 6.0, ((0, 4), (1, 32))),
        "step_raw": draw_step_raw(jax.random.fold_in(splits[8], 71), 0),
        "out_grad": gaussian(splits[2], (BATCH, SEQ, INNER), 0.1, 0.59765625, ((0, 4), (1, 32))),
        "conv_weight": gaussian(splits[3], (KERNEL, CONV), KERNEL ** -0.5, 3.0, (), jnp.float32),
        "conv_bias": gaussian(splits[4], (CONV,), 0.5, 3.0, (), jnp.float32),
        "step_bias": jnp.clip(jax.random.uniform(splits[5], (HEADS,), jnp.float32, -4.0, -3.0), -4.0, -3.0),
        "decay_log": draw_decay_log(jax.random.fold_in(splits[8], 71), 0),
        "skip_gain": jnp.clip(jax.random.uniform(splits[7], (HEADS,), jnp.float32, 0.5, 1.5), 0.5, 1.5),
    }


FULL_PRECISION = lax.Precision.HIGHEST

def causal_conv(padded, conv_weight, conv_bias):
    kernel_len = conv_weight.shape[0]
    seq_len = padded.shape[0] - kernel_len + 1
    summed = jnp.broadcast_to(conv_bias[None, :], (seq_len, padded.shape[1]))
    for offset in range(kernel_len):
        summed = summed + conv_weight[offset][None, :] * padded[offset:offset + seq_len]
    return jax.nn.silu(summed)

def round_trip(values):
    return lax.optimization_barrier(values.astype(jnp.bfloat16)).astype(jnp.float32)

def ssd_core(x_rows, b_rows, c_rows, spread, rates, block_len):
    seq_len, block_count, block_heads, head_dim = x_rows.shape
    state_dim = b_rows.shape[2]
    part_count = seq_len // block_len
    x_parts = x_rows.reshape(part_count, block_len, block_count, block_heads, head_dim)
    b_parts = b_rows.reshape(part_count, block_len, block_count, state_dim)
    c_parts = c_rows.reshape(part_count, block_len, block_count, state_dim)
    step_parts = spread.reshape(part_count, block_len, block_count, block_heads)
    running = jnp.cumsum(step_parts * rates, axis=1)
    causal = jnp.arange(block_len)[:, None] >= jnp.arange(block_len)[None, :]
    gaps = running[:, :, None] - running[:, None, :]
    decays = jnp.exp(jnp.where(causal[None, :, :, None, None], gaps, -1e+30))
    scores = jnp.einsum('ctgn,csgn->ctsg', c_parts, b_parts, precision=FULL_PRECISION)
    weights = decays * scores[..., None] * step_parts[:, None]
    result = jnp.einsum('ctsgk,csgkp->ctgkp', weights, x_parts, precision=FULL_PRECISION)
    closing = running[:, -1]
    to_close = jnp.exp(closing[:, None] - running) * step_parts
    states = jnp.einsum('csgn,csgkp->cgknp', b_parts, x_parts * to_close[..., None], precision=FULL_PRECISION)
    after = jnp.cumsum(closing, axis=0)
    before = after - closing
    strict = jnp.arange(part_count)[:, None] > jnp.arange(part_count)[None, :]
    spans = before[:, None] - after[None, :]
    passing = jnp.exp(jnp.where(strict[:, :, None, None], spans, -1e+30))
    entering = jnp.einsum('cdgk,dgknp->cgknp', passing, states, precision=FULL_PRECISION)
    result = result + jnp.einsum('ctgn,cgknp->ctgkp', c_parts, entering, precision=FULL_PRECISION) * jnp.exp(running)[..., None]
    final_state = entering[-1] * jnp.exp(closing[-1])[..., None, None] + states[-1]
    return (result.reshape(seq_len, block_count, block_heads, head_dim), final_state, after[-1])

def head_block(pieces):
    x_block, b_block, c_block, spread_block, rate_block, gain_block, grad_block = pieces

    def one_head(items):
        x_head, spread_head, rate_head, grad_head = items

        def forward(x_vals, b_vals, c_vals, spread_vals, rate_vals):
            outputs = ssd_core(x_vals[:, None, None], b_vals[:, None], c_vals[:, None], spread_vals[:, None, None], rate_vals[None, None], BLOCK)
            return outputs[0][:, 0, 0]
        _, backward = jax.vjp(forward, x_head, b_block, c_block, spread_head, rate_head)
        return backward(grad_head)
    head_x, head_b, head_c, head_spread, head_rate = lax.map(one_head, (jnp.moveaxis(x_block, 1, 0), jnp.moveaxis(spread_block, 1, 0), rate_block, jnp.moveaxis(grad_block, 1, 0)))
    grad_x = jnp.moveaxis(head_x, 0, 1) + gain_block[None, :, None] * grad_block
    grad_b = lax.optimization_barrier(jnp.sum(head_b, axis=0))
    grad_c = lax.optimization_barrier(jnp.sum(head_c, axis=0))
    grad_spread = jnp.moveaxis(head_spread, 0, 1)
    grad_gain = lax.optimization_barrier(jnp.sum(grad_block * x_block, axis=(0, 2)))
    return (grad_x, grad_b, grad_c, grad_spread, head_rate, grad_gain)

def reference(mixer_input, step_raw, out_grad, conv_weight, conv_bias, step_bias, decay_log, skip_gain):
    per_device = HEADS // N_CTX
    group_copies = N_CTX // GROUPS
    group_width = GROUPS * STATE
    rates = -jnp.exp(decay_log)

    def one_sequence(pieces):
        seq_input, seq_raw, seq_grad = pieces
        padded = jnp.concatenate([jnp.zeros((KERNEL - 1, CONV), jnp.float32), seq_input.astype(jnp.float32)], axis=0)
        activated, conv_back = jax.vjp(causal_conv, padded, conv_weight, conv_bias)
        mixed = round_trip(activated)
        x_all = mixed[:, :INNER].reshape(SEQ, N_CTX, per_device, HEAD_DIM)
        b_all = jnp.repeat(mixed[:, INNER:INNER + group_width].reshape(SEQ, GROUPS, STATE), group_copies, axis=1)
        c_all = jnp.repeat(mixed[:, INNER + group_width:].reshape(SEQ, GROUPS, STATE), group_copies, axis=1)
        gate_in = seq_raw.astype(jnp.float32) + step_bias[None, :]
        spread = jax.nn.softplus(gate_in)
        grads_in = seq_grad.astype(jnp.float32).reshape(SEQ, N_CTX, per_device, HEAD_DIM)
        mapped = (jnp.moveaxis(x_all, 1, 0), jnp.moveaxis(b_all, 1, 0), jnp.moveaxis(c_all, 1, 0), jnp.moveaxis(spread.reshape(SEQ, N_CTX, per_device), 1, 0), rates.reshape(N_CTX, per_device), skip_gain.reshape(N_CTX, per_device), jnp.moveaxis(grads_in, 1, 0))
        grad_x, grad_b, grad_c, grad_spread, grad_rate, grad_gain = lax.map(head_block, mapped)
        grad_inner = round_trip(jnp.moveaxis(grad_x, 0, 1)).reshape(SEQ, INNER)
        sum_b = lax.optimization_barrier(jnp.sum(round_trip(grad_b).reshape(GROUPS, group_copies, SEQ, STATE), axis=1))
        sum_c = lax.optimization_barrier(jnp.sum(round_trip(grad_c).reshape(GROUPS, group_copies, SEQ, STATE), axis=1))
        grad_bgroups = jnp.moveaxis(sum_b, 0, 1).reshape(SEQ, group_width)
        grad_cgroups = jnp.moveaxis(sum_c, 0, 1).reshape(SEQ, group_width)
        grad_steps = round_trip(jnp.moveaxis(grad_spread, 0, 1).reshape(SEQ, HEADS))
        seq_step_grad = grad_steps * jax.nn.sigmoid(gate_in)
        grad_mixed = jnp.concatenate([grad_inner, grad_bgroups, grad_cgroups], axis=1)
        grad_pad, grad_weight, grad_bias = conv_back(grad_mixed)
        seq_input_grad = grad_pad[KERNEL - 1:].astype(jnp.bfloat16)
        conv_part = jnp.concatenate([grad_weight, grad_bias[None, :]], axis=0)
        head_part = jnp.stack([grad_rate.reshape(HEADS) * rates, lax.optimization_barrier(jnp.sum(seq_step_grad, axis=0)), grad_gain.reshape(HEADS)])
        return (seq_input_grad, seq_step_grad, conv_part, head_part)
    input_grad, step_grad, conv_parts, head_parts = lax.map(one_sequence, (mixer_input, step_raw, out_grad))
    factor = 1.0 / math.sqrt(N_DP * SEQ)
    head_total = lax.optimization_barrier(jnp.sum(head_parts, axis=0)) * factor
    return (input_grad, step_grad, lax.optimization_barrier(jnp.sum(conv_parts, axis=0)) * factor, head_total[:2], head_total[2])
```

```python
import functools
import math

import jax
import jax.numpy as jnp
from jax import lax
from jax.experimental import pallas as pl
from jax.experimental.pallas import tpu as pltpu
from jax.sharding import PartitionSpec as P

HEADS = 128
HEAD_DIM = 64
STATE = 128
GROUPS = 8
KERNEL = 4
ROWS = 128
INNER = 8192
CONV = 10240
GROUP_HEADS = HEADS // GROUPS
GROUP_PAIRS = GROUP_HEADS // 2
GROUP_LANES = GROUP_HEADS * HEAD_DIM
PAIRS = HEADS // 2
HALF = PAIRS // 2
MESH = pl.DeviceIdType.MESH
F32 = jnp.float32
BF16 = jnp.bfloat16
EXACT = lax.Precision.HIGHEST


def dot(a, b, precision=None):
    return jnp.dot(a, b, precision=precision, preferred_element_type=F32)


def dot_nt(a, b):
    return lax.dot_general(a, b, (((1,), (1,)), ((), ())), preferred_element_type=F32)


def sigmoid(v):
    return 0.5 + 0.5 * jnp.tanh(0.5 * v)


def softplus(v):
    return jnp.maximum(v, 0.0) + jnp.log1p(jnp.exp(-jnp.abs(v)))


def iota(shape, dim):
    return lax.broadcasted_iota(jnp.int32, shape, dim)


def low_half(shape):
    return iota(shape, len(shape) - 1) < HEAD_DIM


def pair_of(columns, j):
    shape = (columns.shape[0], 2 * HEAD_DIM)
    first = jnp.broadcast_to(columns[:, 2 * j : 2 * j + 1], shape)
    second = jnp.broadcast_to(columns[:, 2 * j + 1 : 2 * j + 2], shape)
    return jnp.where(low_half(shape), first, second)


def conv_pre(pad, tile_ref, halo_ref, taps_ref, lanes):
    pad[0:8, :] = halo_ref[:, lanes]
    pad[8:, :] = tile_ref[:, lanes].astype(F32)
    pre = jnp.broadcast_to(taps_ref[4:5, lanes], (ROWS, 128))
    for k in range(KERNEL):
        pre = pre + taps_ref[k : k + 1, lanes] * pad[5 + k : 5 + k + ROWS, :]
    return pre


def states_kernel(
    x_ref, b_ref, c_ref, hx_ref, hb_ref, hc_ref, tx_ref, tb_ref, tc_ref, raw_ref, bias_ref, rate_ref, dy_ref,
    xm_ref, bm_ref, cm_ref, s_ref, g_ref, a_ref, run_ref, run_t_ref, sp_ref,
    pad,
):
    g = pl.program_id(0)

    @pl.when(g == 0)
    def _():
        spread = softplus(raw_ref[...].astype(F32) + bias_ref[...])
        shape = (ROWS, ROWS)
        lower = jnp.where(iota(shape, 0) >= iota(shape, 1), 1.0, 0.0).astype(F32)
        running = dot(lower, spread * rate_ref[...], EXACT)
        sp_ref[...] = spread
        run_ref[...] = running
        run_t_ref[...] = running.T

    def mixed(slot, tile_ref, halo_ref, taps_ref, lanes):
        pre = conv_pre(pad.at[slot], tile_ref, halo_ref, taps_ref, lanes)
        return (pre * sigmoid(pre)).astype(BF16)

    whole = pl.ds(0, 128)
    b16 = mixed(GROUP_PAIRS, b_ref, hb_ref, tb_ref, whole)
    c16 = mixed(GROUP_PAIRS + 1, c_ref, hc_ref, tc_ref, whole)
    bm_ref[0] = b16
    cm_ref[0] = c16
    b_t = b16.astype(F32).T.astype(BF16)
    c_t = c16.astype(F32).T.astype(BF16)
    back = lax.rem(HEADS - GROUP_HEADS * g, HEADS)
    run = pltpu.roll(run_ref[...], back, 1)
    spread = pltpu.roll(sp_ref[...], back, 1)
    closing = run[ROWS - 1 : ROWS, :]
    grown = jnp.exp(run)
    to_close = jnp.exp(closing - run) * spread
    whole_decay = jnp.exp(closing)
    for j in range(GROUP_PAIRS):
        lanes = pl.ds(128 * j, 128)
        x16 = mixed(j, x_ref, hx_ref, tx_ref, lanes)
        xm_ref[:, lanes] = x16
        s_ref[j] = dot(b_t, (x16.astype(F32) * pair_of(to_close, j)).astype(BF16)).astype(BF16)
        g_ref[j] = dot(c_t, (dy_ref[:, lanes].astype(F32) * pair_of(grown, j)).astype(BF16)).astype(BF16)
        a_ref[j] = pair_of(whole_decay, j)


def full(shape):
    return pl.BlockSpec(shape, lambda g: (0,) * len(shape))


def channel_specs(rows):
    return [
        pl.BlockSpec((rows, GROUP_LANES), lambda g: (0, g)),
        pl.BlockSpec((rows, STATE), lambda g: (0, INNER // STATE + g)),
        pl.BlockSpec((rows, STATE), lambda g: (0, INNER // STATE + GROUPS + g)),
    ]


def states(mixer, halo, taps, raw, bias, rate, dy):
    square = jax.ShapeDtypeStruct((ROWS, HEADS), F32)
    group = jax.ShapeDtypeStruct((GROUPS, ROWS, STATE), BF16)
    state = jax.ShapeDtypeStruct((PAIRS, STATE, 128), BF16)
    group_spec = pl.BlockSpec((1, ROWS, STATE), lambda g: (g, 0, 0))
    state_spec = pl.BlockSpec((GROUP_PAIRS, STATE, 128), lambda g: (g, 0, 0))
    x_spec = pl.BlockSpec((ROWS, GROUP_LANES), lambda g: (0, g))
    return pl.pallas_call(
        states_kernel,
        grid=(GROUPS,),
        in_specs=channel_specs(ROWS) + channel_specs(8) + channel_specs(8)
        + [full((ROWS, HEADS)), full((1, HEADS)), full((1, HEADS)), x_spec],
        out_specs=[
            x_spec, group_spec, group_spec, state_spec, state_spec,
            pl.BlockSpec((GROUP_PAIRS, 1, 128), lambda g: (g, 0, 0)),
            full((ROWS, HEADS)), full((HEADS, ROWS)), full((ROWS, HEADS)),
        ],
        out_shape=[
            jax.ShapeDtypeStruct((ROWS, INNER), BF16), group, group, state, state,
            jax.ShapeDtypeStruct((PAIRS, 1, 128), F32), square, square, square,
        ],
        scratch_shapes=[pltpu.VMEM((GROUP_PAIRS + 2, ROWS + 8, 128), F32)],
        compiler_params=pltpu.CompilerParams(vmem_limit_bytes=40 << 20),
        name="states",
    )(mixer, mixer, mixer, halo, halo, halo, taps, taps, taps, raw, bias, rate, dy)


def pass_kernel(
    s_ref, g_ref, a_ref, h_ref, l_ref,
    s_oth, g_oth, a_oth, s_out, g_out, a_out, s_in, g_in, a_in, h_out, l_out, h_in, l_in, h_oth, l_oth,
    x_send, x_recv, s_send, s_recv, g_send, g_recv, a_send, a_recv, h_send, h_recv, l_send, l_recv, o_send, o_recv,
):
    dp = lax.axis_index("dp")
    ctx = lax.axis_index("ctx")
    core = lax.rem(ctx, 2)
    chip = ctx // 2
    z, y = chip // 4, lax.rem(chip, 4)
    chips = lax.axis_size("ctx") // 2
    own = HALF // chips
    other = ctx + 1 - 2 * core
    mine = core * HALF
    theirs = HALF - mine

    def chip_at(r):
        return lax.rem(z + r // 4, 4) * 4 + lax.rem(y + r, 4)

    def device_at(r):
        return chip_at(r) * 2 + core

    barrier = pltpu.get_barrier_semaphore()
    pl.semaphore_signal(barrier, inc=1, device_id=(dp, other), device_id_type=MESH)

    def greet(r, _):
        pl.semaphore_signal(barrier, inc=1, device_id=(dp, device_at(r)), device_id_type=MESH)
        return 0

    lax.fori_loop(1, chips, greet, 0)
    pl.semaphore_wait(barrier, chips)

    def remote(src, dst, send, recv, device):
        return pltpu.make_async_remote_copy(
            src_ref=src, dst_ref=dst, send_sem=send, recv_sem=recv, device_id=(dp, device), device_id_type=MESH
        )

    swaps = [
        remote(src.at[pl.ds(theirs, HALF)], dst, x_send.at[i], x_recv.at[i], other)
        for i, (src, dst) in enumerate(((a_ref, a_oth), (s_ref, s_oth), (g_ref, g_oth)))
    ]
    for copy in swaps:
        copy.start()
    for copy in swaps:
        copy.wait()

    first = core == 0

    def ordered(held, sent):
        return jnp.where(first, held, sent), jnp.where(first, sent, held)

    def decays(at):
        return ordered(a_ref[pl.ds(mine + at, own)], a_oth[pl.ds(at, own)])

    def values(ref, oth, at):
        return ordered(ref[pl.ds(mine + at, own)].astype(F32), oth[pl.ds(at, own)].astype(F32))

    def out_copies(r):
        chosen = chip_at(r)
        at = pl.ds(chosen * own, own)
        device = device_at(r)
        return (
            remote(a_out.at[at], a_in.at[chip], a_send.at[r], a_recv.at[r], device),
            remote(s_out.at[at], s_in.at[chip], s_send.at[r], s_recv.at[r], device),
            remote(g_out.at[at], g_in.at[chip], g_send.at[r], g_recv.at[r], device),
        )

    def combine(r, _):
        at = chip_at(r) * own
        a0, a1 = decays(at)
        s0, s1 = values(s_ref, s_oth, at)
        g0, g1 = values(g_ref, g_oth, at)
        a_out[pl.ds(at, own)] = a0 * a1
        s_out[pl.ds(at, own)] = (a1 * s0 + s1).astype(BF16)
        g_out[pl.ds(at, own)] = (a0 * g1 + g0).astype(BF16)

        @pl.when(r > 0)
        def _():
            for copy in out_copies(r):
                copy.start()

        return 0

    lax.fori_loop(0, chips, combine, 0)
    at_own = pl.ds(chip * own, own)
    a_in[chip] = a_out[at_own]
    s_in[chip] = s_out[at_own]
    g_in[chip] = g_out[at_own]

    def arrived(r, _):
        for copy in out_copies(r):
            copy.wait_recv()
        return 0

    lax.fori_loop(1, chips, arrived, 0)

    def forth(c, state):
        h_out[c] = state.astype(BF16)
        return a_in[c] * state + s_in[c].astype(F32)

    def back(i, state):
        c = chips - 1 - i
        l_out[c] = state.astype(BF16)
        return a_in[c] * state + g_in[c].astype(F32)

    zero = jnp.zeros((own, STATE, 128), F32)
    lax.fori_loop(0, chips, forth, zero)
    lax.fori_loop(0, chips, back, zero)

    def home_copies(r):
        chosen = chip_at(r)
        device = device_at(r)
        return (
            remote(h_out.at[chosen], h_in.at[pl.ds(chip * own, own)], h_send.at[r], h_recv.at[r], device),
            remote(l_out.at[chosen], l_in.at[pl.ds(chip * own, own)], l_send.at[r], l_recv.at[r], device),
        )

    def send_home(r, _):
        for copy in home_copies(r):
            copy.start()
        return 0

    lax.fori_loop(1, chips, send_home, 0)
    h_in[at_own] = h_out[chip]
    l_in[at_own] = l_out[chip]

    def finish(r, _):
        source = lax.rem(z + 4 - r // 4, 4) * 4 + lax.rem(y + 4 - lax.rem(r, 4), 4)

        @pl.when(r > 0)
        def _():
            for copy in home_copies(r):
                copy.wait_recv()

        at = source * own
        here = pl.ds(at, own)
        held = pl.ds(mine + at, own)
        a0, a1 = decays(at)
        s0, _ = values(s_ref, s_oth, at)
        _, g1 = values(g_ref, g_oth, at)
        h0 = h_in[here]
        h1 = (a0 * h0.astype(F32) + s0).astype(BF16)
        l1 = l_in[here]
        l0 = (a1 * l1.astype(F32) + g1).astype(BF16)
        h_ref[held] = jnp.where(first, h0, h1)
        h_oth[here] = jnp.where(first, h1, h0)
        l_ref[held] = jnp.where(first, l0, l1)
        l_oth[here] = jnp.where(first, l1, l0)
        return 0

    lax.fori_loop(0, chips, finish, 0)
    lasts = [
        remote(src, dst.at[pl.ds(mine, HALF)], o_send.at[i], o_recv.at[i], other)
        for i, (src, dst) in enumerate(((h_oth, h_ref), (l_oth, l_ref)))
    ]
    for copy in lasts:
        copy.start()

    def sent(r, _):
        for copy in out_copies(r) + home_copies(r):
            copy.wait_send()
        return 0

    lax.fori_loop(1, chips, sent, 0)
    for copy in lasts:
        copy.wait()


def pass_states(s, g, a):
    chips = lax.axis_size("ctx") // 2
    own = HALF // chips
    wide = pltpu.VMEM((HALF, STATE, 128), BF16)
    split = pltpu.VMEM((chips, own, STATE, 128), BF16)
    row = pltpu.VMEM((HALF, 1, 128), F32)
    many = pltpu.SemaphoreType.DMA((chips,))
    memory = pl.BlockSpec(memory_space=pltpu.VMEM)
    return pl.pallas_call(
        pass_kernel,
        out_shape=[jax.ShapeDtypeStruct((PAIRS, STATE, 128), BF16)] * 2,
        in_specs=[memory] * 3,
        out_specs=[memory] * 2,
        scratch_shapes=[
            wide, wide, row, wide, wide, row, split, split, pltpu.VMEM((chips, own, 1, 128), F32),
            split, split, wide, wide, wide, wide,
            pltpu.SemaphoreType.DMA((3,)), pltpu.SemaphoreType.DMA((3,)),
        ] + [many] * 10 + [pltpu.SemaphoreType.DMA((2,)), pltpu.SemaphoreType.DMA((2,))],
        compiler_params=pltpu.CompilerParams(
            collective_id=0, has_side_effects=True, vmem_limit_bytes=48 << 20
        ),
        name="pass_states",
    )(s, g, a)


def grads_kernel(
    x_ref, b_ref, c_ref, hx_ref, hb_ref, hc_ref, tx_ref, tb_ref, tc_ref, raw_ref, bias_ref, rate_ref, dy_ref,
    gain_ref, xm_ref, bm_ref, cm_ref, h_ref, l_ref, run_ref, run_t_ref, sp_ref,
    ig_ref, last_ref, spill_ref, taps_out, step_ref, rows_ref,
    pad, dpad, dsc, acc_b, acc_c, col_u, col_q, col_s, row_g, full_u, full_q, full_s, full_r, full_g,
):
    g = pl.program_id(0)
    back = lax.rem(HEADS - GROUP_HEADS * g, HEADS)
    shape = (ROWS, ROWS)

    @pl.when(g == 0)
    def _():
        dpad[:, ROWS:, :] = jnp.zeros((GROUP_PAIRS + 2, 8, 128), F32)
        for ref in (full_u, full_q, full_s, full_g, col_u, col_q, col_s, row_g):
            ref[...] = jnp.zeros(ref.shape, F32)

    b16, c16 = bm_ref[0], cm_ref[0]
    scores = jnp.where(iota(shape, 1) >= iota(shape, 0), dot_nt(b16, c16), 0.0)
    run = pltpu.roll(run_ref[...], back, 1)
    spread = pltpu.roll(sp_ref[...], back, 1)
    grown = jnp.exp(run)
    to_close = jnp.exp(run[ROWS - 1 : ROWS, :] - run) * spread
    low = low_half(shape)
    low_row = low_half((1, 128))
    dsc[...] = jnp.zeros(shape, F32)
    acc_b[...] = jnp.zeros(shape, F32)
    acc_c[...] = jnp.zeros(shape, F32)

    def conv_back(slot, grad, tile_ref, halo_ref, taps_ref, lanes, out):
        here = pad.at[slot]
        there = dpad.at[slot]
        pre = conv_pre(here, tile_ref, halo_ref, taps_ref, lanes)
        gate = sigmoid(pre)
        dpre = grad * (gate * (1.0 + pre * (1.0 - gate)))
        there[0:ROWS, :] = dpre
        whole = jnp.zeros(shape, F32)
        for k in range(KERNEL):
            whole = whole + taps_ref[k : k + 1, lanes] * there[3 - k : 3 - k + ROWS, :]
            taps_out[k : k + 1, out] = jnp.sum(dpre * here[5 + k : 5 + k + ROWS, :], axis=0, keepdims=True)
        taps_out[4:5, out] = jnp.sum(dpre, axis=0, keepdims=True)
        taps_out[5:8, out] = jnp.zeros((3, 128), F32)
        ig_ref[:, out] = whole.astype(BF16)
        last_ref[:, out] = whole[ROWS - 8 :, :]
        head = dpre[0:8, :]
        row = iota((8, 128), 0)
        spilled = jnp.zeros((8, 128), F32)
        for k in range(KERNEL - 1):
            moved = pltpu.roll(head, 5 + k, 0)
            spilled = spilled + jnp.where(row >= 5 + k, taps_ref[k : k + 1, lanes] * moved, 0.0)
        spill_ref[:, out] = spilled

    for j in range(GROUP_PAIRS):
        lanes = pl.ds(128 * j, 128)
        x16 = xm_ref[:, lanes]
        x = x16.astype(F32)
        dy = dy_ref[:, lanes].astype(F32)
        split = jnp.concatenate([jnp.where(low, dy, 0.0), jnp.where(low, 0.0, dy)], axis=0).astype(BF16)
        d_weights = dot_nt(x16, split)
        weights = []
        for i in range(2):
            head = 2 * j + i
            at = GROUP_HEADS * g + head
            step = spread[:, head : head + 1]
            d_weight = d_weights[:, 128 * i : 128 * i + 128]
            decay = jnp.exp(jnp.minimum(run_t_ref[pl.ds(at, 1), :] - run[:, head : head + 1], 0.0))
            plain = decay * scores
            weights.append((plain * step).astype(BF16))
            product = d_weight * plain
            col_s[:, head : head + 1] = jnp.sum(product, axis=1, keepdims=True)
            full_r[pl.ds(at, 1), :] = jnp.sum(product * step, axis=0, keepdims=True)
            dsc[...] += d_weight * decay * step
        h16, l16 = h_ref[j], l_ref[j]
        grown_2 = pair_of(grown, j)
        close_2 = pair_of(to_close, j)
        entered = dy * dot(c16, h16)
        left = dot(b16, l16)
        used = x * left
        for i in range(2):
            head = 2 * j + i
            mask = low if i == 0 else jnp.logical_not(low)
            mask_row = low_row if i == 0 else jnp.logical_not(low_row)
            col_u[:, head : head + 1] = jnp.sum(jnp.where(mask, entered, 0.0), axis=1, keepdims=True)
            col_q[:, head : head + 1] = jnp.sum(jnp.where(mask, used, 0.0), axis=1, keepdims=True)
            crossed = jnp.sum(h16.astype(F32) * l16.astype(F32), axis=0, keepdims=True)
            gained = jnp.sum(dy * x, axis=0, keepdims=True)
            row_g[0:1, head : head + 1] = jnp.sum(jnp.where(mask_row, crossed, 0.0), axis=1, keepdims=True)
            row_g[1:2, head : head + 1] = jnp.sum(jnp.where(mask_row, gained, 0.0), axis=1, keepdims=True)
        acc_c[...] += dot_nt((dy * grown_2).astype(BF16), h16)
        acc_b[...] += dot_nt((x * close_2).astype(BF16), l16)
        grad_x = dot(jnp.concatenate(weights, axis=1), split) + close_2 * left + gain_ref[0, :, lanes] * dy
        conv_back(j, grad_x, x_ref, hx_ref, tx_ref, lanes, pl.ds(pl.multiple_of(g * GROUP_LANES + 128 * j, 128), 128))

    d_scores = jnp.where(iota(shape, 1) >= iota(shape, 0), dsc[...], 0.0)
    grad_b = acc_b[...] + dot(d_scores.astype(BF16), c16)
    grad_c = acc_c[...] + dot(d_scores.T.astype(BF16), b16)
    every = pl.ds(0, 128)
    conv_back(GROUP_PAIRS, grad_b, b_ref, hb_ref, tb_ref, every, pl.ds(pl.multiple_of(INNER + 128 * g, 128), 128))
    conv_back(
        GROUP_PAIRS + 1, grad_c, c_ref, hc_ref, tc_ref, every,
        pl.ds(pl.multiple_of(INNER + GROUPS * STATE + 128 * g, 128), 128),
    )

    forward = lax.rem(GROUP_HEADS * g, HEADS)
    for whole_ref, part_ref in ((full_u, col_u), (full_q, col_q), (full_s, col_s), (full_g, row_g)):
        lane = iota(part_ref.shape, 1)
        whole_ref[...] += pltpu.roll(jnp.where(lane < GROUP_HEADS, part_ref[...], 0.0), forward, 1)

    @pl.when(g == GROUPS - 1)
    def _():
        running, steps = run_ref[...], sp_ref[...]
        rate = rate_ref[...]
        closing = running[ROWS - 1 : ROWS, :]
        from_close = jnp.exp(closing - running)
        direct_q = from_close * full_q[...]
        used_q = direct_q * steps
        summed = full_r[...].T + jnp.exp(running) * full_u[...] - full_s[...] * steps - used_q
        upper = jnp.where(iota(shape, 1) >= iota(shape, 0), 1.0, 0.0).astype(F32)
        constant = jnp.sum(used_q, axis=0, keepdims=True) + jnp.exp(closing) * full_g[0:1, :]
        d_logs = dot(upper, summed, EXACT) + constant
        d_spread = (d_logs * rate + full_s[...] + direct_q).astype(BF16).astype(F32)
        step_grad = d_spread * sigmoid(raw_ref[...].astype(F32) + bias_ref[...])
        step_ref[...] = step_grad
        rows_ref[...] = jnp.zeros((8, HEADS), F32)
        rows_ref[0:1, :] = rate * jnp.sum(d_logs * steps, axis=0, keepdims=True)
        rows_ref[1:2, :] = jnp.sum(step_grad, axis=0, keepdims=True)
        rows_ref[2:3, :] = full_g[1:2, :]


def grads(mixer, halo, taps, raw, bias, rate, dy, gain, xm, bm, cm, h, l, run, run_t, sp):
    x_spec = pl.BlockSpec((ROWS, GROUP_LANES), lambda g: (0, g))
    group_spec = pl.BlockSpec((1, ROWS, STATE), lambda g: (g, 0, 0))
    state_spec = pl.BlockSpec((GROUP_PAIRS, STATE, 128), lambda g: (g, 0, 0))
    square = full((ROWS, HEADS))
    plane = pltpu.VMEM((ROWS, 128), F32)
    tall = pltpu.VMEM((GROUP_PAIRS + 2, ROWS + 8, 128), F32)
    rows = pltpu.VMEM((8, 128), F32)
    edge = jax.ShapeDtypeStruct((8, CONV), F32)
    return pl.pallas_call(
        grads_kernel,
        grid=(GROUPS,),
        in_specs=channel_specs(ROWS) + channel_specs(8) + channel_specs(8)
        + [square, full((1, HEADS)), full((1, HEADS)), x_spec]
        + [pl.BlockSpec((1, 1, GROUP_LANES), lambda g: (g, 0, 0)), x_spec, group_spec, group_spec]
        + [state_spec, state_spec, square, square, square],
        out_specs=[full((ROWS, CONV))] + [full((8, CONV))] * 3 + [square, full((8, HEADS))],
        out_shape=[
            jax.ShapeDtypeStruct((ROWS, CONV), BF16), edge, edge, edge,
            jax.ShapeDtypeStruct((ROWS, HEADS), F32), jax.ShapeDtypeStruct((8, HEADS), F32),
        ],
        scratch_shapes=[tall, tall] + [plane] * 6 + [rows] + [plane] * 4 + [rows],
        compiler_params=pltpu.CompilerParams(vmem_limit_bytes=48 << 20),
        name="grads",
    )(
        mixer, mixer, mixer, halo, halo, halo, taps, taps, taps, raw, bias, rate, dy,
        gain, xm, bm, cm, h, l, run, run_t, sp,
    )


def passed_along(value, axis, steps):
    count = lax.axis_size(axis)
    initial, last = (max(0, -steps), min(count, count - steps))
    return lax.ppermute(value, axis, [(source, source + steps) for source in range(initial, last)])


def local(mixer_input, step_raw, out_grad, conv_weight, conv_bias, step_bias, decay_log, skip_gain):
    mixer, raw, dy = mixer_input[0], step_raw[0], out_grad[0]
    halo = passed_along(mixer[ROWS - 8 :], "ctx", 1).astype(F32)
    taps = jnp.concatenate([conv_weight, conv_bias[None], jnp.zeros((3, CONV), F32)], axis=0)
    bias = step_bias[None]
    rate = -jnp.exp(decay_log)[None]
    gain = jnp.repeat(skip_gain, HEAD_DIM).reshape(GROUPS, 1, GROUP_LANES)
    xm, bm, cm, s, g, a, run, run_t, sp = states(mixer, halo, taps, raw, bias, rate, dy)
    h, l = pass_states(s, g, a)
    input_grad, last, spill, taps_grad, step_grad, rows = grads(
        mixer, halo, taps, raw, bias, rate, dy, gain, xm, bm, cm, h, l, run, run_t, sp
    )
    spilled = passed_along(spill.astype(BF16), "ctx", -1).astype(F32)
    input_grad = lax.dynamic_update_slice(input_grad, (last + spilled).astype(BF16), (ROWS - 8, 0))
    factor = 1.0 / math.sqrt(lax.axis_size("dp") * ROWS * lax.axis_size("ctx"))
    conv_share = lax.psum_scatter(taps_grad[: KERNEL + 1], "dp", scatter_dimension=1, tiled=True)
    head_share = lax.psum_scatter(rows[:3], "dp", scatter_dimension=1, tiled=True)
    conv_total, head_total = lax.psum((conv_share, head_share), "ctx")
    return (
        input_grad[None],
        step_grad[None],
        conv_total * factor,
        head_total[:2] * factor,
        head_total[2] * factor,
    )


def solution(mesh):
    spread = P("dp", "ctx", None)
    in_specs = (spread, spread, spread, P(), P(), P(), P(), P())
    out_specs = (spread, spread, P(None, "dp"), P(None, "dp"), P("dp"))
    return jax.shard_map(local, mesh=mesh, in_specs=in_specs, out_specs=out_specs, check_vma=False)
```

```python
import functools
import math

import jax
import jax.numpy as jnp
from jax import lax
from jax.experimental import pallas as pl
from jax.experimental.pallas import tpu as pltpu
from jax.sharding import PartitionSpec as P

HEADS = 128
HEAD_DIM = 64
STATE = 128
GROUPS = 8
KERNEL = 4
ROWS = 128
INNER = 8192
CONV = 10240
GROUP_HEADS = HEADS // GROUPS
GROUP_PAIRS = GROUP_HEADS // 2
GROUP_LANES = GROUP_HEADS * HEAD_DIM
PAIRS = HEADS // 2
HALF = PAIRS // 2
MESH = pl.DeviceIdType.MESH
F32 = jnp.float32
BF16 = jnp.bfloat16
VMEM = 60 << 20
EARLY, MIDDLE, LATE = 12, 32, 44
EXACT = lax.Precision.HIGHEST


def dot(a, b, precision=None):
    return jnp.dot(a, b, precision=precision, preferred_element_type=F32)


def dot_nt(a, b):
    return lax.dot_general(a, b, (((1,), (1,)), ((), ())), preferred_element_type=F32)


def sigmoid(v):
    return 0.5 + 0.5 * jnp.tanh(0.5 * v)


def softplus(v):
    return jnp.maximum(v, 0.0) + jnp.log1p(jnp.exp(-jnp.abs(v)))


def iota(shape, dim):
    return lax.broadcasted_iota(jnp.int32, shape, dim)


def low_half(shape):
    return iota(shape, len(shape) - 1) < HEAD_DIM


def pair_of(columns, j):
    shape = (columns.shape[0], 2 * HEAD_DIM)
    first = jnp.broadcast_to(columns[:, 2 * j : 2 * j + 1], shape)
    second = jnp.broadcast_to(columns[:, 2 * j + 1 : 2 * j + 2], shape)
    return jnp.where(low_half(shape), first, second)


def conv_pre(pad, tile_ref, halo_ref, taps_ref, lanes):
    pad[0:8, :] = halo_ref[:, lanes]
    pad[8:, :] = tile_ref[:, lanes].astype(F32)
    pre = jnp.broadcast_to(taps_ref[4:5, lanes], (ROWS, 128))
    for k in range(KERNEL):
        pre = pre + taps_ref[k : k + 1, lanes] * pad[5 + k : 5 + k + ROWS, :]
    return pre


def full(shape):
    return pl.BlockSpec(shape, lambda g: (0,) * len(shape))


def channel_specs(rows):
    return [
        pl.BlockSpec((rows, GROUP_LANES), lambda g: (0, g)),
        pl.BlockSpec((rows, STATE), lambda g: (0, INNER // STATE + g)),
        pl.BlockSpec((rows, STATE), lambda g: (0, INNER // STATE + GROUPS + g)),
    ]


def front_kernel(
    mix_ref, halo_ref, taps_ref, raw_ref, bias_ref, rate_ref, dy_ref,
    bm_ref, cm_ref, dxi_ref, dsc_ref, h_ref, l_ref, run_ref, run_t_ref, sp_ref, sum_s_ref, sum_r_ref,
    pad, xm, scores, s_own, g_own, a_own, s_oth, g_oth, a_oth, s_out, g_out, a_out, s_in, g_in, a_in, g_mid,
    h_out, l_out, h_in, l_in, l_mid, h_oth, l_oth,
    x_send, x_recv, y_send, y_recv, z_send, z_recv, a_send, a_recv, s_send, s_recv, g_send, g_recv,
    gm_send, gm_recv, h_send, h_recv, l_send, l_recv, lm_send, lm_recv, p_send, p_recv, q_send, q_recv,
):
    dp = lax.axis_index("dp")
    ctx = lax.axis_index("ctx")
    core = lax.rem(ctx, 2)
    chip = ctx // 2
    z, y = chip // 4, lax.rem(chip, 4)
    chips = lax.axis_size("ctx") // 2
    own = HALF // chips
    other = ctx + 1 - 2 * core
    mine = core * HALF
    theirs = HALF - mine
    half_groups = GROUPS // 2
    shape = (ROWS, ROWS)
    first = core == 0

    def chip_at(r):
        return lax.rem(z + r // 4, 4) * 4 + lax.rem(y + r, 4)

    def chip_before(r):
        return lax.rem(z + 4 - r // 4, 4) * 4 + lax.rem(y + 4 - lax.rem(r, 4), 4)

    def tied(r):
        return (lax.rem(r, 4) == 2) | (r // 4 == 2)

    def below(r):
        return jnp.where(r // 4 == 2, 1, 0), jnp.where(lax.rem(r, 4) == 2, 1, 0)

    def mid_at(r):
        dz, dy = below(r)
        return lax.rem(z + 4 - dz, 4) * 4 + lax.rem(y + 4 - dy, 4)

    def mid_source(r):
        dz, dy = below(r)
        return lax.rem(z + dz, 4) * 4 + lax.rem(y + dy, 4)

    def mid_target(r):
        dz, dy = below(r)
        return lax.rem(z + dz + r // 4, 4) * 4 + lax.rem(y + dy + r, 4)

    barrier = pltpu.get_barrier_semaphore()
    pl.semaphore_signal(barrier, inc=1, device_id=(dp, other), device_id_type=MESH)

    def greet(r, _):
        pl.semaphore_signal(barrier, inc=1, device_id=(dp, chip_at(r) * 2 + core), device_id_type=MESH)
        return 0

    lax.fori_loop(1, chips, greet, 0)

    def remote(src, dst, send, recv, device):
        return pltpu.make_async_remote_copy(
            src_ref=src, dst_ref=dst, send_sem=send, recv_sem=recv, device_id=(dp, device), device_id_type=MESH
        )

    spread = softplus(raw_ref[...].astype(F32) + bias_ref[...])
    lower = jnp.where(iota(shape, 0) >= iota(shape, 1), 1.0, 0.0).astype(F32)
    running = dot(lower, spread * rate_ref[...], EXACT)
    sp_ref[...] = spread
    run_ref[...] = running
    run_t_ref[...] = running.T
    sum_s_ref[...] = jnp.zeros((ROWS, HEADS), F32)

    def mixed(slot, lanes):
        here = pad.at[slot]
        here[0:8, :] = halo_ref[:, lanes]
        here[8:, :] = mix_ref[:, lanes].astype(F32)
        pre = jnp.broadcast_to(taps_ref[4:5, lanes], (ROWS, 128))
        for k in range(KERNEL):
            pre = pre + taps_ref[k : k + 1, lanes] * here[5 + k : 5 + k + ROWS, :]
        return (pre * sigmoid(pre)).astype(BF16)

    def tile(start):
        return pl.ds(pl.multiple_of(start, 128), 128)

    def group_states(g):
        b16 = mixed(GROUP_PAIRS, tile(INNER + STATE * g))
        c16 = mixed(GROUP_PAIRS + 1, tile(INNER + GROUPS * STATE + STATE * g))
        bm_ref[g] = b16
        cm_ref[g] = c16
        scores[g] = jnp.where(iota(shape, 1) >= iota(shape, 0), dot_nt(b16, c16), 0.0)
        dsc_ref[g] = jnp.zeros(shape, F32)
        b_t = b16.astype(F32).T.astype(BF16)
        c_t = c16.astype(F32).T.astype(BF16)
        back = lax.rem(HEADS - GROUP_HEADS * g, HEADS)
        run = pltpu.roll(run_ref[...], back, 1)
        step = pltpu.roll(sp_ref[...], back, 1)
        closing = run[ROWS - 1 : ROWS, :]
        grown = jnp.exp(run)
        to_close = jnp.exp(closing - run) * step
        whole_decay = jnp.exp(closing)
        for j in range(GROUP_PAIRS):
            at = GROUP_PAIRS * g + j
            lanes = tile(GROUP_LANES * g + 128 * j)
            x16 = mixed(j, lanes)
            xm[:, lanes] = x16
            s_own[at] = dot(b_t, (x16.astype(F32) * pair_of(to_close, j)).astype(BF16)).astype(BF16)
            g_own[at] = dot(c_t, (dy_ref[:, lanes].astype(F32) * pair_of(grown, j)).astype(BF16)).astype(BF16)
            a_own[at] = pair_of(whole_decay, j)

    def swaps(i):
        here = pl.ds(i * GROUP_PAIRS, GROUP_PAIRS)
        there = pl.ds(theirs + i * GROUP_PAIRS, GROUP_PAIRS)
        return (
            remote(a_own.at[there], a_oth.at[here], x_send.at[i], x_recv.at[i], other),
            remote(s_own.at[there], s_oth.at[here], y_send.at[i], y_recv.at[i], other),
            remote(g_own.at[there], g_oth.at[here], z_send.at[i], z_recv.at[i], other),
        )

    def ordered(held, sent):
        return jnp.where(first, held, sent), jnp.where(first, sent, held)

    def decays(at):
        return ordered(a_own[pl.ds(mine + at, own)], a_oth[pl.ds(at, own)])

    def values(ref, oth, at):
        return ordered(ref[pl.ds(mine + at, own)].astype(F32), oth[pl.ds(at, own)].astype(F32))

    def small_copies(r):
        at = pl.ds(chip_at(r) * own, own)
        device = chip_at(r) * 2 + core
        return (
            remote(a_out.at[at], a_in.at[chip], a_send.at[r], a_recv.at[r], device),
            remote(s_out.at[at], s_in.at[chip], s_send.at[r], s_recv.at[r], device),
        )

    def g_copy(r):
        at = pl.ds(chip_at(r) * own, own)
        return remote(g_out.at[at], g_in.at[chip], g_send.at[r], g_recv.at[r], chip_at(r) * 2 + core)

    def g_lift(r):
        at = pl.ds(chip_at(r) * own, own)
        return remote(g_out.at[at], g_mid.at[r], g_send.at[r], gm_recv.at[r], mid_at(r) * 2 + core)

    def g_drop(r):
        return remote(g_mid.at[r], g_in.at[mid_source(r)], gm_send.at[r], g_recv.at[r], mid_target(r) * 2 + core)

    def h_copy(r):
        at = pl.ds(chip * own, own)
        return remote(h_out.at[chip_at(r)], h_in.at[at], h_send.at[r], h_recv.at[r], chip_at(r) * 2 + core)

    def l_copy(r):
        at = pl.ds(chip * own, own)
        return remote(l_out.at[chip_at(r)], l_in.at[at], l_send.at[r], l_recv.at[r], chip_at(r) * 2 + core)

    def l_lift(r):
        return remote(l_out.at[chip_at(r)], l_mid.at[r], l_send.at[r], lm_recv.at[r], mid_at(r) * 2 + core)

    def l_drop(r):
        at = pl.ds(mid_source(r) * own, own)
        return remote(l_mid.at[r], l_in.at[at], lm_send.at[r], l_recv.at[r], mid_target(r) * 2 + core)

    def go(r, direct, lifted):
        @pl.when(tied(r))
        def _():
            lifted(r).start()

        @pl.when(jnp.logical_not(tied(r)))
        def _():
            direct(r).start()

    def relay(lifted, dropped):
        def one(r, _):
            @pl.when(tied(r))
            def _():
                lifted(r).wait_recv()
                dropped(r).start()

            return 0

        lax.fori_loop(1, chips, one, 0)

    def group_theirs(i, _):
        group_states(theirs // GROUP_PAIRS + i)

        @pl.when(i == 0)
        def _():
            pl.semaphore_wait(barrier, chips)

        for copy in swaps(i):
            copy.start()
        return 0

    lax.fori_loop(0, half_groups, group_theirs, 0)

    def group_mine(k, _):
        i = lax.rem(z + k, half_groups)
        group_states(mine // GROUP_PAIRS + i)
        for copy in swaps(i):
            copy.wait_recv()

        def combine(d, _):
            r = k * 4 + d
            at = chip_at(r) * own
            a0, a1 = decays(at)
            s0, s1 = values(s_own, s_oth, at)
            g0, g1 = values(g_own, g_oth, at)
            here = pl.ds(at, own)
            a_out[here] = a0 * a1
            s_out[here] = (a1 * s0 + s1).astype(BF16)
            g_out[here] = (a0 * g1 + g0).astype(BF16)

            @pl.when(r > 0)
            def _():
                for copy in small_copies(r):
                    copy.start()
                go(r, g_copy, g_lift)

            return 0

        lax.fori_loop(0, 4, combine, 0)
        return 0

    lax.fori_loop(0, half_groups, group_mine, 0)
    at_own = pl.ds(chip * own, own)
    a_in[chip] = a_out[at_own]
    s_in[chip] = s_out[at_own]
    g_in[chip] = g_out[at_own]

    low = low_half(shape)

    def inside(jj, _):
        g = jj // GROUP_PAIRS
        lanes = tile(128 * jj)
        x16 = xm[:, lanes]
        dy = dy_ref[:, lanes].astype(F32)
        split = jnp.concatenate([jnp.where(low, dy, 0.0), jnp.where(low, 0.0, dy)], axis=0).astype(BF16)
        d_weights = dot_nt(x16, split)
        back = lax.rem(HEADS - 2 * jj, HEADS)
        run = pltpu.roll(run_ref[...], back, 1)
        steps = pltpu.roll(sp_ref[...], back, 1)
        score = scores[g]
        weights = []
        gathered = dsc_ref[g]
        sums = sum_s_ref[...]
        lane = iota(shape, 1)
        for i in range(2):
            at = 2 * jj + i
            step = steps[:, i : i + 1]
            d_weight = d_weights[:, 128 * i : 128 * i + 128]
            decay = jnp.exp(jnp.minimum(run_t_ref[pl.ds(at, 1), :] - run[:, i : i + 1], 0.0))
            plain = decay * score
            weights.append((plain * step).astype(BF16))
            product = d_weight * plain
            sums = jnp.where(lane == at, jnp.sum(product, axis=1, keepdims=True), sums)
            sum_r_ref[pl.ds(at, 1), :] = jnp.sum(product * step, axis=0, keepdims=True)
            gathered = gathered + d_weight * decay * step
        sum_s_ref[...] = sums
        dsc_ref[g] = gathered
        dxi_ref[:, lanes] = dot(jnp.concatenate(weights, axis=1), split).astype(BF16)
        return 0

    lax.fori_loop(0, EARLY, inside, 0)
    relay(g_lift, g_drop)
    lax.fori_loop(EARLY, MIDDLE, inside, 0)

    def arrived(r, _):
        for copy in small_copies(r):
            copy.wait_recv()
        g_copy(r).wait_recv()
        return 0

    lax.fori_loop(1, chips, arrived, 0)

    def forth(c, state):
        h_out[c] = state.astype(BF16)
        return a_in[c] * state + s_in[c].astype(F32)

    def back_again(i, state):
        c = chips - 1 - i
        l_out[c] = state.astype(BF16)
        return a_in[c] * state + g_in[c].astype(F32)

    zero = jnp.zeros((own, STATE, 128), F32)
    lax.fori_loop(0, chips, back_again, zero)

    def send_l(r, _):
        go(r, l_copy, l_lift)
        return 0

    lax.fori_loop(1, chips, send_l, 0)
    lax.fori_loop(0, chips, forth, zero)

    def send_h(r, _):
        h_copy(r).start()
        return 0

    lax.fori_loop(1, chips, send_h, 0)
    h_in[at_own] = h_out[chip]
    l_in[at_own] = l_out[chip]
    lax.fori_loop(MIDDLE, LATE, inside, 0)
    relay(l_lift, l_drop)
    lax.fori_loop(LATE, PAIRS, inside, 0)

    def swap_back(r):
        here = pl.ds(chip_before(r) * own, own)
        there = pl.ds(mine + chip_before(r) * own, own)
        return (
            remote(h_oth.at[here], h_ref.at[there], p_send.at[r], p_recv.at[r], other),
            remote(l_oth.at[here], l_ref.at[there], q_send.at[r], q_recv.at[r], other),
        )

    def finish(r, _):
        at = chip_before(r) * own

        @pl.when(r > 0)
        def _():
            h_copy(r).wait_recv()
            l_copy(r).wait_recv()

        here = pl.ds(at, own)
        held = pl.ds(mine + at, own)
        a0, a1 = decays(at)
        s0, _ = values(s_own, s_oth, at)
        _, g1 = values(g_own, g_oth, at)
        h0 = h_in[here]
        h1 = (a0 * h0.astype(F32) + s0).astype(BF16)
        l1 = l_in[here]
        l0 = (a1 * l1.astype(F32) + g1).astype(BF16)
        h_ref[held] = jnp.where(first, h0, h1)
        h_oth[here] = jnp.where(first, h1, h0)
        l_ref[held] = jnp.where(first, l0, l1)
        l_oth[here] = jnp.where(first, l1, l0)
        for copy in swap_back(r):
            copy.start()
        return 0

    lax.fori_loop(0, chips, finish, 0)

    def swapped(i, _):
        for copy in swaps(i):
            copy.wait_send()
        return 0

    lax.fori_loop(0, half_groups, swapped, 0)

    def sent(r, _):
        for copy in small_copies(r):
            copy.wait_send()
        g_copy(r).wait_send()
        h_copy(r).wait_send()
        l_copy(r).wait_send()

        @pl.when(tied(r))
        def _():
            g_drop(r).wait_send()
            l_drop(r).wait_send()

        return 0

    lax.fori_loop(1, chips, sent, 0)

    def settled(r, _):
        for copy in swap_back(r):
            copy.wait()
        return 0

    lax.fori_loop(0, chips, settled, 0)


def front(mixer, halo, taps, raw, bias, rate, dy):
    chips = lax.axis_size("ctx") // 2
    own = HALF // chips
    square = jax.ShapeDtypeStruct((ROWS, HEADS), F32)
    group = jax.ShapeDtypeStruct((GROUPS, ROWS, STATE), BF16)
    state = jax.ShapeDtypeStruct((PAIRS, STATE, 128), BF16)
    whole = pltpu.VMEM((PAIRS, STATE, 128), BF16)
    wide = pltpu.VMEM((HALF, STATE, 128), BF16)
    split = pltpu.VMEM((chips, own, STATE, 128), BF16)
    row = pltpu.VMEM((HALF, 1, 128), F32)
    few = pltpu.SemaphoreType.DMA((GROUPS // 2,))
    many = pltpu.SemaphoreType.DMA((chips,))
    memory = pl.BlockSpec(memory_space=pltpu.VMEM)
    return pl.pallas_call(
        front_kernel,
        out_shape=[
            group, group, jax.ShapeDtypeStruct((ROWS, INNER), BF16),
            jax.ShapeDtypeStruct((GROUPS, ROWS, ROWS), F32), state, state, square, square, square, square, square,
        ],
        in_specs=[memory] * 7,
        out_specs=[memory] * 11,
        scratch_shapes=[
            pltpu.VMEM((GROUP_PAIRS + 2, ROWS + 8, 128), F32), pltpu.VMEM((ROWS, INNER), BF16),
            pltpu.VMEM((GROUPS, ROWS, ROWS), F32),
            whole, whole, pltpu.VMEM((PAIRS, 1, 128), F32), wide, wide, row, wide, wide, row,
            split, split, pltpu.VMEM((chips, own, 1, 128), F32), split,
            split, split, wide, wide, split, wide, wide,
        ] + [few] * 6 + [many] * 18,
        compiler_params=pltpu.CompilerParams(
            collective_id=0, has_side_effects=True, vmem_limit_bytes=VMEM
        ),
        name="front",
    )(mixer, halo, taps, raw, bias, rate, dy)


def grads_kernel(
    x_ref, b_ref, c_ref, hx_ref, hb_ref, hc_ref, tx_ref, tb_ref, tc_ref, raw_ref, bias_ref, rate_ref, dy_ref,
    gain_ref, bm_ref, cm_ref, dxi_ref, dsc_ref, h_ref, l_ref, run_ref, sp_ref, sum_s_ref, sum_r_ref,
    ig_ref, last_ref, spill_ref, taps_out, step_ref, rows_ref,
    pad, dpad, acc_b, acc_c, col_u, col_q, row_g, full_u, full_q, full_g,
):
    g = pl.program_id(0)
    back = lax.rem(HEADS - GROUP_HEADS * g, HEADS)
    shape = (ROWS, ROWS)

    @pl.when(g == 0)
    def _():
        dpad[:, ROWS:, :] = jnp.zeros((GROUP_PAIRS + 2, 8, 128), F32)
        for ref in (full_u, full_q, full_g, col_u, col_q, row_g):
            ref[...] = jnp.zeros(ref.shape, F32)

    b16, c16 = bm_ref[0], cm_ref[0]
    run = pltpu.roll(run_ref[...], back, 1)
    spread = pltpu.roll(sp_ref[...], back, 1)
    grown = jnp.exp(run)
    to_close = jnp.exp(run[ROWS - 1 : ROWS, :] - run) * spread
    low = low_half(shape)
    low_row = low_half((1, 128))
    acc_b[...] = jnp.zeros(shape, F32)
    acc_c[...] = jnp.zeros(shape, F32)

    def conv_back(slot, grad, pre, gate, taps_ref, lanes, out):
        here = pad.at[slot]
        there = dpad.at[slot]
        dpre = grad * (gate * (1.0 + pre * (1.0 - gate)))
        there[0:ROWS, :] = dpre
        whole = jnp.zeros(shape, F32)
        for k in range(KERNEL):
            whole = whole + taps_ref[k : k + 1, lanes] * there[3 - k : 3 - k + ROWS, :]
            taps_out[k : k + 1, out] = jnp.sum(dpre * here[5 + k : 5 + k + ROWS, :], axis=0, keepdims=True)
        taps_out[4:5, out] = jnp.sum(dpre, axis=0, keepdims=True)
        taps_out[5:8, out] = jnp.zeros((3, 128), F32)
        ig_ref[:, out] = whole.astype(BF16)
        last_ref[:, out] = whole[ROWS - 8 :, :]
        head = dpre[0:8, :]
        row = iota((8, 128), 0)
        spilled = jnp.zeros((8, 128), F32)
        for k in range(KERNEL - 1):
            moved = pltpu.roll(head, 5 + k, 0)
            spilled = spilled + jnp.where(row >= 5 + k, taps_ref[k : k + 1, lanes] * moved, 0.0)
        spill_ref[:, out] = spilled

    for j in range(GROUP_PAIRS):
        lanes = pl.ds(128 * j, 128)
        pre = conv_pre(pad.at[j], x_ref, hx_ref, tx_ref, lanes)
        gate = sigmoid(pre)
        x = (pre * gate).astype(BF16).astype(F32)
        dy = dy_ref[:, lanes].astype(F32)
        h16, l16 = h_ref[j], l_ref[j]
        grown_2 = pair_of(grown, j)
        close_2 = pair_of(to_close, j)
        entered = dy * dot(c16, h16)
        left = dot(b16, l16)
        used = x * left
        for i in range(2):
            head = 2 * j + i
            mask = low if i == 0 else jnp.logical_not(low)
            mask_row = low_row if i == 0 else jnp.logical_not(low_row)
            col_u[:, head : head + 1] = jnp.sum(jnp.where(mask, entered, 0.0), axis=1, keepdims=True)
            col_q[:, head : head + 1] = jnp.sum(jnp.where(mask, used, 0.0), axis=1, keepdims=True)
            crossed = jnp.sum(h16.astype(F32) * l16.astype(F32), axis=0, keepdims=True)
            gained = jnp.sum(dy * x, axis=0, keepdims=True)
            row_g[0:1, head : head + 1] = jnp.sum(jnp.where(mask_row, crossed, 0.0), axis=1, keepdims=True)
            row_g[1:2, head : head + 1] = jnp.sum(jnp.where(mask_row, gained, 0.0), axis=1, keepdims=True)
        acc_c[...] += dot_nt((dy * grown_2).astype(BF16), h16)
        acc_b[...] += dot_nt((x * close_2).astype(BF16), l16)
        grad_x = dxi_ref[:, lanes].astype(F32) + close_2 * left + gain_ref[0, :, lanes] * dy
        conv_back(j, grad_x, pre, gate, tx_ref, lanes, pl.ds(pl.multiple_of(g * GROUP_LANES + 128 * j, 128), 128))

    d_scores = jnp.where(iota(shape, 1) >= iota(shape, 0), dsc_ref[0], 0.0)
    grad_b = acc_b[...] + dot(d_scores.astype(BF16), c16)
    grad_c = acc_c[...] + dot(d_scores.T.astype(BF16), b16)
    every = pl.ds(0, 128)
    for i, (grad, tile_ref, halo_ref, taps_ref) in enumerate(
        ((grad_b, b_ref, hb_ref, tb_ref), (grad_c, c_ref, hc_ref, tc_ref))
    ):
        pre = conv_pre(pad.at[GROUP_PAIRS + i], tile_ref, halo_ref, taps_ref, every)
        out = pl.ds(pl.multiple_of(INNER + GROUPS * STATE * i + 128 * g, 128), 128)
        conv_back(GROUP_PAIRS + i, grad, pre, sigmoid(pre), taps_ref, every, out)

    forward = lax.rem(GROUP_HEADS * g, HEADS)
    for whole_ref, part_ref in ((full_u, col_u), (full_q, col_q), (full_g, row_g)):
        lane = iota(part_ref.shape, 1)
        whole_ref[...] += pltpu.roll(jnp.where(lane < GROUP_HEADS, part_ref[...], 0.0), forward, 1)

    @pl.when(g == GROUPS - 1)
    def _():
        running, steps = run_ref[...], sp_ref[...]
        rate = rate_ref[...]
        closing = running[ROWS - 1 : ROWS, :]
        from_close = jnp.exp(closing - running)
        direct_q = from_close * full_q[...]
        used_q = direct_q * steps
        summed = sum_r_ref[...].T + jnp.exp(running) * full_u[...] - sum_s_ref[...] * steps - used_q
        upper = jnp.where(iota(shape, 1) >= iota(shape, 0), 1.0, 0.0).astype(F32)
        constant = jnp.sum(used_q, axis=0, keepdims=True) + jnp.exp(closing) * full_g[0:1, :]
        d_logs = dot(upper, summed, EXACT) + constant
        d_spread = (d_logs * rate + sum_s_ref[...] + direct_q).astype(BF16).astype(F32)
        step_grad = d_spread * sigmoid(raw_ref[...].astype(F32) + bias_ref[...])
        step_ref[...] = step_grad
        rows_ref[...] = jnp.zeros((8, HEADS), F32)
        rows_ref[0:1, :] = rate * jnp.sum(d_logs * steps, axis=0, keepdims=True)
        rows_ref[1:2, :] = jnp.sum(step_grad, axis=0, keepdims=True)
        rows_ref[2:3, :] = full_g[1:2, :]


def grads(mixer, halo, taps, raw, bias, rate, dy, gain, bm, cm, dxi, dsc, h, l, run, sp, sum_s, sum_r):
    x_spec = pl.BlockSpec((ROWS, GROUP_LANES), lambda g: (0, g))
    group_spec = pl.BlockSpec((1, ROWS, STATE), lambda g: (g, 0, 0))
    state_spec = pl.BlockSpec((GROUP_PAIRS, STATE, 128), lambda g: (g, 0, 0))
    square = full((ROWS, HEADS))
    plane = pltpu.VMEM((ROWS, 128), F32)
    tall = pltpu.VMEM((GROUP_PAIRS + 2, ROWS + 8, 128), F32)
    rows = pltpu.VMEM((8, 128), F32)
    edge = jax.ShapeDtypeStruct((8, CONV), F32)
    return pl.pallas_call(
        grads_kernel,
        grid=(GROUPS,),
        in_specs=channel_specs(ROWS) + channel_specs(8) + channel_specs(8)
        + [square, full((1, HEADS)), full((1, HEADS)), x_spec]
        + [pl.BlockSpec((1, 1, GROUP_LANES), lambda g: (g, 0, 0)), group_spec, group_spec, x_spec, group_spec]
        + [state_spec, state_spec, square, square, square, square],
        out_specs=[full((ROWS, CONV))] + [full((8, CONV))] * 3 + [square, full((8, HEADS))],
        out_shape=[
            jax.ShapeDtypeStruct((ROWS, CONV), BF16), edge, edge, edge,
            jax.ShapeDtypeStruct((ROWS, HEADS), F32), jax.ShapeDtypeStruct((8, HEADS), F32),
        ],
        scratch_shapes=[tall, tall] + [plane] * 4 + [rows] + [plane] * 2 + [rows],
        compiler_params=pltpu.CompilerParams(vmem_limit_bytes=VMEM),
        name="grads",
    )(
        mixer, mixer, mixer, halo, halo, halo, taps, taps, taps, raw, bias, rate, dy,
        gain, bm, cm, dxi, dsc, h, l, run, sp, sum_s, sum_r,
    )


def reduce_kernel(
    taps_ref, rows_ref, conv_ref, head_ref,
    taps_oth, rows_oth, shards, arrived, flat, packed, packed_in, total, total_oth,
    x_send, x_recv, d_send, d_recv, c_send, c_recv, o_send, o_recv,
):
    dp = lax.axis_index("dp")
    ctx = lax.axis_index("ctx")
    shard_count = lax.axis_size("dp")
    core = lax.rem(ctx, 2)
    chip = ctx // 2
    z, y = chip // 4, lax.rem(chip, 4)
    chips = lax.axis_size("ctx") // 2
    other = ctx + 1 - 2 * core
    width = total.shape[1]
    half = width // 2

    def chip_at(r):
        return lax.rem(z + r // 4, 4) * 4 + lax.rem(y + r, 4)

    def dp_at(r):
        return lax.rem(dp + r, shard_count)

    barrier = pltpu.get_barrier_semaphore()
    pl.semaphore_signal(barrier, inc=1, device_id=(dp, other), device_id_type=MESH)
    for r in range(1, shard_count):
        pl.semaphore_signal(barrier, inc=1, device_id=(dp_at(r), ctx), device_id_type=MESH)

    def greet(r, _):
        pl.semaphore_signal(barrier, inc=1, device_id=(dp, chip_at(r) * 2 + core), device_id_type=MESH)
        return 0

    lax.fori_loop(1, chips, greet, 0)
    pl.semaphore_wait(barrier, chips + shard_count - 1)

    def remote(src, dst, send, recv, d, c):
        return pltpu.make_async_remote_copy(
            src_ref=src, dst_ref=dst, send_sem=send, recv_sem=recv, device_id=(d, c), device_id_type=MESH
        )

    def columns(shard, part):
        return pl.ds(pl.multiple_of(shard * (2 * width) + part * width, 128), width)

    swaps = [
        remote(taps_ref.at[:, columns(i, 1 - core)], taps_oth.at[i], x_send.at[i], x_recv.at[i], dp, other)
        for i in range(shard_count)
    ]
    swaps.append(remote(rows_ref, rows_oth, x_send.at[shard_count], x_recv.at[shard_count], dp, other))
    for copy in swaps:
        copy.start()
    for copy in swaps:
        copy.wait()
    for i in range(shard_count):
        shards[i, :, 0:width] = taps_ref[:, columns(i, core)] + taps_oth[i]
        shards[i, :, width:] = rows_ref[...] + rows_oth[...]

    def shard_copy(r):
        return remote(shards.at[dp_at(r)], arrived.at[r], d_send.at[r], d_recv.at[r], dp_at(r), ctx)

    for r in range(1, shard_count):
        shard_copy(r).start()
    summed = shards[dp]
    for r in range(1, shard_count):
        shard_copy(r).wait()
        summed = summed + arrived[r]
    flat[0:4, 0:half] = summed[0:4, 0:half]
    flat[4:8, 0:half] = summed[0:4, half:width]
    flat[8:9, 0:half] = summed[4:5, 0:half]
    flat[9:10, 0:half] = summed[4:5, half:width]
    flat[10:16, 0:half] = jnp.zeros((6, half), F32)
    flat[0:8, half:] = summed[:, width:]
    flat[8:16, half:] = jnp.zeros((8, 128), F32)
    packed[...] = flat[...].astype(BF16)

    def chip_copy(r):
        return remote(packed, packed_in.at[r], c_send.at[r], c_recv.at[r], dp, chip_at(r) * 2 + core)

    def send(r, _):
        chip_copy(r).start()
        return 0

    def take(r, _):
        chip_copy(r).wait()
        flat[...] += packed_in[r].astype(F32)
        return 0

    lax.fori_loop(1, chips, send, 0)
    lax.fori_loop(1, chips, take, 0)
    total[0:4, 0:half] = flat[0:4, 0:half]
    total[0:4, half:] = flat[4:8, 0:half]
    total[4:5, 0:half] = flat[8:9, 0:half]
    total[4:5, half:] = flat[9:10, 0:half]
    total[5:8, :] = jnp.zeros((3, width), F32)
    last = remote(total, total_oth, o_send.at[0], o_recv.at[0], dp, other)
    last.start()
    head_ref[...] = pltpu.roll(flat[0:8, half:], lax.rem(HEADS - (HEADS // shard_count) * dp, HEADS), 1)
    conv_ref[:, pl.ds(pl.multiple_of(core * width, 128), width)] = total[...]
    last.wait()
    conv_ref[:, pl.ds(pl.multiple_of((1 - core) * width, 128), width)] = total_oth[...]


def reduce_params(taps_grad, rows):
    shards = lax.axis_size("dp")
    chips = lax.axis_size("ctx") // 2
    width = CONV // shards // 2
    memory = pl.BlockSpec(memory_space=pltpu.VMEM)
    dma = pltpu.SemaphoreType.DMA
    return pl.pallas_call(
        reduce_kernel,
        out_shape=[jax.ShapeDtypeStruct((8, 2 * width), F32), jax.ShapeDtypeStruct((8, HEADS), F32)],
        in_specs=[memory] * 2,
        out_specs=[memory] * 2,
        scratch_shapes=[
            pltpu.VMEM((shards, 8, width), F32), pltpu.VMEM((8, HEADS), F32),
            pltpu.VMEM((shards, 8, width + 128), F32), pltpu.VMEM((shards, 8, width + 128), F32),
            pltpu.VMEM((16, width // 2 + 128), F32), pltpu.VMEM((16, width // 2 + 128), BF16),
            pltpu.VMEM((chips, 16, width // 2 + 128), BF16),
            pltpu.VMEM((8, width), F32), pltpu.VMEM((8, width), F32),
            dma((shards + 1,)), dma((shards + 1,)), dma((shards,)), dma((shards,)),
            dma((chips,)), dma((chips,)), dma((1,)), dma((1,)),
        ],
        compiler_params=pltpu.CompilerParams(
            collective_id=1, has_side_effects=True, vmem_limit_bytes=VMEM
        ),
        name="reduce_params",
    )(taps_grad, rows)


def passed_along(value, axis, steps):
    count = lax.axis_size(axis)
    initial, last = (max(0, -steps), min(count, count - steps))
    return lax.ppermute(value, axis, [(source, source + steps) for source in range(initial, last)])


def local(mixer_input, step_raw, out_grad, conv_weight, conv_bias, step_bias, decay_log, skip_gain):
    mixer, raw, dy = mixer_input[0], step_raw[0], out_grad[0]
    halo = passed_along(mixer[ROWS - 8 :], "ctx", 1).astype(F32)
    taps = jnp.concatenate([conv_weight, conv_bias[None], jnp.zeros((3, CONV), F32)], axis=0)
    bias = step_bias[None]
    rate = -jnp.exp(decay_log)[None]
    gain = jnp.repeat(skip_gain, HEAD_DIM).reshape(GROUPS, 1, GROUP_LANES)
    bm, cm, dxi, dsc, h, l, run, _, sp, sum_s, sum_r = front(mixer, halo, taps, raw, bias, rate, dy)
    input_grad, last, spill, taps_grad, step_grad, rows = grads(
        mixer, halo, taps, raw, bias, rate, dy, gain, bm, cm, dxi, dsc, h, l, run, sp, sum_s, sum_r
    )
    spilled = passed_along(spill.astype(BF16), "ctx", -1).astype(F32)
    input_grad = lax.dynamic_update_slice(input_grad, (last + spilled).astype(BF16), (ROWS - 8, 0))
    factor = 1.0 / math.sqrt(lax.axis_size("dp") * ROWS * lax.axis_size("ctx"))
    conv_total, head_total = reduce_params(taps_grad, rows)
    return (
        input_grad[None],
        step_grad[None],
        conv_total[: KERNEL + 1] * factor,
        head_total[:2, : HEADS // lax.axis_size("dp")] * factor,
        head_total[2, : HEADS // lax.axis_size("dp")] * factor,
    )


def solution(mesh):
    spread = P("dp", "ctx", None)
    in_specs = (spread, spread, spread, P(), P(), P(), P(), P())
    out_specs = (spread, spread, P(None, "dp"), P(None, "dp"), P("dp"))
    return jax.shard_map(local, mesh=mesh, in_specs=in_specs, out_specs=out_specs, check_vma=False)
```

```python
import functools
import math

import jax
import jax.numpy as jnp
from jax import lax
from jax.experimental import pallas as pl
from jax.experimental.pallas import tpu as pltpu
from jax.sharding import PartitionSpec as P

HEADS = 128
HEAD_DIM = 64
STATE = 128
GROUPS = 8
KERNEL = 4
ROWS = 128
INNER = 8192
CONV = 10240
GROUP_HEADS = HEADS // GROUPS
GROUP_PAIRS = GROUP_HEADS // 2
GROUP_LANES = GROUP_HEADS * HEAD_DIM
PAIRS = HEADS // 2
HALF = PAIRS // 2
MESH = pl.DeviceIdType.MESH
F32 = jnp.float32
BF16 = jnp.bfloat16
VMEM = 60 << 20
BATCHES = 4
BLOCK_ROWS = 64
FIRST, SLICE = 6, 14
EXACT = lax.Precision.HIGHEST


def dot(a, b, precision=None):
    return jnp.dot(a, b, precision=precision, preferred_element_type=F32)


def dot_nt(a, b):
    return lax.dot_general(a, b, (((1,), (1,)), ((), ())), preferred_element_type=F32)


def sigmoid(v):
    return 0.5 + 0.5 * jnp.tanh(0.5 * v)


def softplus(v):
    return jnp.maximum(v, 0.0) + jnp.log1p(jnp.exp(-jnp.abs(v)))


def iota(shape, dim):
    return lax.broadcasted_iota(jnp.int32, shape, dim)


def low_half(shape):
    return iota(shape, len(shape) - 1) < HEAD_DIM


def pair_of(columns, j):
    shape = (columns.shape[0], 2 * HEAD_DIM)
    first = jnp.broadcast_to(columns[:, 2 * j : 2 * j + 1], shape)
    second = jnp.broadcast_to(columns[:, 2 * j + 1 : 2 * j + 2], shape)
    return jnp.where(low_half(shape), first, second)


def mixer_kernel(
    mix_ref, halo_ref, weight_ref, shift_ref, raw_ref, bias_ref, decay_ref, gain_ref, dy_ref,
    ig_ref, step_ref, conv_ref, head_ref,
    run_ref, run_t_ref, sp_ref, close_own, close_oth, close_out, close_in, decay_own, decay_oth, decay_in, pad, dpad,
    xm, bm, cm, scores, dxi, dsc, sum_s, sum_r, s_own, g_own, s_oth, g_oth, sg_out, sg_in, hl_out, hl_in,
    h_all, l_all, h_oth, l_oth, acc_b, acc_c, col_u, col_q, row_g, full_u, full_q, full_g,
    last, spill, spill_in, taps, rows, taps_oth, rows_oth, shards, arrived, flat, packed, packed_in, total, total_oth,
    e_send, e_recv, k_send, k_recv, x_send, x_recv, y_send, y_recv, sg_send, sg_recv, hl_send, hl_recv,
    p_send, p_recv, q_send, q_recv, sp_send, sp_recv, t_send, t_recv, d_send, d_recv, c_send, c_recv, o_send, o_recv,
):
    dp = lax.axis_index("dp")
    ctx = lax.axis_index("ctx")
    shard_count = lax.axis_size("dp")
    devices = lax.axis_size("ctx")
    core = lax.rem(ctx, 2)
    chip = ctx // 2
    z, y = chip // 4, lax.rem(chip, 4)
    chips = devices // 2
    other = ctx + 1 - 2 * core
    beyond = lax.rem(ctx + devices - 1 + 2 * core, devices)
    half_blocks = HALF * STATE // BLOCK_ROWS
    mine = core * half_blocks
    half_groups = GROUPS // 2
    mine_group = core * half_groups
    theirs_group = half_groups - mine_group
    shape = (ROWS, ROWS)
    first = core == 0
    low = low_half(shape)
    low_row = low_half((1, 128))

    def chip_at(r):
        return lax.rem(z + r // 4, 4) * 4 + lax.rem(y + r, 4)

    def chip_before(r):
        return lax.rem(z + 4 - r // 4, 4) * 4 + lax.rem(y + 4 - lax.rem(r, 4), 4)

    def dp_at(r):
        return lax.rem(dp + r, shard_count)

    barrier = pltpu.get_barrier_semaphore()
    for device in (other, beyond):
        pl.semaphore_signal(barrier, inc=1, device_id=(dp, device), device_id_type=MESH)
    for r in range(1, shard_count):
        pl.semaphore_signal(barrier, inc=1, device_id=(dp_at(r), ctx), device_id_type=MESH)

    def greet(r, _):
        pl.semaphore_signal(barrier, inc=1, device_id=(dp, chip_at(r) * 2 + core), device_id_type=MESH)
        return 0

    lax.fori_loop(1, chips, greet, 0)

    def remote(src, dst, send, recv, device, d=None):
        return pltpu.make_async_remote_copy(
            src_ref=src, dst_ref=dst, send_sem=send, recv_sem=recv,
            device_id=(dp if d is None else d, device), device_id_type=MESH,
        )

    def tile(start):
        return pl.ds(pl.multiple_of(start, 128), 128)

    rate = -jnp.exp(decay_ref[...])
    spread = softplus(raw_ref[...].astype(F32) + bias_ref[...])
    lower = jnp.where(iota(shape, 0) >= iota(shape, 1), 1.0, 0.0).astype(F32)
    running = dot(lower, spread * rate, EXACT)
    sp_ref[...] = spread
    run_ref[...] = running
    run_t_ref[...] = running.T
    close_own[...] = jnp.broadcast_to(running[ROWS - 1 : ROWS, :], (8, HEADS))
    sum_s[...] = jnp.zeros((ROWS, HEADS), F32)

    def conv_pre(slot, lanes):
        here = pad.at[slot]
        here[0:8, :] = halo_ref[:, lanes].astype(F32)
        here[8:, :] = mix_ref[:, lanes].astype(F32)
        pre = jnp.broadcast_to(shift_ref[:, lanes], (ROWS, 128))
        for k in range(KERNEL):
            pre = pre + weight_ref[k : k + 1, lanes] * here[5 + k : 5 + k + ROWS, :]
        return pre

    def mixed(slot, lanes):
        pre = conv_pre(slot, lanes)
        return (pre * sigmoid(pre)).astype(BF16)

    def group_states(g):
        b16 = mixed(GROUP_PAIRS, tile(INNER + STATE * g))
        c16 = mixed(GROUP_PAIRS + 1, tile(INNER + GROUPS * STATE + STATE * g))
        bm[g] = b16
        cm[g] = c16
        scores[g] = jnp.where(iota(shape, 1) >= iota(shape, 0), dot_nt(b16, c16), 0.0)
        dsc[g] = jnp.zeros(shape, F32)
        b_t = b16.astype(F32).T.astype(BF16)
        c_t = c16.astype(F32).T.astype(BF16)
        back = lax.rem(HEADS - GROUP_HEADS * g, HEADS)
        run = pltpu.roll(run_ref[...], back, 1)
        step = pltpu.roll(sp_ref[...], back, 1)
        grown = jnp.exp(run)
        to_close = jnp.exp(run[ROWS - 1 : ROWS, :] - run) * step
        for j in range(GROUP_PAIRS):
            at = pl.ds(2 * (GROUP_PAIRS * g + j), 2)
            lanes = tile(GROUP_LANES * g + 128 * j)
            x16 = mixed(j, lanes)
            xm[:, lanes] = x16
            state = dot(b_t, (x16.astype(F32) * pair_of(to_close, j)).astype(BF16))
            s_own[at] = state.astype(BF16).reshape(2, BLOCK_ROWS, 128)
            state = dot(c_t, (dy_ref[:, lanes].astype(F32) * pair_of(grown, j)).astype(BF16))
            g_own[at] = state.astype(BF16).reshape(2, BLOCK_ROWS, 128)

    def batch(i):
        return pl.ds(i * chips, chips)

    def swaps(i):
        there = pl.ds(half_blocks - mine + i * chips, chips)
        return (
            remote(s_own.at[there], s_oth.at[batch(i)], x_send.at[i], x_recv.at[i], other),
            remote(g_own.at[there], g_oth.at[batch(i)], y_send.at[i], y_recv.at[i], other),
        )

    def swap_back(i):
        there = pl.ds(mine + i * chips, chips)
        return (
            remote(h_oth.at[batch(i)], h_all.at[there], p_send.at[i], p_recv.at[i], other),
            remote(l_oth.at[batch(i)], l_all.at[there], q_send.at[i], q_recv.at[i], other),
        )

    close_swap = remote(close_own, close_oth, e_send.at[0], e_recv.at[0], other)

    def close_copy(r):
        return remote(close_out, close_in.at[chip], k_send.at[r], k_recv.at[r], chip_at(r) * 2 + core)

    def sg_copy(i, r):
        q = chip_at(r)
        return remote(sg_out.at[i, q], sg_in.at[i, chip], sg_send.at[i, r], sg_recv.at[i, r], q * 2 + core)

    def hl_copy(i, r):
        q = chip_at(r)
        return remote(hl_out.at[i, q], hl_in.at[i, chip], hl_send.at[i, r], hl_recv.at[i, r], q * 2 + core)

    def ordered(held, sent):
        return jnp.where(first, held, sent), jnp.where(first, sent, held)

    def spread_pairs(closing, pairs):
        head = iota(closing.shape, 1)
        picked = jnp.where(head // 2 == pairs, closing, 0.0)
        shape = (HEADS, 128)
        lanes = jnp.where(lax.rem(iota(shape, 0), 2) == iota(shape, 1) // HEAD_DIM, 1.0, 0.0).astype(F32)
        return jnp.exp(dot(picked, lanes, EXACT))

    def held_decays(closing_ref):
        pairs = core * HALF + iota((HALF, HEADS), 0)
        return spread_pairs(jnp.broadcast_to(closing_ref[0:1, :], (HALF, HEADS)), pairs)

    def values(ref, oth, b):
        return ordered(ref[mine + b].astype(F32), oth[b].astype(F32))

    def both_decays(b):
        row = pl.ds(b // 2, 1)
        return ordered(decay_own[row, :], decay_oth[row, :])

    def build(u, _):
        i = u // 2
        theirs = lax.rem(u, 2) == 0
        group_states(jnp.where(theirs, theirs_group, mine_group) + i)

        @pl.when(u == 0)
        def _():
            pl.semaphore_wait(barrier, chips + shard_count)
            close_swap.start()

        @pl.when(theirs)
        def _():
            for copy in swaps(i):
                copy.start()

        @pl.when(u == 1)
        def _():
            close_swap.wait_recv()
            close_out[...] = close_own[...] + close_oth[...]
            decay_own[...] = held_decays(close_own)
            decay_oth[...] = held_decays(close_oth)
            close_in[chip] = close_out[...]

            def send(r, _):
                close_copy(r).start()
                return 0

            lax.fori_loop(1, chips, send, 0)

        @pl.when(jnp.logical_not(theirs))
        def _():
            for copy in swaps(i):
                copy.wait_recv()

            def combine(r, _):
                q = chip_at(r)
                b = chips * i + q
                a0, a1 = both_decays(b)
                s0, s1 = values(s_own, s_oth, b)
                g0, g1 = values(g_own, g_oth, b)
                sg_out[i, q, 0] = (a1 * s0 + s1).astype(BF16)
                sg_out[i, q, 1] = (a0 * g1 + g0).astype(BF16)

                @pl.when(r > 0)
                def _():
                    sg_copy(i, r).start()

                return 0

            lax.fori_loop(0, chips, combine, 0)
            sg_in[i, chip] = sg_out[i, chip]

        return 0

    lax.fori_loop(0, 2 * BATCHES, build, 0)

    def inside(jj, _):
        g = jj // GROUP_PAIRS
        lanes = tile(128 * jj)
        x16 = xm[:, lanes]
        dy = dy_ref[:, lanes].astype(F32)
        split = jnp.concatenate([jnp.where(low, dy, 0.0), jnp.where(low, 0.0, dy)], axis=0).astype(BF16)
        d_weights = dot_nt(x16, split)
        back = lax.rem(HEADS - 2 * jj, HEADS)
        run = pltpu.roll(run_ref[...], back, 1)
        steps = pltpu.roll(sp_ref[...], back, 1)
        score = scores[g]
        weights = []
        gathered = dsc[g]
        sums = sum_s[...]
        lane = iota(shape, 1)
        for i in range(2):
            at = 2 * jj + i
            step = steps[:, i : i + 1]
            d_weight = d_weights[:, 128 * i : 128 * i + 128]
            decay = jnp.exp(jnp.minimum(run_t_ref[pl.ds(at, 1), :] - run[:, i : i + 1], 0.0))
            plain = decay * score
            weights.append((plain * step).astype(BF16))
            product = d_weight * plain
            sums = jnp.where(lane == at, jnp.sum(product, axis=1, keepdims=True), sums)
            sum_r[pl.ds(at, 1), :] = jnp.sum(product * step, axis=0, keepdims=True)
            gathered = gathered + d_weight * decay * step
        sum_s[...] = sums
        dsc[g] = gathered
        dxi[:, lanes] = dot(jnp.concatenate(weights, axis=1), split).astype(BF16)
        return 0

    def scan(i):
        def arrive(r, _):
            @pl.when(i == 0)
            def _():
                close_copy(r).wait_recv()

            sg_copy(i, r).wait_recv()
            return 0

        lax.fori_loop(1, chips, arrive, 0)
        decay_in[...] = spread_pairs(close_in[:, 0, :], (mine + chips * i + chip) // 2)

        def both(c, states):
            forth, back = states
            d = chips - 1 - c
            hl_out[i, c, 0] = forth.astype(BF16)
            hl_out[i, d, 1] = back.astype(BF16)
            forth = decay_in[pl.ds(c, 1), :] * forth + sg_in[i, c, 0].astype(F32)
            back = decay_in[pl.ds(d, 1), :] * back + sg_in[i, d, 1].astype(F32)
            return forth, back

        zero = jnp.zeros((BLOCK_ROWS, 128), F32)
        lax.fori_loop(0, chips, both, (zero, zero), unroll=4)

        def send(r, _):
            hl_copy(i, r).start()
            return 0

        lax.fori_loop(1, chips, send, 0)
        hl_in[i, chip] = hl_out[i, chip]

    def middle(i, _):
        lax.fori_loop(jnp.maximum(SLICE * (i - 1) + FIRST, 0), SLICE * i + FIRST, inside, 0)
        scan(i)
        return 0

    lax.fori_loop(0, BATCHES, middle, 0)
    lax.fori_loop(SLICE * (BATCHES - 1) + FIRST, PAIRS, inside, 0)

    dpad[:, ROWS:, :] = jnp.zeros((GROUP_PAIRS + 2, 8, 128), F32)
    taps[...] = jnp.zeros(taps.shape, F32)
    for ref in (full_u, full_q, full_g, col_u, col_q, row_g):
        ref[...] = jnp.zeros(ref.shape, F32)

    def conv_back(slot, grad, pre, gate, lanes):
        here = pad.at[slot]
        there = dpad.at[slot]
        dpre = grad * (gate * (1.0 + pre * (1.0 - gate)))
        there[0:ROWS, :] = dpre
        whole = jnp.zeros(shape, F32)
        for k in range(KERNEL):
            whole = whole + weight_ref[k : k + 1, lanes] * there[3 - k : 3 - k + ROWS, :]
            taps[k : k + 1, lanes] = jnp.sum(dpre * here[5 + k : 5 + k + ROWS, :], axis=0, keepdims=True)
        taps[4:5, lanes] = jnp.sum(dpre, axis=0, keepdims=True)
        ig_ref[:, lanes] = whole.astype(BF16)
        last[:, lanes] = whole[ROWS - 16 :, :]
        edge = dpre[0:8, :]
        row = iota((8, 128), 0)
        spilled = jnp.zeros((8, 128), F32)
        for k in range(KERNEL - 1):
            moved = pltpu.roll(edge, 5 + k, 0)
            spilled = spilled + jnp.where(row >= 5 + k, weight_ref[k : k + 1, lanes] * moved, 0.0)
        spill[:, lanes] = spilled

    before = lax.rem(ctx + devices - 1, devices)

    def spill_copies(g):
        parts = (
            pl.ds(pl.multiple_of(GROUP_LANES * g, 128), GROUP_LANES),
            tile(INNER + STATE * g),
            tile(INNER + GROUPS * STATE + STATE * g),
        )
        return [
            remote(spill.at[:, lanes], spill_in.at[:, lanes], sp_send.at[g, n], sp_recv.at[g, n], before)
            for n, lanes in enumerate(parts)
        ]

    def group_grads(g):
        back = lax.rem(HEADS - GROUP_HEADS * g, HEADS)
        b16, c16 = bm[g], cm[g]
        run = pltpu.roll(run_ref[...], back, 1)
        step = pltpu.roll(sp_ref[...], back, 1)
        gain = pltpu.roll(jnp.broadcast_to(gain_ref[...], (8, HEADS)), back, 1)
        grown = jnp.exp(run)
        to_close = jnp.exp(run[ROWS - 1 : ROWS, :] - run) * step
        acc_b[...] = jnp.zeros(shape, F32)
        acc_c[...] = jnp.zeros(shape, F32)
        for j in range(GROUP_PAIRS):
            lanes = tile(GROUP_LANES * g + 128 * j)
            at = pl.ds(2 * (GROUP_PAIRS * g + j), 2)
            pre = conv_pre(j, lanes)
            gate = sigmoid(pre)
            x = xm[:, lanes].astype(F32)
            dy = dy_ref[:, lanes].astype(F32)
            h16 = h_all[at].reshape(STATE, 128)
            l16 = l_all[at].reshape(STATE, 128)
            close_2 = pair_of(to_close, j)
            entered = dy * dot(c16, h16)
            left = dot(b16, l16)
            used = x * left
            crossed = jnp.sum(h16.astype(F32) * l16.astype(F32), axis=0, keepdims=True)
            gained = jnp.sum(dy * x, axis=0, keepdims=True)
            for i in range(2):
                head = 2 * j + i
                mask = low if i == 0 else jnp.logical_not(low)
                mask_row = low_row if i == 0 else jnp.logical_not(low_row)
                col_u[:, head : head + 1] = jnp.sum(jnp.where(mask, entered, 0.0), axis=1, keepdims=True)
                col_q[:, head : head + 1] = jnp.sum(jnp.where(mask, used, 0.0), axis=1, keepdims=True)
                row_g[0:1, head : head + 1] = jnp.sum(jnp.where(mask_row, crossed, 0.0), axis=1, keepdims=True)
                row_g[1:2, head : head + 1] = jnp.sum(jnp.where(mask_row, gained, 0.0), axis=1, keepdims=True)
            acc_c[...] += dot_nt((dy * pair_of(grown, j)).astype(BF16), h16)
            acc_b[...] += dot_nt((x * close_2).astype(BF16), l16)
            grad_x = dxi[:, lanes].astype(F32) + close_2 * left + pair_of(gain, j)[0:1, :] * dy
            conv_back(j, grad_x, pre, gate, lanes)
        d_scores = jnp.where(iota(shape, 1) >= iota(shape, 0), dsc[g], 0.0)
        grad_b = acc_b[...] + dot(d_scores.astype(BF16), c16)
        grad_c = acc_c[...] + dot(d_scores.T.astype(BF16), b16)
        for i, grad in enumerate((grad_b, grad_c)):
            lanes = tile(INNER + GROUPS * STATE * i + STATE * g)
            pre = conv_pre(GROUP_PAIRS + i, lanes)
            conv_back(GROUP_PAIRS + i, grad, pre, sigmoid(pre), lanes)
        forward = lax.rem(GROUP_HEADS * g, HEADS)
        for whole_ref, part_ref in ((full_u, col_u), (full_q, col_q), (full_g, row_g)):
            lane = iota(part_ref.shape, 1)
            whole_ref[...] += pltpu.roll(jnp.where(lane < GROUP_HEADS, part_ref[...], 0.0), forward, 1)

        @pl.when(ctx > 0)
        def _():
            for copy in spill_copies(g):
                copy.start()

    def gather(i):
        def finish(r, _):
            q = chip_before(r)

            @pl.when(r > 0)
            def _():
                hl_copy(i, r).wait_recv()

            b = chips * i + q
            a0, a1 = both_decays(b)
            s0, _ = values(s_own, s_oth, b)
            _, g1 = values(g_own, g_oth, b)
            h0 = hl_in[i, q, 0]
            h1 = (a0 * h0.astype(F32) + s0).astype(BF16)
            l1 = hl_in[i, q, 1]
            l0 = (a1 * l1.astype(F32) + g1).astype(BF16)
            h_all[mine + b] = jnp.where(first, h0, h1)
            h_oth[b] = jnp.where(first, h1, h0)
            l_all[mine + b] = jnp.where(first, l0, l1)
            l_oth[b] = jnp.where(first, l1, l0)
            return 0

        lax.fori_loop(0, chips, finish, 0)
        for copy in swap_back(i):
            copy.start()

    def outer(u, _):
        i = u // 2
        held = lax.rem(u, 2) == 0

        @pl.when(held)
        def _():
            gather(i)

        @pl.when(jnp.logical_not(held))
        def _():
            for copy in swap_back(i):
                copy.wait_recv()

        group_grads(jnp.where(held, mine_group, theirs_group) + i)
        return 0

    lax.fori_loop(0, 2 * BATCHES, outer, 0)

    closing = run_ref[ROWS - 1 : ROWS, :]
    running = run_ref[...]
    steps = sp_ref[...]
    direct_q = jnp.exp(closing - running) * full_q[...]
    used_q = direct_q * steps
    summed = sum_r[...].T + jnp.exp(running) * full_u[...] - sum_s[...] * steps - used_q
    upper = jnp.where(iota(shape, 1) >= iota(shape, 0), 1.0, 0.0).astype(F32)
    constant = jnp.sum(used_q, axis=0, keepdims=True) + jnp.exp(closing) * full_g[0:1, :]
    d_logs = dot(upper, summed, EXACT) + constant
    d_spread = (d_logs * (-jnp.exp(decay_ref[...])) + sum_s[...] + direct_q).astype(BF16).astype(F32)
    step_grad = d_spread * sigmoid(raw_ref[...].astype(F32) + bias_ref[...])
    step_ref[...] = step_grad
    rows[...] = jnp.zeros((8, HEADS), F32)
    rows[0:1, :] = -jnp.exp(decay_ref[...]) * jnp.sum(d_logs * steps, axis=0, keepdims=True)
    rows[1:2, :] = jnp.sum(step_grad, axis=0, keepdims=True)
    rows[2:3, :] = full_g[1:2, :]

    width = total.shape[1]
    half = width // 2

    def columns(shard, part):
        return pl.ds(pl.multiple_of(shard * (2 * width) + part * width, 128), width)

    sums = [
        remote(taps.at[:, columns(i, 1 - core)], taps_oth.at[i], t_send.at[i], t_recv.at[i], other)
        for i in range(shard_count)
    ]
    sums.append(remote(rows, rows_oth, t_send.at[shard_count], t_recv.at[shard_count], other))
    for copy in sums:
        copy.start()
    for copy in sums:
        copy.wait()
    for i in range(shard_count):
        shards[i, :, 0:width] = taps[:, columns(i, core)] + taps_oth[i]
        shards[i, :, width:] = rows[...] + rows_oth[...]

    def shard_copy(r):
        return remote(shards.at[dp_at(r)], arrived.at[r], d_send.at[r], d_recv.at[r], ctx, dp_at(r))

    for r in range(1, shard_count):
        shard_copy(r).start()

    @pl.when(ctx < devices - 1)
    def _():
        def landed(g, _):
            for copy in spill_copies(g):
                copy.wait_recv()
            return 0

        lax.fori_loop(0, GROUPS, landed, 0)
        last[8:16, :] += spill_in[...]

    ig_ref[ROWS - 16 :, :] = last[...].astype(BF16)

    summed = shards[dp]
    for r in range(1, shard_count):
        shard_copy(r).wait()
        summed = summed + arrived[r]
    flat[0:4, 0:half] = summed[0:4, 0:half]
    flat[4:8, 0:half] = summed[0:4, half:width]
    flat[8:9, 0:half] = summed[4:5, 0:half]
    flat[9:10, 0:half] = summed[4:5, half:width]
    flat[10:16, 0:half] = jnp.zeros((6, half), F32)
    flat[0:8, half:] = summed[:, width:]
    flat[8:16, half:] = jnp.zeros((8, 128), F32)
    packed[...] = flat[...].astype(BF16)

    def chip_copy(r):
        return remote(packed, packed_in.at[r], c_send.at[r], c_recv.at[r], chip_at(r) * 2 + core)

    def send(r, _):
        chip_copy(r).start()
        return 0

    lax.fori_loop(1, chips, send, 0)

    close_swap.wait_send()

    def cleared(i, _):
        for copy in swaps(i) + swap_back(i):
            copy.wait_send()

        def sent(r, _):
            @pl.when(i == 0)
            def _():
                close_copy(r).wait_send()

            sg_copy(i, r).wait_send()
            hl_copy(i, r).wait_send()
            return 0

        lax.fori_loop(1, chips, sent, 0)
        return 0

    lax.fori_loop(0, BATCHES, cleared, 0)

    @pl.when(ctx > 0)
    def _():
        def left_here(g, _):
            for copy in spill_copies(g):
                copy.wait_send()
            return 0

        lax.fori_loop(0, GROUPS, left_here, 0)

    def take(r, _):
        chip_copy(r).wait()
        flat[...] += packed_in[r].astype(F32)
        return 0

    lax.fori_loop(1, chips, take, 0)
    total[0:4, 0:half] = flat[0:4, 0:half]
    total[0:4, half:] = flat[4:8, 0:half]
    total[4:5, 0:half] = flat[8:9, 0:half]
    total[4:5, half:] = flat[9:10, 0:half]
    total[5:8, :] = jnp.zeros((3, width), F32)
    final = remote(total, total_oth, o_send.at[0], o_recv.at[0], other)
    final.start()
    head_ref[...] = pltpu.roll(flat[0:8, half:], lax.rem(HEADS - (HEADS // shard_count) * dp, HEADS), 1)
    conv_ref[:, pl.ds(pl.multiple_of(core * width, 128), width)] = total[...]
    final.wait()
    conv_ref[:, pl.ds(pl.multiple_of((1 - core) * width, 128), width)] = total_oth[...]


def mixer_grads(mixer, halo, weight, shift, raw, bias, decay, gain, dy):
    chips = lax.axis_size("ctx") // 2
    shards = lax.axis_size("dp")
    width = CONV // shards // 2
    V = pltpu.VMEM
    dma = pltpu.SemaphoreType.DMA
    blocks = PAIRS * STATE // BLOCK_ROWS
    plane = V((ROWS, HEADS), F32)
    row = V((8, HEADS), F32)
    tall = V((GROUP_PAIRS + 2, ROWS + 8, 128), F32)
    group16 = V((GROUPS, ROWS, STATE), BF16)
    group32 = V((GROUPS, ROWS, ROWS), F32)
    inner = V((ROWS, INNER), BF16)
    whole = V((blocks, BLOCK_ROWS, 128), BF16)
    part = V((blocks // 2, BLOCK_ROWS, 128), BF16)
    sent = V((BATCHES, chips, 2, BLOCK_ROWS, 128), BF16)
    edge = V((8, CONV), F32)
    memory = pl.BlockSpec(memory_space=pltpu.VMEM)
    return pl.pallas_call(
        mixer_kernel,
        out_shape=[
            jax.ShapeDtypeStruct((ROWS, CONV), BF16), jax.ShapeDtypeStruct((ROWS, HEADS), F32),
            jax.ShapeDtypeStruct((8, 2 * width), F32), jax.ShapeDtypeStruct((8, HEADS), F32),
        ],
        in_specs=[memory] * 9,
        out_specs=[memory] * 4,
        scratch_shapes=[
            plane, plane, plane, row, row, row, V((chips, 8, HEADS), F32),
            V((HALF, 128), F32), V((HALF, 128), F32), V((chips, 128), F32), tall, tall,
            inner, group16, group16, group32, inner, group32, plane, plane, whole, whole, part, part,
            sent, sent, sent, sent, whole, whole, part, part, plane, plane, plane, plane, row, plane, plane, row,
            V((16, CONV), F32), edge, edge, edge, row,
            V((shards, 8, width), F32), row, V((shards, 8, width + 128), F32), V((shards, 8, width + 128), F32),
            V((16, width // 2 + 128), F32), V((16, width // 2 + 128), BF16),
            V((chips, 16, width // 2 + 128), BF16), V((8, width), F32), V((8, width), F32),
            dma((1,)), dma((1,)), dma((chips,)), dma((chips,)),
        ]
        + [dma((BATCHES,))] * 4 + [dma((BATCHES, chips))] * 4 + [dma((BATCHES,))] * 4
        + [dma((GROUPS, 3))] * 2 + [dma((shards + 1,))] * 2 + [dma((shards,))] * 2 + [dma((chips,))] * 2 + [dma((1,))] * 2,
        compiler_params=pltpu.CompilerParams(
            collective_id=0, has_side_effects=True, vmem_limit_bytes=VMEM
        ),
        name="mixer_grads",
    )(mixer, halo, weight, shift, raw, bias, decay, gain, dy)


def finish_kernel(factor, ig_ref, step_ref, conv_ref, head_ref, ig_out, step_out, conv_out, head_out, gain_out):
    ig_out[...] = ig_ref[...]

    @pl.when(pl.program_id(0) == 0)
    def _():
        step_out[...] = step_ref[...]
        conv_out[...] = conv_ref[0 : KERNEL + 1, :] * factor
        head_out[...] = head_ref[0:2, 0 : head_out.shape[1]] * factor
        gain_out[...] = head_ref[2:3, 0 : gain_out.shape[1]] * factor


def finish(factor, input_grad, step_grad, conv, head):
    heads = HEADS // lax.axis_size("dp")
    parts = 4
    block = pl.BlockSpec((ROWS // parts, CONV), lambda i: (i, 0))

    def full(shape):
        return pl.BlockSpec(shape, lambda i: (0,) * len(shape))

    return pl.pallas_call(
        functools.partial(finish_kernel, factor),
        grid=(parts,),
        in_specs=[block, full(step_grad.shape), full(conv.shape), full(head.shape)],
        out_specs=[block, full(step_grad.shape), full((KERNEL + 1, conv.shape[1])), full((2, heads)), full((1, heads))],
        out_shape=[
            jax.ShapeDtypeStruct((ROWS, CONV), BF16), jax.ShapeDtypeStruct((ROWS, HEADS), F32),
            jax.ShapeDtypeStruct((KERNEL + 1, conv.shape[1]), F32),
            jax.ShapeDtypeStruct((2, heads), F32), jax.ShapeDtypeStruct((1, heads), F32),
        ],
        compiler_params=pltpu.CompilerParams(vmem_limit_bytes=VMEM),
        name="finish",
    )(input_grad, step_grad, conv, head)


def passed_along(value, axis, steps):
    count = lax.axis_size(axis)
    initial, last = (max(0, -steps), min(count, count - steps))
    return lax.ppermute(value, axis, [(source, source + steps) for source in range(initial, last)])


def local(mixer_input, step_raw, out_grad, conv_weight, conv_bias, step_bias, decay_log, skip_gain):
    mixer, raw, dy = mixer_input[0], step_raw[0], out_grad[0]
    halo = passed_along(mixer[ROWS - 8 :], "ctx", 1)
    input_grad, step_grad, conv, head = mixer_grads(
        mixer, halo, conv_weight, conv_bias[None], raw, step_bias[None], decay_log[None], skip_gain[None], dy
    )
    factor = 1.0 / math.sqrt(lax.axis_size("dp") * ROWS * lax.axis_size("ctx"))
    input_grad, step_grad, conv, head, gain = finish(factor, input_grad, step_grad, conv, head)
    return input_grad[None], step_grad[None], conv, head, gain[0]


def solution(mesh):
    spread = P("dp", "ctx", None)
    in_specs = (spread, spread, spread, P(), P(), P(), P(), P())
    out_specs = (spread, spread, P(None, "dp"), P(None, "dp"), P("dp"))
    return jax.shard_map(local, mesh=mesh, in_specs=in_specs, out_specs=out_specs, check_vma=False)
```

```python
import functools
import math

import jax
import jax.numpy as jnp
from jax import lax
from jax.experimental import pallas as pl
from jax.experimental.pallas import tpu as pltpu
from jax.sharding import PartitionSpec as P

HEADS = 128
HEAD_DIM = 64
STATE = 128
GROUPS = 8
KERNEL = 4
ROWS = 128
INNER = 8192
CONV = 10240
GROUP_HEADS = HEADS // GROUPS
GROUP_PAIRS = GROUP_HEADS // 2
GROUP_LANES = GROUP_HEADS * HEAD_DIM
PAIRS = HEADS // 2
HALF = PAIRS // 2
MESH = pl.DeviceIdType.MESH
F32 = jnp.float32
BF16 = jnp.bfloat16
VMEM = 60 << 20
BATCHES = 4
BLOCK_ROWS = 64
FIRST, SLICE = 2, 3
FINISH_PARTS = 2
EXACT = lax.Precision.HIGHEST


def dot(a, b, precision=None):
    return jnp.dot(a, b, precision=precision, preferred_element_type=F32)


def dot_nt(a, b):
    return lax.dot_general(a, b, (((1,), (1,)), ((), ())), preferred_element_type=F32)


def sigmoid(v):
    return 0.5 + 0.5 * jnp.tanh(0.5 * v)


def softplus(v):
    return jnp.maximum(v, 0.0) + jnp.log1p(jnp.exp(-jnp.abs(v)))


def iota(shape, dim):
    return lax.broadcasted_iota(jnp.int32, shape, dim)


def low_half(shape):
    return iota(shape, len(shape) - 1) < HEAD_DIM


def pair_of(columns, j):
    shape = (columns.shape[0], 2 * HEAD_DIM)
    first = jnp.broadcast_to(columns[:, 2 * j : 2 * j + 1], shape)
    second = jnp.broadcast_to(columns[:, 2 * j + 1 : 2 * j + 2], shape)
    return jnp.where(low_half(shape), first, second)


def mixer_kernel(
    mix_hbm, halo_ref, weight_ref, shift_ref, raw_ref, bias_ref, decay_ref, gain_ref, dy_hbm,
    ig_hbm, step_ref, conv_ref, head_ref,
    mix_ref, dy_ref, ig_ref, run_ref, run_t_ref, sp_ref, close_own, close_oth, close_out, close_in, decay_own, decay_oth, decay_in, pad, dpad,
    xm, bm, cm, scores, dxi, dsc, sum_s, sum_r, s_own, g_own, s_oth, g_oth, sg_out, sg_in, hl_out, hl_in,
    h_all, l_all, h_oth, l_oth, acc_b, acc_c, col_s, xc, dyg, close, ones, ent, use, row_g, full_u, full_q, full_g,
    last, spill, spill_in, taps, rows, taps_oth, rows_oth, shards, arrived, flat, packed, packed_in, total, total_oth,
    e_send, e_recv, k_send, k_recv, x_send, x_recv, y_send, y_recv, sg_send, sg_recv, hl_send, hl_recv,
    p_send, p_recv, q_send, q_recv, sp_send, sp_recv, t_send, t_recv, d_send, d_recv, c_send, c_recv, o_send, o_recv,
    in_sem, out_sem, last_sem,
):
    dp = lax.axis_index("dp")
    ctx = lax.axis_index("ctx")
    shard_count = lax.axis_size("dp")
    devices = lax.axis_size("ctx")
    core = lax.rem(ctx, 2)
    chip = ctx // 2
    z, y = chip // 4, lax.rem(chip, 4)
    chips = devices // 2
    other = ctx + 1 - 2 * core
    beyond = lax.rem(ctx + devices - 1 + 2 * core, devices)
    half_blocks = HALF * STATE // BLOCK_ROWS
    mine = core * half_blocks
    half_groups = GROUPS // 2
    mine_group = core * half_groups
    theirs_group = half_groups - mine_group
    shape = (ROWS, ROWS)
    first = core == 0
    low = low_half(shape)
    low_row = low_half((1, 128))

    def chip_at(r):
        return lax.rem(z + r // 4, 4) * 4 + lax.rem(y + r, 4)

    def chip_before(r):
        return lax.rem(z + 4 - r // 4, 4) * 4 + lax.rem(y + 4 - lax.rem(r, 4), 4)

    def dp_at(r):
        return lax.rem(dp + r, shard_count)

    def tile(start):
        return pl.ds(pl.multiple_of(start, 128), 128)

    def group_lanes(g):
        return (
            pl.ds(pl.multiple_of(GROUP_LANES * g, 128), GROUP_LANES),
            tile(INNER + STATE * g),
            tile(INNER + GROUPS * STATE + STATE * g),
        )

    def loads(g):
        lanes = group_lanes(g)
        copies = [
            pltpu.make_async_copy(mix_hbm.at[:, part], mix_ref.at[:, part], in_sem.at[g, n])
            for n, part in enumerate(lanes)
        ]
        copies.append(pltpu.make_async_copy(dy_hbm.at[:, lanes[0]], dy_ref.at[:, lanes[0]], in_sem.at[g, 3]))
        return copies

    def stores(g):
        top = pl.ds(0, ROWS - 16)
        return [
            pltpu.make_async_copy(ig_ref.at[top, part], ig_hbm.at[top, part], out_sem.at[g, n])
            for n, part in enumerate(group_lanes(g))
        ]

    def group_of(u):
        return jnp.where(lax.rem(u, 2) == 0, theirs_group, mine_group) + u // 2

    def load(u, _):
        for copy in loads(group_of(u)):
            copy.start()
        return 0

    lax.fori_loop(0, GROUPS, load, 0)
    barrier = pltpu.get_barrier_semaphore()
    for device in (other, beyond):
        pl.semaphore_signal(barrier, inc=1, device_id=(dp, device), device_id_type=MESH)
    for r in range(1, shard_count):
        pl.semaphore_signal(barrier, inc=1, device_id=(dp_at(r), ctx), device_id_type=MESH)

    def greet(r, _):
        pl.semaphore_signal(barrier, inc=1, device_id=(dp, chip_at(r) * 2 + core), device_id_type=MESH)
        return 0

    lax.fori_loop(1, chips, greet, 0)

    def remote(src, dst, send, recv, device, d=None):
        return pltpu.make_async_remote_copy(
            src_ref=src, dst_ref=dst, send_sem=send, recv_sem=recv,
            device_id=(dp if d is None else d, device), device_id_type=MESH,
        )

    rate = -jnp.exp(decay_ref[...])
    spread = softplus(raw_ref[...].astype(F32) + bias_ref[...])
    lower = jnp.where(iota(shape, 0) >= iota(shape, 1), 1.0, 0.0).astype(F32)
    running = dot(lower, spread * rate, EXACT)
    sp_ref[...] = spread
    run_ref[...] = running
    run_t_ref[...] = running.T
    close_own[...] = jnp.broadcast_to(running[ROWS - 1 : ROWS, :], (8, HEADS))
    sum_s[...] = jnp.zeros((ROWS, HEADS), F32)
    col_s[...] = jnp.zeros((ROWS, HEADS), F32)

    def conv_pre(slot, lanes):
        here = pad.at[slot]
        here[0:8, :] = halo_ref[:, lanes].astype(F32)
        here[8:, :] = mix_ref[:, lanes].astype(F32)
        pre = jnp.broadcast_to(shift_ref[:, lanes], (ROWS, 128))
        for k in range(KERNEL):
            pre = pre + weight_ref[k : k + 1, lanes] * here[5 + k : 5 + k + ROWS, :]
        return pre

    def mixed(slot, lanes):
        pre = conv_pre(slot, lanes)
        return (pre * sigmoid(pre)).astype(BF16)

    def group_states(g):
        b16 = mixed(GROUP_PAIRS, tile(INNER + STATE * g))
        c16 = mixed(GROUP_PAIRS + 1, tile(INNER + GROUPS * STATE + STATE * g))
        bm[g] = b16
        cm[g] = c16
        scores[g] = jnp.where(iota(shape, 1) >= iota(shape, 0), dot_nt(b16, c16), 0.0)
        dsc[g] = jnp.zeros(shape, F32)
        b_t = b16.astype(F32).T.astype(BF16)
        c_t = c16.astype(F32).T.astype(BF16)
        back = lax.rem(HEADS - GROUP_HEADS * g, HEADS)
        run = pltpu.roll(run_ref[...], back, 1)
        step = pltpu.roll(sp_ref[...], back, 1)
        grown = jnp.exp(run)
        to_close = jnp.exp(run[ROWS - 1 : ROWS, :] - run) * step
        for j in range(GROUP_PAIRS):
            at = pl.ds(2 * (GROUP_PAIRS * g + j), 2)
            lanes = tile(GROUP_LANES * g + 128 * j)
            x16 = mixed(j, lanes)
            xm[:, lanes] = x16
            close_2 = pair_of(to_close, j)
            close[:, lanes] = close_2
            x_closed = (x16.astype(F32) * close_2).astype(BF16)
            xc[:, lanes] = x_closed
            state = dot(b_t, x_closed)
            s_own[at] = state.astype(BF16).reshape(2, BLOCK_ROWS, 128)
            dy_grown = (dy_ref[:, lanes].astype(F32) * pair_of(grown, j)).astype(BF16)
            dyg[:, lanes] = dy_grown
            state = dot(c_t, dy_grown)
            g_own[at] = state.astype(BF16).reshape(2, BLOCK_ROWS, 128)

    def batch(i):
        return pl.ds(i * chips, chips)

    def swaps(i):
        there = pl.ds(half_blocks - mine + i * chips, chips)
        return (
            remote(s_own.at[there], s_oth.at[batch(i)], x_send.at[i], x_recv.at[i], other),
            remote(g_own.at[there], g_oth.at[batch(i)], y_send.at[i], y_recv.at[i], other),
        )

    def swap_back(i):
        there = pl.ds(mine + i * chips, chips)
        return (
            remote(h_oth.at[batch(i)], h_all.at[there], p_send.at[i], p_recv.at[i], other),
            remote(l_oth.at[batch(i)], l_all.at[there], q_send.at[i], q_recv.at[i], other),
        )

    close_swap = remote(close_own, close_oth, e_send.at[0], e_recv.at[0], other)

    def close_copy(r):
        return remote(close_out, close_in.at[chip], k_send.at[r], k_recv.at[r], chip_at(r) * 2 + core)

    def sg_copy(i, r):
        q = chip_at(r)
        return remote(sg_out.at[i, q], sg_in.at[i, chip], sg_send.at[i, r], sg_recv.at[i, r], q * 2 + core)

    def hl_copy(i, r):
        q = chip_at(r)
        return remote(hl_out.at[i, q], hl_in.at[i, chip], hl_send.at[i, r], hl_recv.at[i, r], q * 2 + core)

    def ordered(held, sent):
        return jnp.where(first, held, sent), jnp.where(first, sent, held)

    def spread_pairs(closing, pairs):
        head = iota(closing.shape, 1)
        picked = jnp.where(head // 2 == pairs, closing, 0.0)
        shape = (HEADS, 128)
        lanes = jnp.where(lax.rem(iota(shape, 0), 2) == iota(shape, 1) // HEAD_DIM, 1.0, 0.0).astype(F32)
        return jnp.exp(dot(picked, lanes, EXACT))

    def held_decays(closing_ref):
        pairs = core * HALF + iota((HALF, HEADS), 0)
        return spread_pairs(jnp.broadcast_to(closing_ref[0:1, :], (HALF, HEADS)), pairs)

    def values(ref, oth, b):
        return ordered(ref[mine + b].astype(F32), oth[b].astype(F32))

    def both_decays(b):
        row = pl.ds(b // 2, 1)
        return ordered(decay_own[row, :], decay_oth[row, :])

    def build(u, _):
        i = u // 2
        theirs = lax.rem(u, 2) == 0
        for copy in loads(group_of(u)):
            copy.wait()
        group_states(group_of(u))

        @pl.when(u == 0)
        def _():
            pl.semaphore_wait(barrier, chips + shard_count)
            close_swap.start()

        @pl.when(theirs)
        def _():
            for copy in swaps(i):
                copy.start()

        @pl.when(u == 1)
        def _():
            close_swap.wait_recv()
            close_out[...] = close_own[...] + close_oth[...]
            decay_own[...] = held_decays(close_own)
            decay_oth[...] = held_decays(close_oth)
            close_in[chip] = close_out[...]

            def send(r, _):
                close_copy(r).start()
                return 0

            lax.fori_loop(1, chips, send, 0)

        @pl.when(jnp.logical_not(theirs))
        def _():
            for copy in swaps(i):
                copy.wait_recv()

            def combine(r, _):
                q = chip_at(r)
                b = chips * i + q
                a0, a1 = both_decays(b)
                s0, s1 = values(s_own, s_oth, b)
                g0, g1 = values(g_own, g_oth, b)
                sg_out[i, q, 0] = (a1 * s0 + s1).astype(BF16)
                sg_out[i, q, 1] = (a0 * g1 + g0).astype(BF16)

                @pl.when(r > 0)
                def _():
                    sg_copy(i, r).start()

                return 0

            lax.fori_loop(0, chips, combine, 0)
            sg_in[i, chip] = sg_out[i, chip]

        return 0

    lax.fori_loop(0, 2 * BATCHES, build, 0)

    def inside(n, _):
        g = n // 2
        back = lax.rem(HEADS - 8 * n, HEADS)
        run = pltpu.roll(run_ref[...], back, 1)
        steps = pltpu.roll(sp_ref[...], back, 1)
        for j in range(4):
            lanes = tile(512 * n + 128 * j)
            dy = dy_ref[:, lanes].astype(F32)
            split = jnp.concatenate([jnp.where(low, dy, 0.0), jnp.where(low, 0.0, dy)], axis=0).astype(BF16)
            d_weights = dot_nt(xm[:, lanes], split)
            weights = []
            gathered = jnp.zeros(shape, F32)
            for i in range(2):
                head = 2 * j + i
                at = pl.ds(8 * n + head, 1)
                step = steps[:, head : head + 1]
                d_weight = d_weights[:, 128 * i : 128 * i + 128]
                decay = jnp.exp(jnp.minimum(run_t_ref[at, :] - run[:, head : head + 1], 0.0))
                plain = decay * scores[g]
                weights.append((plain * step).astype(BF16))
                product = d_weight * plain
                col_s[:, head : head + 1] = jnp.sum(product, axis=1, keepdims=True)
                sum_r[at, :] = jnp.sum(product * step, axis=0, keepdims=True)
                gathered = gathered + d_weight * decay * step
            dsc[g] += gathered
            dxi[:, lanes] = dot(jnp.concatenate(weights, axis=1), split).astype(BF16)
        kept = jnp.where(iota(shape, 1) < 8, col_s[...], 0.0)
        sum_s[...] += pltpu.roll(kept, lax.rem(8 * n, HEADS), 1)
        return 0

    def scan(i):
        def arrive(r, _):
            @pl.when(i == 0)
            def _():
                close_copy(r).wait_recv()

            sg_copy(i, r).wait_recv()
            return 0

        lax.fori_loop(1, chips, arrive, 0)
        decay_in[...] = spread_pairs(close_in[:, 0, :], (mine + chips * i + chip) // 2)

        def both(c, states):
            forth, back = states
            d = chips - 1 - c
            hl_out[i, c, 0] = forth.astype(BF16)
            hl_out[i, d, 1] = back.astype(BF16)
            forth = decay_in[pl.ds(c, 1), :] * forth + sg_in[i, c, 0].astype(F32)
            back = decay_in[pl.ds(d, 1), :] * back + sg_in[i, d, 1].astype(F32)
            return forth, back

        zero = jnp.zeros((BLOCK_ROWS, 128), F32)
        lax.fori_loop(0, chips, both, (zero, zero), unroll=4)

        def send(r, _):
            hl_copy(i, r).start()
            return 0

        lax.fori_loop(1, chips, send, 0)
        hl_in[i, chip] = hl_out[i, chip]

    def middle(i, _):
        lax.fori_loop(jnp.maximum(SLICE * (i - 1) + FIRST, 0), SLICE * i + FIRST, inside, 0)
        scan(i)
        return 0

    lax.fori_loop(0, BATCHES, middle, 0)
    lax.fori_loop(SLICE * (BATCHES - 1) + FIRST, PAIRS // 4, inside, 0)

    ones[...] = jnp.where(iota(ones.shape, 0) // HEAD_DIM == iota(ones.shape, 1), 1.0, 0.0).astype(BF16)
    dpad[:, ROWS:, :] = jnp.zeros((GROUP_PAIRS + 2, 8, 128), F32)
    taps[...] = jnp.zeros(taps.shape, F32)
    for ref in (full_u, full_q, full_g, row_g):
        ref[...] = jnp.zeros(ref.shape, F32)

    def conv_back(slot, grad, pre, gate, lanes):
        here = pad.at[slot]
        there = dpad.at[slot]
        dpre = grad * (gate * (1.0 + pre * (1.0 - gate)))
        there[0:ROWS, :] = dpre
        whole = jnp.zeros(shape, F32)
        for k in range(KERNEL):
            whole = whole + weight_ref[k : k + 1, lanes] * there[3 - k : 3 - k + ROWS, :]
            taps[k : k + 1, lanes] = jnp.sum(dpre * here[5 + k : 5 + k + ROWS, :], axis=0, keepdims=True)
        taps[4:5, lanes] = jnp.sum(dpre, axis=0, keepdims=True)
        ig_ref[:, lanes] = whole.astype(BF16)
        last[:, lanes] = whole[ROWS - 16 :, :]
        edge = dpre[0:8, :]
        row = iota((8, 128), 0)
        spilled = jnp.zeros((8, 128), F32)
        for k in range(KERNEL - 1):
            moved = pltpu.roll(edge, 5 + k, 0)
            spilled = spilled + jnp.where(row >= 5 + k, weight_ref[k : k + 1, lanes] * moved, 0.0)
        spill[:, lanes] = spilled

    before = lax.rem(ctx + devices - 1, devices)

    def spill_copies(g):
        return [
            remote(spill.at[:, lanes], spill_in.at[:, lanes], sp_send.at[g, n], sp_recv.at[g, n], before)
            for n, lanes in enumerate(group_lanes(g))
        ]

    def group_grads(g):
        back = lax.rem(HEADS - GROUP_HEADS * g, HEADS)
        b16, c16 = bm[g], cm[g]
        gain = pltpu.roll(jnp.broadcast_to(gain_ref[...], (8, HEADS)), back, 1)
        acc_b[...] = jnp.zeros(shape, F32)
        acc_c[...] = jnp.zeros(shape, F32)
        for j in range(GROUP_PAIRS):
            lanes = tile(GROUP_LANES * g + 128 * j)
            here = pl.ds(128 * j, 128)
            at = pl.ds(2 * (GROUP_PAIRS * g + j), 2)
            pre = conv_pre(j, lanes)
            gate = sigmoid(pre)
            x = xm[:, lanes].astype(F32)
            dy = dy_ref[:, lanes].astype(F32)
            h16 = h_all[at].reshape(STATE, 128)
            l16 = l_all[at].reshape(STATE, 128)
            left = dot(b16, l16)
            ent[:, here] = (dy * dot(c16, h16)).astype(BF16)
            use[:, here] = (x * left).astype(BF16)
            row_g[0:1, here] = jnp.sum(h16.astype(F32) * l16.astype(F32), axis=0, keepdims=True)
            row_g[1:2, here] = jnp.sum(dy * x, axis=0, keepdims=True)
            acc_c[...] += dot_nt(dyg[:, lanes], h16)
            acc_b[...] += dot_nt(xc[:, lanes], l16)
            grad_x = dxi[:, lanes].astype(F32) + close[:, lanes] * left + pair_of(gain, j)[0:1, :] * dy
            conv_back(j, grad_x, pre, gate, lanes)
        d_scores = jnp.where(iota(shape, 1) >= iota(shape, 0), dsc[g], 0.0)
        grad_b = acc_b[...] + dot(d_scores.astype(BF16), c16)
        grad_c = acc_c[...] + dot(d_scores.T.astype(BF16), b16)
        for i, grad in enumerate((grad_b, grad_c)):
            lanes = tile(INNER + GROUPS * STATE * i + STATE * g)
            pre = conv_pre(GROUP_PAIRS + i, lanes)
            conv_back(GROUP_PAIRS + i, grad, pre, sigmoid(pre), lanes)
        forward = lax.rem(GROUP_HEADS * g, HEADS)
        full_u[...] += pltpu.roll(dot(ent[...], ones[...]), forward, 1)
        full_q[...] += pltpu.roll(dot(use[...], ones[...]), forward, 1)
        rest = row_g[...]
        thirds = []
        for _ in range(3):
            part = rest.astype(BF16)
            thirds.append(part.astype(F32))
            rest = rest - thirds[-1]
        sums = dot(jnp.concatenate(thirds, axis=0).astype(BF16), ones[...])
        full_g[...] += pltpu.roll(sums[0:8] + sums[8:16] + sums[16:24], forward, 1)

        for copy in stores(g):
            copy.start()

        @pl.when(ctx > 0)
        def _():
            for copy in spill_copies(g):
                copy.start()

    def gather(i):
        def finish(r, _):
            q = chip_before(r)

            @pl.when(r > 0)
            def _():
                hl_copy(i, r).wait_recv()

            b = chips * i + q
            a0, a1 = both_decays(b)
            s0, _ = values(s_own, s_oth, b)
            _, g1 = values(g_own, g_oth, b)
            h0 = hl_in[i, q, 0]
            h1 = (a0 * h0.astype(F32) + s0).astype(BF16)
            l1 = hl_in[i, q, 1]
            l0 = (a1 * l1.astype(F32) + g1).astype(BF16)
            h_all[mine + b] = jnp.where(first, h0, h1)
            h_oth[b] = jnp.where(first, h1, h0)
            l_all[mine + b] = jnp.where(first, l0, l1)
            l_oth[b] = jnp.where(first, l1, l0)
            return 0

        lax.fori_loop(0, chips, finish, 0)
        for copy in swap_back(i):
            copy.start()

    def outer(u, _):
        i = u // 2
        held = lax.rem(u, 2) == 0

        @pl.when(held)
        def _():
            gather(i)

        @pl.when(jnp.logical_not(held))
        def _():
            for copy in swap_back(i):
                copy.wait_recv()

        group_grads(jnp.where(held, mine_group, theirs_group) + i)
        return 0

    lax.fori_loop(0, 2 * BATCHES, outer, 0)

    closing = run_ref[ROWS - 1 : ROWS, :]
    running = run_ref[...]
    steps = sp_ref[...]
    direct_q = jnp.exp(closing - running) * full_q[...]
    used_q = direct_q * steps
    summed = sum_r[...].T + jnp.exp(running) * full_u[...] - sum_s[...] * steps - used_q
    upper = jnp.where(iota(shape, 1) >= iota(shape, 0), 1.0, 0.0).astype(F32)
    constant = jnp.sum(used_q, axis=0, keepdims=True) + jnp.exp(closing) * full_g[0:1, :]
    d_logs = dot(upper, summed, EXACT) + constant
    d_spread = (d_logs * (-jnp.exp(decay_ref[...])) + sum_s[...] + direct_q).astype(BF16).astype(F32)
    step_grad = d_spread * sigmoid(raw_ref[...].astype(F32) + bias_ref[...])
    step_ref[...] = step_grad
    rows[...] = jnp.zeros((8, HEADS), F32)
    rows[0:1, :] = -jnp.exp(decay_ref[...]) * jnp.sum(d_logs * steps, axis=0, keepdims=True)
    rows[1:2, :] = jnp.sum(step_grad, axis=0, keepdims=True)
    rows[2:3, :] = full_g[1:2, :]

    width = total.shape[1]
    half = width // 2

    def columns(shard, part):
        return pl.ds(pl.multiple_of(shard * (2 * width) + part * width, 128), width)

    sums = [
        remote(taps.at[:, columns(i, 1 - core)], taps_oth.at[i], t_send.at[i], t_recv.at[i], other)
        for i in range(shard_count)
    ]
    sums.append(remote(rows, rows_oth, t_send.at[shard_count], t_recv.at[shard_count], other))
    for copy in sums:
        copy.start()
    for copy in sums:
        copy.wait()
    for i in range(shard_count):
        shards[i, :, 0:width] = taps[:, columns(i, core)] + taps_oth[i]
        shards[i, :, width:] = rows[...] + rows_oth[...]

    def shard_copy(r):
        return remote(shards.at[dp_at(r)], arrived.at[r], d_send.at[r], d_recv.at[r], ctx, dp_at(r))

    for r in range(1, shard_count):
        shard_copy(r).start()

    @pl.when(ctx < devices - 1)
    def _():
        def landed(g, _):
            for copy in spill_copies(g):
                copy.wait_recv()
            return 0

        lax.fori_loop(0, GROUPS, landed, 0)
        last[8:16, :] += spill_in[...]

    ig_ref[ROWS - 16 :, :] = last[...].astype(BF16)
    bottom = pl.ds(ROWS - 16, 16)
    last_store = pltpu.make_async_copy(ig_ref.at[bottom], ig_hbm.at[bottom], last_sem.at[0])
    last_store.start()

    summed = shards[dp]
    for r in range(1, shard_count):
        shard_copy(r).wait()
        summed = summed + arrived[r]
    flat[0:4, 0:half] = summed[0:4, 0:half]
    flat[4:8, 0:half] = summed[0:4, half:width]
    flat[8:9, 0:half] = summed[4:5, 0:half]
    flat[9:10, 0:half] = summed[4:5, half:width]
    flat[10:16, 0:half] = jnp.zeros((6, half), F32)
    flat[0:8, half:] = summed[:, width:]
    flat[8:16, half:] = jnp.zeros((8, 128), F32)
    packed[...] = flat[...].astype(BF16)

    def chip_copy(r):
        return remote(packed, packed_in.at[r], c_send.at[r], c_recv.at[r], chip_at(r) * 2 + core)

    def send(r, _):
        chip_copy(r).start()
        return 0

    lax.fori_loop(1, chips, send, 0)

    close_swap.wait_send()
    last_store.wait()

    def stored(g, _):
        for copy in stores(g):
            copy.wait()
        return 0

    lax.fori_loop(0, GROUPS, stored, 0)

    def cleared(i, _):
        for copy in swaps(i) + swap_back(i):
            copy.wait_send()

        def sent(r, _):
            @pl.when(i == 0)
            def _():
                close_copy(r).wait_send()

            sg_copy(i, r).wait_send()
            hl_copy(i, r).wait_send()
            return 0

        lax.fori_loop(1, chips, sent, 0)
        return 0

    lax.fori_loop(0, BATCHES, cleared, 0)

    @pl.when(ctx > 0)
    def _():
        def left_here(g, _):
            for copy in spill_copies(g):
                copy.wait_send()
            return 0

        lax.fori_loop(0, GROUPS, left_here, 0)

    def take(r, _):
        chip_copy(r).wait()
        flat[...] += packed_in[r].astype(F32)
        return 0

    lax.fori_loop(1, chips, take, 0)
    total[0:4, 0:half] = flat[0:4, 0:half]
    total[0:4, half:] = flat[4:8, 0:half]
    total[4:5, 0:half] = flat[8:9, 0:half]
    total[4:5, half:] = flat[9:10, 0:half]
    total[5:8, :] = jnp.zeros((3, width), F32)
    final = remote(total, total_oth, o_send.at[0], o_recv.at[0], other)
    final.start()
    head_ref[...] = pltpu.roll(flat[0:8, half:], lax.rem(HEADS - (HEADS // shard_count) * dp, HEADS), 1)
    conv_ref[:, pl.ds(pl.multiple_of(core * width, 128), width)] = total[...]
    final.wait()
    conv_ref[:, pl.ds(pl.multiple_of((1 - core) * width, 128), width)] = total_oth[...]


def mixer_grads(mixer, halo, weight, shift, raw, bias, decay, gain, dy):
    chips = lax.axis_size("ctx") // 2
    shards = lax.axis_size("dp")
    width = CONV // shards // 2
    V = pltpu.VMEM
    dma = pltpu.SemaphoreType.DMA
    blocks = PAIRS * STATE // BLOCK_ROWS
    plane = V((ROWS, HEADS), F32)
    row = V((8, HEADS), F32)
    tall = V((GROUP_PAIRS + 2, ROWS + 8, 128), F32)
    group16 = V((GROUPS, ROWS, STATE), BF16)
    group32 = V((GROUPS, ROWS, ROWS), F32)
    inner = V((ROWS, INNER), BF16)
    whole = V((blocks, BLOCK_ROWS, 128), BF16)
    part = V((blocks // 2, BLOCK_ROWS, 128), BF16)
    sent = V((BATCHES, chips, 2, BLOCK_ROWS, 128), BF16)
    edge = V((8, CONV), F32)
    memory = pl.BlockSpec(memory_space=pltpu.VMEM)
    remote_memory = pl.BlockSpec(memory_space=pl.ANY)
    return pl.pallas_call(
        mixer_kernel,
        out_shape=[
            jax.ShapeDtypeStruct((ROWS, CONV), BF16), jax.ShapeDtypeStruct((ROWS, HEADS), F32),
            jax.ShapeDtypeStruct((8, 2 * width), F32), jax.ShapeDtypeStruct((8, HEADS), F32),
        ],
        in_specs=[remote_memory] + [memory] * 7 + [remote_memory],
        out_specs=[remote_memory] + [memory] * 3,
        scratch_shapes=[
            V((ROWS, CONV), BF16), inner, V((ROWS, CONV), BF16), plane, plane, plane, row, row, row, V((chips, 8, HEADS), F32),
            V((HALF, 128), F32), V((HALF, 128), F32), V((chips, 128), F32), tall, tall,
            inner, group16, group16, group32, inner, group32, plane, plane, whole, whole, part, part,
            sent, sent, sent, sent, whole, whole, part, part, plane, plane, plane,
            inner, inner, V((ROWS, INNER), F32), V((GROUP_LANES, 128), BF16),
            V((ROWS, GROUP_LANES), BF16), V((ROWS, GROUP_LANES), BF16), V((8, GROUP_LANES), F32), plane, plane, row,
            V((16, CONV), F32), edge, edge, edge, row,
            V((shards, 8, width), F32), row, V((shards, 8, width + 128), F32), V((shards, 8, width + 128), F32),
            V((16, width // 2 + 128), F32), V((16, width // 2 + 128), BF16),
            V((chips, 16, width // 2 + 128), BF16), V((8, width), F32), V((8, width), F32),
            dma((1,)), dma((1,)), dma((chips,)), dma((chips,)),
        ]
        + [dma((BATCHES,))] * 4 + [dma((BATCHES, chips))] * 4 + [dma((BATCHES,))] * 4
        + [dma((GROUPS, 3))] * 2 + [dma((shards + 1,))] * 2 + [dma((shards,))] * 2 + [dma((chips,))] * 2 + [dma((1,))] * 2
        + [dma((GROUPS, 4)), dma((GROUPS, 3)), dma((1,))],
        compiler_params=pltpu.CompilerParams(
            collective_id=0, has_side_effects=True, vmem_limit_bytes=VMEM
        ),
        name="mixer_grads",
    )(mixer, halo, weight, shift, raw, bias, decay, gain, dy)


def finish_kernel(factor, ig_ref, step_ref, conv_ref, head_ref, ig_out, step_out, conv_out, head_out, gain_out):
    ig_out[...] = ig_ref[...]

    @pl.when(pl.program_id(0) == 0)
    def _():
        step_out[...] = step_ref[...]
        conv_out[...] = conv_ref[0 : KERNEL + 1, :] * factor
        head_out[...] = head_ref[0:2, 0 : head_out.shape[1]] * factor
        gain_out[...] = head_ref[2:3, 0 : gain_out.shape[1]] * factor


def finish(factor, input_grad, step_grad, conv, head):
    heads = HEADS // lax.axis_size("dp")
    block = pl.BlockSpec((ROWS // FINISH_PARTS, CONV), lambda i: (i, 0))

    def full(shape):
        return pl.BlockSpec(shape, lambda i: (0,) * len(shape))

    return pl.pallas_call(
        functools.partial(finish_kernel, factor),
        grid=(FINISH_PARTS,),
        in_specs=[block, full(step_grad.shape), full(conv.shape), full(head.shape)],
        out_specs=[block, full(step_grad.shape), full((KERNEL + 1, conv.shape[1])), full((2, heads)), full((1, heads))],
        out_shape=[
            jax.ShapeDtypeStruct((ROWS, CONV), BF16), jax.ShapeDtypeStruct((ROWS, HEADS), F32),
            jax.ShapeDtypeStruct((KERNEL + 1, conv.shape[1]), F32),
            jax.ShapeDtypeStruct((2, heads), F32), jax.ShapeDtypeStruct((1, heads), F32),
        ],
        compiler_params=pltpu.CompilerParams(vmem_limit_bytes=VMEM),
        name="finish",
    )(input_grad, step_grad, conv, head)


def passed_along(value, axis, steps):
    count = lax.axis_size(axis)
    initial, last = (max(0, -steps), min(count, count - steps))
    return lax.ppermute(value, axis, [(source, source + steps) for source in range(initial, last)])


def local(mixer_input, step_raw, out_grad, conv_weight, conv_bias, step_bias, decay_log, skip_gain):
    mixer, raw, dy = mixer_input[0], step_raw[0], out_grad[0]
    halo = passed_along(mixer[ROWS - 8 :], "ctx", 1)
    input_grad, step_grad, conv, head = mixer_grads(
        mixer, halo, conv_weight, conv_bias[None], raw, step_bias[None], decay_log[None], skip_gain[None], dy
    )
    factor = 1.0 / math.sqrt(lax.axis_size("dp") * ROWS * lax.axis_size("ctx"))
    input_grad, step_grad, conv, head, gain = finish(factor, input_grad, step_grad, conv, head)
    return input_grad[None], step_grad[None], conv, head, gain[0]


def solution(mesh):
    spread = P("dp", "ctx", None)
    in_specs = (spread, spread, spread, P(), P(), P(), P(), P())
    out_specs = (spread, spread, P(None, "dp"), P(None, "dp"), P("dp"))
    return jax.shard_map(local, mesh=mesh, in_specs=in_specs, out_specs=out_specs, check_vma=False)
```

```python
import functools
import math

import jax
import jax.numpy as jnp
from jax import lax
from jax.experimental import pallas as pl
from jax.experimental.pallas import tpu as pltpu
from jax.sharding import PartitionSpec as P

HEADS = 128
HEAD_DIM = 64
STATE = 128
GROUPS = 8
KERNEL = 4
ROWS = 128
INNER = 8192
CONV = 10240
GROUP_HEADS = HEADS // GROUPS
GROUP_PAIRS = GROUP_HEADS // 2
GROUP_LANES = GROUP_HEADS * HEAD_DIM
PAIRS = HEADS // 2
HALF = PAIRS // 2
MESH = pl.DeviceIdType.MESH
F32 = jnp.float32
BF16 = jnp.bfloat16
VMEM = 60 << 20
BATCHES = 4
BLOCK_ROWS = 64
FIRST, SLICE = 2, 4
FINISH_PARTS = 2
EXACT = lax.Precision.HIGHEST


def dot(a, b, precision=None):
    return jnp.dot(a, b, precision=precision, preferred_element_type=F32)


def dot_nt(a, b):
    return lax.dot_general(a, b, (((1,), (1,)), ((), ())), preferred_element_type=F32)


def sigmoid(v):
    return 0.5 + 0.5 * jnp.tanh(0.5 * v)


def softplus(v):
    return jnp.maximum(v, 0.0) + jnp.log1p(jnp.exp(-jnp.abs(v)))


def iota(shape, dim):
    return lax.broadcasted_iota(jnp.int32, shape, dim)


def low_half(shape):
    return iota(shape, len(shape) - 1) < HEAD_DIM


def pair_of(columns, j):
    shape = (columns.shape[0], 2 * HEAD_DIM)
    first = jnp.broadcast_to(columns[:, 2 * j : 2 * j + 1], shape)
    second = jnp.broadcast_to(columns[:, 2 * j + 1 : 2 * j + 2], shape)
    return jnp.where(low_half(shape), first, second)


def mixer_kernel(
    mix_hbm, halo_ref, weight_ref, shift_ref, raw_ref, bias_ref, decay_ref, gain_ref, dy_hbm,
    ig_hbm, step_ref, conv_ref, head_ref,
    mix_ref, dy_ref, ig_ref, slope, run_ref, run_t_ref, sp_ref, close_own, close_oth, close_out, close_in, decay_own, decay_oth, decay_in, decay_row, pad, dpad,
    xm, bm, cm, scores, dxi, dsc, sum_s, sum_r, s_own, g_own, s_oth, g_oth, sg_out, sg_in, hl_out, hl_in, row_out, row_in,
    h_all, l_all, h_oth, l_oth, acc_b, acc_c, col_s, xc, dyg, close, ones, ent, use, row_g, full_u, full_q, full_g,
    last, spill, spill_in, taps, rows, taps_oth, rows_oth, shards, arrived, flat, packed, packed_in, total, total_oth,
    e_send, e_recv, k_send, k_recv, x_send, x_recv, y_send, y_recv, sg_send, sg_recv, hl_send, hl_recv, r_send, r_recv,
    p_send, p_recv, q_send, q_recv, sp_send, sp_recv, t_send, t_recv, d_send, d_recv, c_send, c_recv, o_send, o_recv,
    in_sem, out_sem, last_sem,
):
    dp = lax.axis_index("dp")
    ctx = lax.axis_index("ctx")
    shard_count = lax.axis_size("dp")
    devices = lax.axis_size("ctx")
    core = lax.rem(ctx, 2)
    chip = ctx // 2
    z, y = chip // 4, lax.rem(chip, 4)
    chips = devices // 2
    other = ctx + 1 - 2 * core
    beyond = lax.rem(ctx + devices - 1 + 2 * core, devices)
    half_blocks = HALF * STATE // BLOCK_ROWS
    mine = core * half_blocks
    half_groups = GROUPS // 2
    mine_group = core * half_groups
    theirs_group = half_groups - mine_group
    shape = (ROWS, ROWS)
    first = core == 0
    low = low_half(shape)
    low_row = low_half((1, 128))

    def chip_at(r):
        return lax.rem(z + r // 4, 4) * 4 + lax.rem(y + r, 4)

    def dp_at(r):
        return lax.rem(dp + r, shard_count)

    def tile(start):
        return pl.ds(pl.multiple_of(start, 128), 128)

    def group_lanes(g):
        return (
            pl.ds(pl.multiple_of(GROUP_LANES * g, 128), GROUP_LANES),
            tile(INNER + STATE * g),
            tile(INNER + GROUPS * STATE + STATE * g),
        )

    def loads(g):
        lanes = group_lanes(g)
        copies = [
            pltpu.make_async_copy(mix_hbm.at[:, part], mix_ref.at[:, part], in_sem.at[g, n])
            for n, part in enumerate(lanes)
        ]
        copies.append(pltpu.make_async_copy(dy_hbm.at[:, lanes[0]], dy_ref.at[:, lanes[0]], in_sem.at[g, 3]))
        return copies

    def stores(g):
        top = pl.ds(0, ROWS - 16)
        return [
            pltpu.make_async_copy(ig_ref.at[top, part], ig_hbm.at[top, part], out_sem.at[g, n])
            for n, part in enumerate(group_lanes(g))
        ]

    def group_of(u):
        return jnp.where(lax.rem(u, 2) == 0, theirs_group, mine_group) + u // 2

    def load(u, _):
        for copy in loads(group_of(u)):
            copy.start()
        return 0

    lax.fori_loop(0, GROUPS, load, 0)
    barrier = pltpu.get_barrier_semaphore()
    for device in (other, beyond):
        pl.semaphore_signal(barrier, inc=1, device_id=(dp, device), device_id_type=MESH)
    for r in range(1, shard_count):
        pl.semaphore_signal(barrier, inc=1, device_id=(dp_at(r), ctx), device_id_type=MESH)

    def greet(r, _):
        pl.semaphore_signal(barrier, inc=1, device_id=(dp, chip_at(r) * 2 + core), device_id_type=MESH)
        return 0

    lax.fori_loop(1, chips, greet, 0)

    def remote(src, dst, send, recv, device, d=None):
        return pltpu.make_async_remote_copy(
            src_ref=src, dst_ref=dst, send_sem=send, recv_sem=recv,
            device_id=(dp if d is None else d, device), device_id_type=MESH,
        )

    rate = -jnp.exp(decay_ref[...])
    spread = softplus(raw_ref[...].astype(F32) + bias_ref[...])
    lower = jnp.where(iota(shape, 0) >= iota(shape, 1), 1.0, 0.0).astype(F32)
    running = dot(lower, spread * rate, EXACT)
    sp_ref[...] = spread
    run_ref[...] = running
    run_t_ref[...] = running.T
    close_own[...] = jnp.broadcast_to(running[ROWS - 1 : ROWS, :], (8, HEADS))
    sum_s[...] = jnp.zeros((ROWS, HEADS), F32)
    col_s[...] = jnp.zeros((ROWS, HEADS), F32)

    def padded(slot, lanes):
        here = pad.at[slot]
        here[0:8, :] = halo_ref[:, lanes].astype(F32)
        here[8:, :] = mix_ref[:, lanes].astype(F32)
        return here

    def conv_pre(slot, lanes):
        here = padded(slot, lanes)
        pre = jnp.broadcast_to(shift_ref[:, lanes], (ROWS, 128))
        for k in range(KERNEL):
            pre = pre + weight_ref[k : k + 1, lanes] * here[5 + k : 5 + k + ROWS, :]
        return pre

    def mixed(slot, lanes):
        pre = conv_pre(slot, lanes)
        gate = sigmoid(pre)
        slope[:, lanes] = gate * (1.0 + pre * (1.0 - gate))
        return (pre * gate).astype(BF16)

    def group_states(g):
        b16 = mixed(GROUP_PAIRS, tile(INNER + STATE * g))
        c16 = mixed(GROUP_PAIRS + 1, tile(INNER + GROUPS * STATE + STATE * g))
        bm[g] = b16
        cm[g] = c16
        scores[g] = jnp.where(iota(shape, 1) >= iota(shape, 0), dot_nt(b16, c16), 0.0)
        dsc[g] = jnp.zeros(shape, F32)
        b_t = b16.astype(F32).T.astype(BF16)
        c_t = c16.astype(F32).T.astype(BF16)
        back = lax.rem(HEADS - GROUP_HEADS * g, HEADS)
        run = pltpu.roll(run_ref[...], back, 1)
        step = pltpu.roll(sp_ref[...], back, 1)
        grown = jnp.exp(run)
        to_close = jnp.exp(run[ROWS - 1 : ROWS, :] - run) * step
        for j in range(GROUP_PAIRS):
            at = pl.ds(2 * (GROUP_PAIRS * g + j), 2)
            lanes = tile(GROUP_LANES * g + 128 * j)
            x16 = mixed(j, lanes)
            xm[:, lanes] = x16
            close_2 = pair_of(to_close, j)
            close[:, lanes] = close_2
            x_closed = (x16.astype(F32) * close_2).astype(BF16)
            xc[:, lanes] = x_closed
            state = dot(b_t, x_closed)
            s_own[at] = state.astype(BF16).reshape(2, BLOCK_ROWS, 128)
            dy_grown = (dy_ref[:, lanes].astype(F32) * pair_of(grown, j)).astype(BF16)
            dyg[:, lanes] = dy_grown
            state = dot(c_t, dy_grown)
            g_own[at] = state.astype(BF16).reshape(2, BLOCK_ROWS, 128)

    def batch(i):
        return pl.ds(i * chips, chips)

    def swaps(i):
        there = pl.ds(half_blocks - mine + i * chips, chips)
        return (
            remote(s_own.at[there], s_oth.at[batch(i)], x_send.at[i], x_recv.at[i], other),
            remote(g_own.at[there], g_oth.at[batch(i)], y_send.at[i], y_recv.at[i], other),
        )

    def swap_back(i):
        there = pl.ds(mine + i * chips, chips)
        return (
            remote(h_oth.at[batch(i)], h_all.at[there], p_send.at[i], p_recv.at[i], other),
            remote(l_oth.at[batch(i)], l_all.at[there], q_send.at[i], q_recv.at[i], other),
        )

    close_swap = remote(close_own, close_oth, e_send.at[0], e_recv.at[0], other)

    def close_copy(r):
        return remote(close_out, close_in.at[chip], k_send.at[r], k_recv.at[r], chip_at(r) * 2 + core)

    def beside(r):
        return lax.rem(y + r, 4)

    def sg_copy(i, r):
        q = beside(r)
        return remote(sg_out.at[i, q], sg_in.at[i, y], sg_send.at[i, r], sg_recv.at[i, r], (z * 4 + q) * 2 + core)

    def row_copy(i, r):
        q = lax.rem(z + r, 4)
        return remote(row_out.at[i], row_in.at[i, z], r_send.at[i, r], r_recv.at[i, r], (q * 4 + y) * 2 + core)

    def hl_copy(i, r):
        q = beside(r)
        return remote(hl_out.at[i, q], hl_in.at[i, y], hl_send.at[i, r], hl_recv.at[i, r], (z * 4 + q) * 2 + core)

    def ordered(held, sent):
        return jnp.where(first, held, sent), jnp.where(first, sent, held)

    def spread_pairs(closing, pairs):
        head = iota(closing.shape, 1)
        picked = jnp.where(head // 2 == pairs, closing, 0.0)
        shape = (HEADS, 128)
        lanes = jnp.where(lax.rem(iota(shape, 0), 2) == iota(shape, 1) // HEAD_DIM, 1.0, 0.0).astype(F32)
        return jnp.exp(dot(picked, lanes, EXACT))

    def held_decays(closing_ref):
        pairs = core * HALF + iota((HALF, HEADS), 0)
        return spread_pairs(jnp.broadcast_to(closing_ref[0:1, :], (HALF, HEADS)), pairs)

    def values(ref, oth, b):
        return ordered(ref[mine + b].astype(F32), oth[b].astype(F32))

    def both_decays(b):
        row = pl.ds(b // 2, 1)
        return ordered(decay_own[row, :], decay_oth[row, :])

    def build(u, _):
        i = u // 2
        theirs = lax.rem(u, 2) == 0
        for copy in loads(group_of(u)):
            copy.wait()
        group_states(group_of(u))

        @pl.when(u == 0)
        def _():
            pl.semaphore_wait(barrier, chips + shard_count)
            close_swap.start()

        @pl.when(theirs)
        def _():
            for copy in swaps(i):
                copy.start()

        @pl.when(u == 1)
        def _():
            close_swap.wait_recv()
            close_out[...] = close_own[...] + close_oth[...]
            decay_own[...] = held_decays(close_own)
            decay_oth[...] = held_decays(close_oth)
            close_in[chip] = close_out[...]

            def send(r, _):
                close_copy(r).start()
                return 0

            lax.fori_loop(1, chips, send, 0)

        @pl.when(jnp.logical_not(theirs))
        def _():
            for copy in swaps(i):
                copy.wait_recv()

            def combine(r, _):
                q = beside(r)
                for k in range(4):
                    b = chips * i + 4 * q + k
                    a0, a1 = both_decays(b)
                    s0, s1 = values(s_own, s_oth, b)
                    g0, g1 = values(g_own, g_oth, b)
                    sg_out[i, q, k, 0] = (a1 * s0 + s1).astype(BF16)
                    sg_out[i, q, k, 1] = (a0 * g1 + g0).astype(BF16)

                @pl.when(r > 0)
                def _():
                    sg_copy(i, r).start()

                return 0

            lax.fori_loop(0, 4, combine, 0)
            sg_in[i, y] = sg_out[i, y]

        return 0

    lax.fori_loop(0, 2 * BATCHES, build, 0)

    def inside(n, _):
        g = n // 2
        back = lax.rem(HEADS - 8 * n, HEADS)
        run = pltpu.roll(run_ref[...], back, 1)
        steps = pltpu.roll(sp_ref[...], back, 1)
        for j in range(4):
            lanes = tile(512 * n + 128 * j)
            dy = dy_ref[:, lanes].astype(F32)
            split = jnp.concatenate([jnp.where(low, dy, 0.0), jnp.where(low, 0.0, dy)], axis=0).astype(BF16)
            d_weights = dot_nt(xm[:, lanes], split)
            weights = []
            gathered = jnp.zeros(shape, F32)
            for i in range(2):
                head = 2 * j + i
                at = pl.ds(8 * n + head, 1)
                step = steps[:, head : head + 1]
                d_weight = d_weights[:, 128 * i : 128 * i + 128]
                decay = jnp.exp(jnp.minimum(run_t_ref[at, :] - run[:, head : head + 1], 0.0))
                plain = decay * scores[g]
                weights.append((plain * step).astype(BF16))
                product = d_weight * plain
                col_s[:, head : head + 1] = jnp.sum(product, axis=1, keepdims=True)
                sum_r[at, :] = jnp.sum(product * step, axis=0, keepdims=True)
                gathered = gathered + d_weight * decay * step
            dsc[g] += gathered
            dxi[:, lanes] = dot(jnp.concatenate(weights, axis=1), split).astype(BF16)
        kept = jnp.where(iota(shape, 1) < 8, col_s[...], 0.0)
        sum_s[...] += pltpu.roll(kept, lax.rem(8 * n, HEADS), 1)
        return 0

    def row_totals(i):
        @pl.when(i == 0)
        def _():
            def known(r, _):
                close_copy(r).wait_recv()
                return 0

            lax.fori_loop(1, chips, known, 0)

        closing = close_in[:, 0, :]
        by_row = [jnp.sum(closing[4 * q : 4 * q + 4], axis=0, keepdims=True) for q in range(4)]
        by_row = jnp.concatenate(by_row + [jnp.zeros((4, HEADS), F32)], axis=0)
        for p in range(2):
            pair = (mine + chips * i + 4 * y) // 2 + p
            decay_in[i, p] = spread_pairs(closing, pair)
            decay_row[i, p] = spread_pairs(by_row, pair)
        for r in range(1, 4):
            sg_copy(i, r).wait_recv()
        for k in range(4):
            forth = jnp.zeros((BLOCK_ROWS, 128), F32)
            back = forth
            for c in range(4):
                d = 3 - c
                forth = decay_in[i, k // 2, pl.ds(4 * z + c, 1), :] * forth + sg_in[i, c, k, 0].astype(F32)
                back = decay_in[i, k // 2, pl.ds(4 * z + d, 1), :] * back + sg_in[i, d, k, 1].astype(F32)
            row_out[i, k, 0] = forth.astype(BF16)
            row_out[i, k, 1] = back.astype(BF16)
        for r in range(1, 4):
            row_copy(i, r).start()
        row_in[i, z] = row_out[i]

    def scan(i):
        for r in range(1, 4):
            row_copy(i, r).wait_recv()
        for k in range(4):
            forth = jnp.zeros((BLOCK_ROWS, 128), F32)
            back = forth
            for q in range(4):
                d = 3 - q
                step = decay_row[i, k // 2, q : q + 1, :] * forth + row_in[i, q, k, 0].astype(F32)
                forth = jnp.where(q < z, step, forth)
                step = decay_row[i, k // 2, d : d + 1, :] * back + row_in[i, d, k, 1].astype(F32)
                back = jnp.where(d > z, step, back)
            for c in range(4):
                d = 3 - c
                hl_out[i, c, k, 0] = forth.astype(BF16)
                hl_out[i, d, k, 1] = back.astype(BF16)
                forth = decay_in[i, k // 2, pl.ds(4 * z + c, 1), :] * forth + sg_in[i, c, k, 0].astype(F32)
                back = decay_in[i, k // 2, pl.ds(4 * z + d, 1), :] * back + sg_in[i, d, k, 1].astype(F32)
        for r in range(1, 4):
            hl_copy(i, r).start()
        hl_in[i, y] = hl_out[i, y]

    def middle(i, _):
        lax.fori_loop(jnp.maximum(SLICE * (i - 1) + FIRST, 0), SLICE * i + FIRST, inside, 0)

        @pl.when(i < BATCHES)
        def _():
            row_totals(i)

        @pl.when(i > 0)
        def _():
            scan(i - 1)

        return 0

    lax.fori_loop(0, BATCHES, middle, 0)
    lax.fori_loop(SLICE * (BATCHES - 1) + FIRST, PAIRS // 4, inside, 0)

    ones[...] = jnp.where(iota(ones.shape, 0) // HEAD_DIM == iota(ones.shape, 1), 1.0, 0.0).astype(BF16)
    dpad[:, ROWS:, :] = jnp.zeros((GROUP_PAIRS + 2, 8, 128), F32)
    taps[...] = jnp.zeros(taps.shape, F32)
    for ref in (full_u, full_q, full_g, row_g):
        ref[...] = jnp.zeros(ref.shape, F32)

    def conv_back(slot, grad, lanes):
        here = padded(slot, lanes)
        there = dpad.at[slot]
        dpre = grad * slope[:, lanes]
        there[0:ROWS, :] = dpre
        whole = jnp.zeros(shape, F32)
        for k in range(KERNEL):
            whole = whole + weight_ref[k : k + 1, lanes] * there[3 - k : 3 - k + ROWS, :]
            taps[k : k + 1, lanes] = jnp.sum(dpre * here[5 + k : 5 + k + ROWS, :], axis=0, keepdims=True)
        taps[4:5, lanes] = jnp.sum(dpre, axis=0, keepdims=True)
        ig_ref[:, lanes] = whole.astype(BF16)
        last[:, lanes] = whole[ROWS - 16 :, :]
        edge = dpre[0:8, :]
        row = iota((8, 128), 0)
        spilled = jnp.zeros((8, 128), F32)
        for k in range(KERNEL - 1):
            moved = pltpu.roll(edge, 5 + k, 0)
            spilled = spilled + jnp.where(row >= 5 + k, weight_ref[k : k + 1, lanes] * moved, 0.0)
        spill[:, lanes] = spilled

    before = lax.rem(ctx + devices - 1, devices)

    def spill_copies(g):
        return [
            remote(spill.at[:, lanes], spill_in.at[:, lanes], sp_send.at[g, n], sp_recv.at[g, n], before)
            for n, lanes in enumerate(group_lanes(g))
        ]

    def group_grads(g):
        back = lax.rem(HEADS - GROUP_HEADS * g, HEADS)
        b16, c16 = bm[g], cm[g]
        gain = pltpu.roll(jnp.broadcast_to(gain_ref[...], (8, HEADS)), back, 1)
        acc_b[...] = jnp.zeros(shape, F32)
        acc_c[...] = jnp.zeros(shape, F32)
        for j in range(GROUP_PAIRS):
            lanes = tile(GROUP_LANES * g + 128 * j)
            here = pl.ds(128 * j, 128)
            at = pl.ds(2 * (GROUP_PAIRS * g + j), 2)
            x = xm[:, lanes].astype(F32)
            dy = dy_ref[:, lanes].astype(F32)
            h16 = h_all[at].reshape(STATE, 128)
            l16 = l_all[at].reshape(STATE, 128)
            left = dot(b16, l16)
            ent[:, here] = (dy * dot(c16, h16)).astype(BF16)
            use[:, here] = (x * left).astype(BF16)
            row_g[0:1, here] = jnp.sum(h16.astype(F32) * l16.astype(F32), axis=0, keepdims=True)
            row_g[1:2, here] = jnp.sum(dy * x, axis=0, keepdims=True)
            acc_c[...] += dot_nt(dyg[:, lanes], h16)
            acc_b[...] += dot_nt(xc[:, lanes], l16)
            grad_x = dxi[:, lanes].astype(F32) + close[:, lanes] * left + pair_of(gain, j)[0:1, :] * dy
            conv_back(j, grad_x, lanes)
        d_scores = jnp.where(iota(shape, 1) >= iota(shape, 0), dsc[g], 0.0)
        grad_b = acc_b[...] + dot(d_scores.astype(BF16), c16)
        grad_c = acc_c[...] + dot(d_scores.T.astype(BF16), b16)
        for i, grad in enumerate((grad_b, grad_c)):
            lanes = tile(INNER + GROUPS * STATE * i + STATE * g)
            conv_back(GROUP_PAIRS + i, grad, lanes)
        forward = lax.rem(GROUP_HEADS * g, HEADS)
        full_u[...] += pltpu.roll(dot(ent[...], ones[...]), forward, 1)
        full_q[...] += pltpu.roll(dot(use[...], ones[...]), forward, 1)
        rest = row_g[...]
        thirds = []
        for _ in range(3):
            part = rest.astype(BF16)
            thirds.append(part.astype(F32))
            rest = rest - thirds[-1]
        sums = dot(jnp.concatenate(thirds, axis=0).astype(BF16), ones[...])
        full_g[...] += pltpu.roll(sums[0:8] + sums[8:16] + sums[16:24], forward, 1)

        for copy in stores(g):
            copy.start()

        @pl.when(ctx > 0)
        def _():
            for copy in spill_copies(g):
                copy.start()

    def gather(i):
        def finish(r, _):
            q = lax.rem(y + 4 - r, 4)

            @pl.when(r > 0)
            def _():
                hl_copy(i, r).wait_recv()

            for k in range(4):
                b = chips * i + 4 * q + k
                a0, a1 = both_decays(b)
                s0, _ = values(s_own, s_oth, b)
                _, g1 = values(g_own, g_oth, b)
                h0 = hl_in[i, q, k, 0]
                h1 = (a0 * h0.astype(F32) + s0).astype(BF16)
                l1 = hl_in[i, q, k, 1]
                l0 = (a1 * l1.astype(F32) + g1).astype(BF16)
                h_all[mine + b] = jnp.where(first, h0, h1)
                h_oth[b] = jnp.where(first, h1, h0)
                l_all[mine + b] = jnp.where(first, l0, l1)
                l_oth[b] = jnp.where(first, l1, l0)
            return 0

        lax.fori_loop(0, 4, finish, 0)
        for copy in swap_back(i):
            copy.start()

    def outer(u, _):
        i = u // 2
        held = lax.rem(u, 2) == 0

        @pl.when(u == 1)
        def _():
            scan(BATCHES - 1)

        @pl.when(held)
        def _():
            gather(i)

        @pl.when(jnp.logical_not(held))
        def _():
            for copy in swap_back(i):
                copy.wait_recv()

        group_grads(jnp.where(held, mine_group, theirs_group) + i)
        return 0

    lax.fori_loop(0, 2 * BATCHES, outer, 0)

    width = total.shape[1]
    half = width // 2

    def columns(shard, part):
        return pl.ds(pl.multiple_of(shard * (2 * width) + part * width, 128), width)

    sums = [
        remote(taps.at[:, columns(i, 1 - core)], taps_oth.at[i], t_send.at[i], t_recv.at[i], other)
        for i in range(shard_count)
    ]
    for copy in sums:
        copy.start()

    closing = run_ref[ROWS - 1 : ROWS, :]
    running = run_ref[...]
    steps = sp_ref[...]
    direct_q = jnp.exp(closing - running) * full_q[...]
    used_q = direct_q * steps
    summed = sum_r[...].T + jnp.exp(running) * full_u[...] - sum_s[...] * steps - used_q
    upper = jnp.where(iota(shape, 1) >= iota(shape, 0), 1.0, 0.0).astype(F32)
    constant = jnp.sum(used_q, axis=0, keepdims=True) + jnp.exp(closing) * full_g[0:1, :]
    d_logs = dot(upper, summed, EXACT) + constant
    d_spread = (d_logs * (-jnp.exp(decay_ref[...])) + sum_s[...] + direct_q).astype(BF16).astype(F32)
    step_grad = d_spread * sigmoid(raw_ref[...].astype(F32) + bias_ref[...])
    step_ref[...] = step_grad
    rows[...] = jnp.zeros((8, HEADS), F32)
    rows[0:1, :] = -jnp.exp(decay_ref[...]) * jnp.sum(d_logs * steps, axis=0, keepdims=True)
    rows[1:2, :] = jnp.sum(step_grad, axis=0, keepdims=True)
    rows[2:3, :] = full_g[1:2, :]

    rows_sum = remote(rows, rows_oth, t_send.at[shard_count], t_recv.at[shard_count], other)
    rows_sum.start()
    for copy in sums + [rows_sum]:
        copy.wait()
    for i in range(shard_count):
        shards[i, :, 0:width] = taps[:, columns(i, core)] + taps_oth[i]
        shards[i, :, width:] = rows[...] + rows_oth[...]

    def shard_copy(r):
        return remote(shards.at[dp_at(r)], arrived.at[r], d_send.at[r], d_recv.at[r], ctx, dp_at(r))

    for r in range(1, shard_count):
        shard_copy(r).start()

    @pl.when(ctx < devices - 1)
    def _():
        def landed(g, _):
            for copy in spill_copies(g):
                copy.wait_recv()
            return 0

        lax.fori_loop(0, GROUPS, landed, 0)
        last[8:16, :] += spill_in[...]

    ig_ref[ROWS - 16 :, :] = last[...].astype(BF16)
    bottom = pl.ds(ROWS - 16, 16)
    last_store = pltpu.make_async_copy(ig_ref.at[bottom], ig_hbm.at[bottom], last_sem.at[0])
    last_store.start()

    summed = shards[dp]
    for r in range(1, shard_count):
        shard_copy(r).wait()
        summed = summed + arrived[r]
    flat[0:4, 0:half] = summed[0:4, 0:half]
    flat[4:8, 0:half] = summed[0:4, half:width]
    flat[8:9, 0:half] = summed[4:5, 0:half]
    flat[9:10, 0:half] = summed[4:5, half:width]
    flat[10:16, 0:half] = jnp.zeros((6, half), F32)
    flat[0:8, half:] = summed[:, width:]
    flat[8:16, half:] = jnp.zeros((8, 128), F32)
    packed[...] = flat[...].astype(BF16)

    def chip_copy(r):
        return remote(packed, packed_in.at[r], c_send.at[r], c_recv.at[r], chip_at(r) * 2 + core)

    def send(r, _):
        chip_copy(r).start()
        return 0

    lax.fori_loop(1, chips, send, 0)

    close_swap.wait_send()
    last_store.wait()

    def stored(g, _):
        for copy in stores(g):
            copy.wait()
        return 0

    lax.fori_loop(0, GROUPS, stored, 0)

    def cleared(i, _):
        for copy in swaps(i) + swap_back(i):
            copy.wait_send()

        def sent(r, _):
            @pl.when(i == 0)
            def _():
                close_copy(r).wait_send()

            @pl.when(r < 4)
            def _():
                sg_copy(i, r).wait_send()
                row_copy(i, r).wait_send()
                hl_copy(i, r).wait_send()

            return 0

        lax.fori_loop(1, chips, sent, 0)
        return 0

    lax.fori_loop(0, BATCHES, cleared, 0)

    @pl.when(ctx > 0)
    def _():
        def left_here(g, _):
            for copy in spill_copies(g):
                copy.wait_send()
            return 0

        lax.fori_loop(0, GROUPS, left_here, 0)

    def take(r, _):
        chip_copy(r).wait()
        flat[...] += packed_in[r].astype(F32)
        return 0

    lax.fori_loop(1, chips, take, 0)
    total[0:4, 0:half] = flat[0:4, 0:half]
    total[0:4, half:] = flat[4:8, 0:half]
    total[4:5, 0:half] = flat[8:9, 0:half]
    total[4:5, half:] = flat[9:10, 0:half]
    total[5:8, :] = jnp.zeros((3, width), F32)
    final = remote(total, total_oth, o_send.at[0], o_recv.at[0], other)
    final.start()
    head_ref[...] = pltpu.roll(flat[0:8, half:], lax.rem(HEADS - (HEADS // shard_count) * dp, HEADS), 1)
    conv_ref[:, pl.ds(pl.multiple_of(core * width, 128), width)] = total[...]
    final.wait()
    conv_ref[:, pl.ds(pl.multiple_of((1 - core) * width, 128), width)] = total_oth[...]


def mixer_grads(mixer, halo, weight, shift, raw, bias, decay, gain, dy):
    chips = lax.axis_size("ctx") // 2
    shards = lax.axis_size("dp")
    width = CONV // shards // 2
    V = pltpu.VMEM
    dma = pltpu.SemaphoreType.DMA
    blocks = PAIRS * STATE // BLOCK_ROWS
    plane = V((ROWS, HEADS), F32)
    row = V((8, HEADS), F32)
    tall = V((GROUP_PAIRS + 2, ROWS + 8, 128), F32)
    group16 = V((GROUPS, ROWS, STATE), BF16)
    group32 = V((GROUPS, ROWS, ROWS), F32)
    inner = V((ROWS, INNER), BF16)
    whole = V((blocks, BLOCK_ROWS, 128), BF16)
    part = V((blocks // 2, BLOCK_ROWS, 128), BF16)
    sent = V((BATCHES, 4, 4, 2, BLOCK_ROWS, 128), BF16)
    edge = V((8, CONV), F32)
    memory = pl.BlockSpec(memory_space=pltpu.VMEM)
    remote_memory = pl.BlockSpec(memory_space=pl.ANY)
    return pl.pallas_call(
        mixer_kernel,
        out_shape=[
            jax.ShapeDtypeStruct((ROWS, CONV), BF16), jax.ShapeDtypeStruct((ROWS, HEADS), F32),
            jax.ShapeDtypeStruct((8, 2 * width), F32), jax.ShapeDtypeStruct((8, HEADS), F32),
        ],
        in_specs=[remote_memory] + [memory] * 7 + [remote_memory],
        out_specs=[remote_memory] + [memory] * 3,
        scratch_shapes=[
            V((ROWS, CONV), BF16), inner, V((ROWS, CONV), BF16), V((ROWS, CONV), F32), plane, plane, plane, row, row, row, V((chips, 8, HEADS), F32),
            V((HALF, 128), F32), V((HALF, 128), F32),
            V((BATCHES, 2, chips, 128), F32), V((BATCHES, 2, 8, 128), F32), tall, tall,
            inner, group16, group16, group32, inner, group32, plane, plane, whole, whole, part, part,
            sent, sent, sent, sent, V((BATCHES, 4, 2, BLOCK_ROWS, 128), BF16), sent, whole, whole, part, part, plane, plane, plane,
            inner, inner, V((ROWS, INNER), F32), V((GROUP_LANES, 128), BF16),
            V((ROWS, GROUP_LANES), BF16), V((ROWS, GROUP_LANES), BF16), V((8, GROUP_LANES), F32), plane, plane, row,
            V((16, CONV), F32), edge, edge, edge, row,
            V((shards, 8, width), F32), row, V((shards, 8, width + 128), F32), V((shards, 8, width + 128), F32),
            V((16, width // 2 + 128), F32), V((16, width // 2 + 128), BF16),
            V((chips, 16, width // 2 + 128), BF16), V((8, width), F32), V((8, width), F32),
            dma((1,)), dma((1,)), dma((chips,)), dma((chips,)),
        ]
        + [dma((BATCHES,))] * 4 + [dma((BATCHES, 4))] * 6 + [dma((BATCHES,))] * 4
        + [dma((GROUPS, 3))] * 2 + [dma((shards + 1,))] * 2 + [dma((shards,))] * 2 + [dma((chips,))] * 2 + [dma((1,))] * 2
        + [dma((GROUPS, 4)), dma((GROUPS, 3)), dma((1,))],
        compiler_params=pltpu.CompilerParams(
            collective_id=0, has_side_effects=True, vmem_limit_bytes=VMEM
        ),
        name="mixer_grads",
    )(mixer, halo, weight, shift, raw, bias, decay, gain, dy)


def finish_kernel(factor, ig_ref, step_ref, conv_ref, head_ref, ig_out, step_out, conv_out, head_out, gain_out):
    ig_out[...] = ig_ref[...]

    @pl.when(pl.program_id(0) == 0)
    def _():
        step_out[...] = step_ref[...]
        conv_out[...] = conv_ref[0 : KERNEL + 1, :] * factor
        head_out[...] = head_ref[0:2, 0 : head_out.shape[1]] * factor
        gain_out[...] = head_ref[2:3, 0 : gain_out.shape[1]] * factor


def finish(factor, input_grad, step_grad, conv, head):
    heads = HEADS // lax.axis_size("dp")
    block = pl.BlockSpec((ROWS // FINISH_PARTS, CONV), lambda i: (i, 0))

    def full(shape):
        return pl.BlockSpec(shape, lambda i: (0,) * len(shape))

    return pl.pallas_call(
        functools.partial(finish_kernel, factor),
        grid=(FINISH_PARTS,),
        in_specs=[block, full(step_grad.shape), full(conv.shape), full(head.shape)],
        out_specs=[block, full(step_grad.shape), full((KERNEL + 1, conv.shape[1])), full((2, heads)), full((1, heads))],
        out_shape=[
            jax.ShapeDtypeStruct((ROWS, CONV), BF16), jax.ShapeDtypeStruct((ROWS, HEADS), F32),
            jax.ShapeDtypeStruct((KERNEL + 1, conv.shape[1]), F32),
            jax.ShapeDtypeStruct((2, heads), F32), jax.ShapeDtypeStruct((1, heads), F32),
        ],
        compiler_params=pltpu.CompilerParams(vmem_limit_bytes=VMEM),
        name="finish",
    )(input_grad, step_grad, conv, head)


def passed_along(value, axis, steps):
    count = lax.axis_size(axis)
    initial, last = (max(0, -steps), min(count, count - steps))
    return lax.ppermute(value, axis, [(source, source + steps) for source in range(initial, last)])


def local(mixer_input, step_raw, out_grad, conv_weight, conv_bias, step_bias, decay_log, skip_gain):
    mixer, raw, dy = mixer_input[0], step_raw[0], out_grad[0]
    halo = passed_along(mixer[ROWS - 8 :], "ctx", 1)
    input_grad, step_grad, conv, head = mixer_grads(
        mixer, halo, conv_weight, conv_bias[None], raw, step_bias[None], decay_log[None], skip_gain[None], dy
    )
    factor = 1.0 / math.sqrt(lax.axis_size("dp") * ROWS * lax.axis_size("ctx"))
    input_grad, step_grad, conv, head, gain = finish(factor, input_grad, step_grad, conv, head)
    return input_grad[None], step_grad[None], conv, head, gain[0]


def solution(mesh):
    spread = P("dp", "ctx", None)
    in_specs = (spread, spread, spread, P(), P(), P(), P(), P())
    out_specs = (spread, spread, P(None, "dp"), P(None, "dp"), P("dp"))
    return jax.shard_map(local, mesh=mesh, in_specs=in_specs, out_specs=out_specs, check_vma=False)
```

```python
import functools
import math

import jax
import jax.numpy as jnp
from jax import lax
from jax.experimental import pallas as pl
from jax.experimental.pallas import tpu as pltpu
from jax.sharding import PartitionSpec as P

HEADS = 128
HEAD_DIM = 64
STATE = 128
GROUPS = 8
KERNEL = 4
ROWS = 128
INNER = 8192
CONV = 10240
GROUP_HEADS = HEADS // GROUPS
GROUP_PAIRS = GROUP_HEADS // 2
GROUP_LANES = GROUP_HEADS * HEAD_DIM
PAIRS = HEADS // 2
HALF = PAIRS // 2
MESH = pl.DeviceIdType.MESH
F32 = jnp.float32
BF16 = jnp.bfloat16
VMEM = 60 << 20
BATCHES = 4
BLOCK_ROWS = 64
FIRST, SLICE = 2, 4
FINISH_PARTS = 2
EXACT = lax.Precision.HIGHEST


def dot(a, b, precision=None):
    return jnp.dot(a, b, precision=precision, preferred_element_type=F32)


def dot_nt(a, b):
    return lax.dot_general(a, b, (((1,), (1,)), ((), ())), preferred_element_type=F32)


def sigmoid(v):
    return 0.5 + 0.5 * jnp.tanh(0.5 * v)


def softplus(v):
    return jnp.maximum(v, 0.0) + jnp.log1p(jnp.exp(-jnp.abs(v)))


def iota(shape, dim):
    return lax.broadcasted_iota(jnp.int32, shape, dim)


def low_half(shape):
    return iota(shape, len(shape) - 1) < HEAD_DIM


def pair_of(columns, j):
    shape = (columns.shape[0], 2 * HEAD_DIM)
    first = jnp.broadcast_to(columns[:, 2 * j : 2 * j + 1], shape)
    second = jnp.broadcast_to(columns[:, 2 * j + 1 : 2 * j + 2], shape)
    return jnp.where(low_half(shape), first, second)


def mixer_kernel(
    mix_hbm, halo_ref, weight_ref, shift_ref, raw_ref, bias_ref, decay_ref, gain_ref, dy_hbm,
    ig_hbm, step_ref, conv_ref, head_ref,
    mix_ref, dy_ref, ig_ref, slope, run_ref, run_t_ref, sp_ref, close_own, close_oth, close_out, close_in, decay_own, decay_oth, decay_in, decay_row, pad, dpad,
    xm, bm, cm, scores, dxi, dsc, sum_s, sum_r, s_own, g_own, s_oth, g_oth, sg_out, sg_in, hl_out, hl_in, row_out, row_in,
    h_all, l_all, h_oth, l_oth, col_s, xc, dyg, close, ones, ent, use, row_g, full_u, full_q, full_g,
    last, spill, spill_in, taps, rows, taps_oth, rows_oth, shards, arrived, flat, packed, packed_in, total, total_oth,
    e_send, e_recv, k_send, k_recv, x_send, x_recv, y_send, y_recv, sg_send, sg_recv, hl_send, hl_recv, r_send, r_recv,
    p_send, p_recv, q_send, q_recv, sp_send, sp_recv, t_send, t_recv, d_send, d_recv, c_send, c_recv, o_send, o_recv,
    in_sem, out_sem, last_sem,
):
    dp = lax.axis_index("dp")
    ctx = lax.axis_index("ctx")
    shard_count = lax.axis_size("dp")
    devices = lax.axis_size("ctx")
    core = lax.rem(ctx, 2)
    chip = ctx // 2
    z, y = chip // 4, lax.rem(chip, 4)
    chips = devices // 2
    other = ctx + 1 - 2 * core
    beyond = lax.rem(ctx + devices - 1 + 2 * core, devices)
    half_blocks = HALF * STATE // BLOCK_ROWS
    mine = core * half_blocks
    half_groups = GROUPS // 2
    mine_group = core * half_groups
    theirs_group = half_groups - mine_group
    shape = (ROWS, ROWS)
    first = core == 0
    low = low_half(shape)
    low_row = low_half((1, 128))

    def chip_at(r):
        return lax.rem(z + r // 4, 4) * 4 + lax.rem(y + r, 4)

    def dp_at(r):
        return lax.rem(dp + r, shard_count)

    def tile(start):
        return pl.ds(pl.multiple_of(start, 128), 128)

    def group_lanes(g):
        return (
            pl.ds(pl.multiple_of(GROUP_LANES * g, 128), GROUP_LANES),
            tile(INNER + STATE * g),
            tile(INNER + GROUPS * STATE + STATE * g),
        )

    def loads(g):
        lanes = group_lanes(g)
        copies = [
            pltpu.make_async_copy(mix_hbm.at[:, part], mix_ref.at[:, part], in_sem.at[g, n])
            for n, part in enumerate(lanes)
        ]
        copies.append(pltpu.make_async_copy(dy_hbm.at[:, lanes[0]], dy_ref.at[:, lanes[0]], in_sem.at[g, 3]))
        return copies

    def stores(g):
        top = pl.ds(0, ROWS - 16)
        return [
            pltpu.make_async_copy(ig_ref.at[top, part], ig_hbm.at[top, part], out_sem.at[g, n])
            for n, part in enumerate(group_lanes(g))
        ]

    def group_of(u):
        return jnp.where(lax.rem(u, 2) == 0, theirs_group, mine_group) + u // 2

    def load(u, _):
        for copy in loads(group_of(u)):
            copy.start()
        return 0

    lax.fori_loop(0, GROUPS, load, 0)
    barrier = pltpu.get_barrier_semaphore()
    for device in (other, beyond):
        pl.semaphore_signal(barrier, inc=1, device_id=(dp, device), device_id_type=MESH)
    for r in range(1, shard_count):
        pl.semaphore_signal(barrier, inc=1, device_id=(dp_at(r), ctx), device_id_type=MESH)

    def greet(r, _):
        pl.semaphore_signal(barrier, inc=1, device_id=(dp, chip_at(r) * 2 + core), device_id_type=MESH)
        return 0

    lax.fori_loop(1, chips, greet, 0)

    def remote(src, dst, send, recv, device, d=None):
        return pltpu.make_async_remote_copy(
            src_ref=src, dst_ref=dst, send_sem=send, recv_sem=recv,
            device_id=(dp if d is None else d, device), device_id_type=MESH,
        )

    rate = -jnp.exp(decay_ref[...])
    spread = softplus(raw_ref[...].astype(F32) + bias_ref[...])
    lower = jnp.where(iota(shape, 0) >= iota(shape, 1), 1.0, 0.0).astype(F32)
    running = dot(lower, spread * rate, EXACT)
    sp_ref[...] = spread
    run_ref[...] = running
    run_t_ref[...] = running.T
    close_own[...] = jnp.broadcast_to(running[ROWS - 1 : ROWS, :], (8, HEADS))
    sum_s[...] = jnp.zeros((ROWS, HEADS), F32)
    col_s[...] = jnp.zeros((ROWS, HEADS), F32)

    def padded(slot, lanes):
        here = pad.at[slot]
        here[0:8, :] = halo_ref[:, lanes].astype(F32)
        here[8:, :] = mix_ref[:, lanes].astype(F32)
        return here

    def conv_pre(slot, lanes):
        here = padded(slot, lanes)
        pre = jnp.broadcast_to(shift_ref[:, lanes], (ROWS, 128))
        for k in range(KERNEL):
            pre = pre + weight_ref[k : k + 1, lanes] * here[5 + k : 5 + k + ROWS, :]
        return pre

    def mixed(slot, lanes):
        pre = conv_pre(slot, lanes)
        gate = sigmoid(pre)
        slope[:, lanes] = gate * (1.0 + pre * (1.0 - gate))
        return (pre * gate).astype(BF16)

    def group_states(g):
        b16 = mixed(GROUP_PAIRS, tile(INNER + STATE * g))
        c16 = mixed(GROUP_PAIRS + 1, tile(INNER + GROUPS * STATE + STATE * g))
        bm[g] = b16
        cm[g] = c16
        scores[g] = jnp.where(iota(shape, 1) >= iota(shape, 0), dot_nt(b16, c16), 0.0)
        dsc[g] = jnp.zeros(shape, F32)
        b_t = b16.astype(F32).T.astype(BF16)
        c_t = c16.astype(F32).T.astype(BF16)
        back = lax.rem(HEADS - GROUP_HEADS * g, HEADS)
        run = pltpu.roll(run_ref[...], back, 1)
        step = pltpu.roll(sp_ref[...], back, 1)
        grown = jnp.exp(run)
        to_close = jnp.exp(run[ROWS - 1 : ROWS, :] - run) * step
        for j in range(GROUP_PAIRS):
            at = pl.ds(2 * (GROUP_PAIRS * g + j), 2)
            lanes = tile(GROUP_LANES * g + 128 * j)
            x16 = mixed(j, lanes)
            xm[:, lanes] = x16
            close_2 = pair_of(to_close, j)
            close[:, lanes] = close_2
            x_closed = (x16.astype(F32) * close_2).astype(BF16)
            xc[:, lanes] = x_closed
            state = dot(b_t, x_closed)
            s_own[at] = state.astype(BF16).reshape(2, BLOCK_ROWS, 128)
            dy_grown = (dy_ref[:, lanes].astype(F32) * pair_of(grown, j)).astype(BF16)
            dyg[:, lanes] = dy_grown
            state = dot(c_t, dy_grown)
            g_own[at] = state.astype(BF16).reshape(2, BLOCK_ROWS, 128)

    def batch(i):
        return pl.ds(i * chips, chips)

    def swaps(i):
        there = pl.ds(half_blocks - mine + i * chips, chips)
        return (
            remote(s_own.at[there], s_oth.at[batch(i)], x_send.at[i], x_recv.at[i], other),
            remote(g_own.at[there], g_oth.at[batch(i)], y_send.at[i], y_recv.at[i], other),
        )

    def swap_back(i):
        there = pl.ds(mine + i * chips, chips)
        return (
            remote(h_oth.at[batch(i)], h_all.at[there], p_send.at[i], p_recv.at[i], other),
            remote(l_oth.at[batch(i)], l_all.at[there], q_send.at[i], q_recv.at[i], other),
        )

    close_swap = remote(close_own, close_oth, e_send.at[0], e_recv.at[0], other)

    def close_copy(r):
        return remote(close_out, close_in.at[chip], k_send.at[r], k_recv.at[r], chip_at(r) * 2 + core)

    def beside(r):
        return lax.rem(y + r, 4)

    def sg_copy(i, r):
        q = beside(r)
        return remote(sg_out.at[i, q], sg_in.at[i, y], sg_send.at[i, r], sg_recv.at[i, r], (z * 4 + q) * 2 + core)

    def row_copy(i, r):
        q = lax.rem(z + r, 4)
        return remote(row_out.at[i], row_in.at[i, z], r_send.at[i, r], r_recv.at[i, r], (q * 4 + y) * 2 + core)

    def hl_copy(i, r):
        q = beside(r)
        return remote(hl_out.at[i, q], hl_in.at[i, y], hl_send.at[i, r], hl_recv.at[i, r], (z * 4 + q) * 2 + core)

    def ordered(held, sent):
        return jnp.where(first, held, sent), jnp.where(first, sent, held)

    def spread_pairs(closing, pairs):
        head = iota(closing.shape, 1)
        picked = jnp.where(head // 2 == pairs, closing, 0.0)
        shape = (HEADS, 128)
        lanes = jnp.where(lax.rem(iota(shape, 0), 2) == iota(shape, 1) // HEAD_DIM, 1.0, 0.0).astype(F32)
        return jnp.exp(dot(picked, lanes, EXACT))

    def held_decays(closing_ref):
        pairs = core * HALF + iota((HALF, HEADS), 0)
        return spread_pairs(jnp.broadcast_to(closing_ref[0:1, :], (HALF, HEADS)), pairs)

    def values(ref, oth, b):
        return ordered(ref[mine + b].astype(F32), oth[b].astype(F32))

    def both_decays(b):
        row = pl.ds(b // 2, 1)
        return ordered(decay_own[row, :], decay_oth[row, :])

    def build(u, _):
        i = u // 2
        theirs = lax.rem(u, 2) == 0
        for copy in loads(group_of(u)):
            copy.wait()
        group_states(group_of(u))

        @pl.when(u == 0)
        def _():
            pl.semaphore_wait(barrier, chips + shard_count)
            close_swap.start()

        @pl.when(theirs)
        def _():
            for copy in swaps(i):
                copy.start()

        @pl.when(u == 1)
        def _():
            close_swap.wait_recv()
            close_out[...] = close_own[...] + close_oth[...]
            decay_own[...] = held_decays(close_own)
            decay_oth[...] = held_decays(close_oth)
            close_in[chip] = close_out[...]

            def send(r, _):
                close_copy(r).start()
                return 0

            lax.fori_loop(1, chips, send, 0)

        @pl.when(jnp.logical_not(theirs))
        def _():
            for copy in swaps(i):
                copy.wait_recv()

            def combine(r, _):
                q = beside(r)
                for k in range(4):
                    b = chips * i + 4 * q + k
                    a0, a1 = both_decays(b)
                    s0, s1 = values(s_own, s_oth, b)
                    g0, g1 = values(g_own, g_oth, b)
                    sg_out[i, q, k, 0] = (a1 * s0 + s1).astype(BF16)
                    sg_out[i, q, k, 1] = (a0 * g1 + g0).astype(BF16)

                @pl.when(r > 0)
                def _():
                    sg_copy(i, r).start()

                return 0

            lax.fori_loop(0, 4, combine, 0)
            sg_in[i, y] = sg_out[i, y]

        return 0

    lax.fori_loop(0, 2 * BATCHES, build, 0)

    def inside(n, _):
        g = n // 2
        back = lax.rem(HEADS - 8 * n, HEADS)
        run = pltpu.roll(run_ref[...], back, 1)
        steps = pltpu.roll(sp_ref[...], back, 1)
        for j in range(4):
            lanes = tile(512 * n + 128 * j)
            dy = dy_ref[:, lanes].astype(F32)
            split = jnp.concatenate([jnp.where(low, dy, 0.0), jnp.where(low, 0.0, dy)], axis=0).astype(BF16)
            d_weights = dot_nt(xm[:, lanes], split)
            weights = []
            gathered = jnp.zeros(shape, F32)
            for i in range(2):
                head = 2 * j + i
                at = pl.ds(8 * n + head, 1)
                step = steps[:, head : head + 1]
                d_weight = d_weights[:, 128 * i : 128 * i + 128]
                decay = jnp.exp(jnp.minimum(run_t_ref[at, :] - run[:, head : head + 1], 0.0))
                plain = decay * scores[g]
                weights.append((plain * step).astype(BF16))
                product = d_weight * plain
                col_s[:, head : head + 1] = jnp.sum(product, axis=1, keepdims=True)
                sum_r[at, :] = jnp.sum(product * step, axis=0, keepdims=True)
                gathered = gathered + d_weight * decay * step
            dsc[g] += gathered
            dxi[:, lanes] = dot(jnp.concatenate(weights, axis=1), split).astype(BF16)
        kept = jnp.where(iota(shape, 1) < 8, col_s[...], 0.0)
        sum_s[...] += pltpu.roll(kept, lax.rem(8 * n, HEADS), 1)
        return 0

    def row_totals(i):
        @pl.when(i == 0)
        def _():
            def known(r, _):
                close_copy(r).wait_recv()
                return 0

            lax.fori_loop(1, chips, known, 0)

        closing = close_in[:, 0, :]
        by_row = [jnp.sum(closing[4 * q : 4 * q + 4], axis=0, keepdims=True) for q in range(4)]
        by_row = jnp.concatenate(by_row + [jnp.zeros((4, HEADS), F32)], axis=0)
        for p in range(2):
            pair = (mine + chips * i + 4 * y) // 2 + p
            decay_in[i, p] = spread_pairs(closing, pair)
            decay_row[i, p] = spread_pairs(by_row, pair)
        for r in range(1, 4):
            sg_copy(i, r).wait_recv()
        for k in range(4):
            forth = jnp.zeros((BLOCK_ROWS, 128), F32)
            back = forth
            for c in range(4):
                d = 3 - c
                forth = decay_in[i, k // 2, pl.ds(4 * z + c, 1), :] * forth + sg_in[i, c, k, 0].astype(F32)
                back = decay_in[i, k // 2, pl.ds(4 * z + d, 1), :] * back + sg_in[i, d, k, 1].astype(F32)
            row_out[i, k, 0] = forth.astype(BF16)
            row_out[i, k, 1] = back.astype(BF16)
        for r in range(1, 4):
            row_copy(i, r).start()
        row_in[i, z] = row_out[i]

    def scan(i):
        for r in range(1, 4):
            row_copy(i, r).wait_recv()
        for k in range(4):
            forth = jnp.zeros((BLOCK_ROWS, 128), F32)
            back = forth
            for q in range(4):
                d = 3 - q
                step = decay_row[i, k // 2, q : q + 1, :] * forth + row_in[i, q, k, 0].astype(F32)
                forth = jnp.where(q < z, step, forth)
                step = decay_row[i, k // 2, d : d + 1, :] * back + row_in[i, d, k, 1].astype(F32)
                back = jnp.where(d > z, step, back)
            for c in range(4):
                d = 3 - c
                hl_out[i, c, k, 0] = forth.astype(BF16)
                hl_out[i, d, k, 1] = back.astype(BF16)
                forth = decay_in[i, k // 2, pl.ds(4 * z + c, 1), :] * forth + sg_in[i, c, k, 0].astype(F32)
                back = decay_in[i, k // 2, pl.ds(4 * z + d, 1), :] * back + sg_in[i, d, k, 1].astype(F32)
        for r in range(1, 4):
            hl_copy(i, r).start()
        hl_in[i, y] = hl_out[i, y]

    def middle(i, _):
        lax.fori_loop(jnp.maximum(SLICE * (i - 1) + FIRST, 0), SLICE * i + FIRST, inside, 0)

        @pl.when(i < BATCHES)
        def _():
            row_totals(i)

        @pl.when(i > 0)
        def _():
            scan(i - 1)

        return 0

    lax.fori_loop(0, BATCHES, middle, 0)
    lax.fori_loop(SLICE * (BATCHES - 1) + FIRST, PAIRS // 4, inside, 0)

    ones[...] = jnp.where(iota(ones.shape, 0) // HEAD_DIM == iota(ones.shape, 1), 1.0, 0.0).astype(BF16)
    dpad[:, ROWS:, :] = jnp.zeros((GROUP_PAIRS + 2, 8, 128), F32)
    taps[...] = jnp.zeros(taps.shape, F32)
    for ref in (full_u, full_q, full_g, row_g):
        ref[...] = jnp.zeros(ref.shape, F32)

    def conv_back(slot, grad, lanes):
        here = padded(slot, lanes)
        there = dpad.at[slot]
        dpre = grad * slope[:, lanes]
        there[0:ROWS, :] = dpre
        whole = jnp.zeros(shape, F32)
        for k in range(KERNEL):
            whole = whole + weight_ref[k : k + 1, lanes] * there[3 - k : 3 - k + ROWS, :]
            taps[k : k + 1, lanes] = jnp.sum(dpre * here[5 + k : 5 + k + ROWS, :], axis=0, keepdims=True)
        taps[4:5, lanes] = jnp.sum(dpre, axis=0, keepdims=True)
        ig_ref[:, lanes] = whole.astype(BF16)
        last[:, lanes] = whole[ROWS - 16 :, :]
        edge = dpre[0:8, :]
        row = iota((8, 128), 0)
        spilled = jnp.zeros((8, 128), F32)
        for k in range(KERNEL - 1):
            moved = pltpu.roll(edge, 5 + k, 0)
            spilled = spilled + jnp.where(row >= 5 + k, weight_ref[k : k + 1, lanes] * moved, 0.0)
        spill[:, lanes] = spilled

    before = lax.rem(ctx + devices - 1, devices)

    def spill_copies(g):
        return [
            remote(spill.at[:, lanes], spill_in.at[:, lanes], sp_send.at[g, n], sp_recv.at[g, n], before)
            for n, lanes in enumerate(group_lanes(g))
        ]

    def group_grads(g):
        back = lax.rem(HEADS - GROUP_HEADS * g, HEADS)
        b16, c16 = bm[g], cm[g]
        gain = pltpu.roll(jnp.broadcast_to(gain_ref[...], (8, HEADS)), back, 1)
        for j in range(GROUP_PAIRS):
            lanes = tile(GROUP_LANES * g + 128 * j)
            here = pl.ds(128 * j, 128)
            at = pl.ds(2 * (GROUP_PAIRS * g + j), 2)
            x = xm[:, lanes].astype(F32)
            dy = dy_ref[:, lanes].astype(F32)
            h16 = h_all[at].reshape(STATE, 128)
            l16 = l_all[at].reshape(STATE, 128)
            left = dot(b16, l16)
            ent[:, here] = (dy * dot(c16, h16)).astype(BF16)
            use[:, here] = (x * left).astype(BF16)
            row_g[0:1, here] = jnp.sum(h16.astype(F32) * l16.astype(F32), axis=0, keepdims=True)
            row_g[1:2, here] = jnp.sum(dy * x, axis=0, keepdims=True)
            grad_x = dxi[:, lanes].astype(F32) + close[:, lanes] * left + pair_of(gain, j)[0:1, :] * dy
            conv_back(j, grad_x, lanes)
        d_scores = jnp.where(iota(shape, 1) >= iota(shape, 0), dsc[g], 0.0)
        channels = group_lanes(g)[0]

        def side_by_side(ref):
            ats = [pl.ds(2 * (GROUP_PAIRS * g + j), 2) for j in range(GROUP_PAIRS)]
            return jnp.concatenate([ref[at].reshape(STATE, 128) for at in ats], axis=1)

        grad_b = dot_nt(xc[:, channels], side_by_side(l_all)) + dot(d_scores.astype(BF16), c16)
        grad_c = dot_nt(dyg[:, channels], side_by_side(h_all)) + dot(d_scores.T.astype(BF16), b16)
        for i, grad in enumerate((grad_b, grad_c)):
            lanes = tile(INNER + GROUPS * STATE * i + STATE * g)
            conv_back(GROUP_PAIRS + i, grad, lanes)
        forward = lax.rem(GROUP_HEADS * g, HEADS)
        full_u[...] += pltpu.roll(dot(ent[...], ones[...]), forward, 1)
        full_q[...] += pltpu.roll(dot(use[...], ones[...]), forward, 1)
        rest = row_g[...]
        thirds = []
        for _ in range(3):
            part = rest.astype(BF16)
            thirds.append(part.astype(F32))
            rest = rest - thirds[-1]
        sums = dot(jnp.concatenate(thirds, axis=0).astype(BF16), ones[...])
        full_g[...] += pltpu.roll(sums[0:8] + sums[8:16] + sums[16:24], forward, 1)

        for copy in stores(g):
            copy.start()

        @pl.when(ctx > 0)
        def _():
            for copy in spill_copies(g):
                copy.start()

    def gather(i):
        def finish(r, _):
            q = lax.rem(y + 4 - r, 4)

            @pl.when(r > 0)
            def _():
                hl_copy(i, r).wait_recv()

            for k in range(4):
                b = chips * i + 4 * q + k
                a0, a1 = both_decays(b)
                s0, _ = values(s_own, s_oth, b)
                _, g1 = values(g_own, g_oth, b)
                h0 = hl_in[i, q, k, 0]
                h1 = (a0 * h0.astype(F32) + s0).astype(BF16)
                l1 = hl_in[i, q, k, 1]
                l0 = (a1 * l1.astype(F32) + g1).astype(BF16)
                h_all[mine + b] = jnp.where(first, h0, h1)
                h_oth[b] = jnp.where(first, h1, h0)
                l_all[mine + b] = jnp.where(first, l0, l1)
                l_oth[b] = jnp.where(first, l1, l0)
            return 0

        lax.fori_loop(0, 4, finish, 0)
        for copy in swap_back(i):
            copy.start()

    def outer(u, _):
        i = u // 2
        held = lax.rem(u, 2) == 0

        @pl.when(u == 1)
        def _():
            scan(BATCHES - 1)

        @pl.when(held)
        def _():
            gather(i)

        @pl.when(jnp.logical_not(held))
        def _():
            for copy in swap_back(i):
                copy.wait_recv()

        group_grads(jnp.where(held, mine_group, theirs_group) + i)
        return 0

    lax.fori_loop(0, 2 * BATCHES, outer, 0)

    width = total.shape[1]
    half = width // 2

    def columns(shard, part):
        return pl.ds(pl.multiple_of(shard * (2 * width) + part * width, 128), width)

    sums = [
        remote(taps.at[:, columns(i, 1 - core)], taps_oth.at[i], t_send.at[i], t_recv.at[i], other)
        for i in range(shard_count)
    ]
    for copy in sums:
        copy.start()

    closing = run_ref[ROWS - 1 : ROWS, :]
    running = run_ref[...]
    steps = sp_ref[...]
    direct_q = jnp.exp(closing - running) * full_q[...]
    used_q = direct_q * steps
    summed = sum_r[...].T + jnp.exp(running) * full_u[...] - sum_s[...] * steps - used_q
    upper = jnp.where(iota(shape, 1) >= iota(shape, 0), 1.0, 0.0).astype(F32)
    constant = jnp.sum(used_q, axis=0, keepdims=True) + jnp.exp(closing) * full_g[0:1, :]
    d_logs = dot(upper, summed, EXACT) + constant
    d_spread = (d_logs * (-jnp.exp(decay_ref[...])) + sum_s[...] + direct_q).astype(BF16).astype(F32)
    step_grad = d_spread * sigmoid(raw_ref[...].astype(F32) + bias_ref[...])
    step_ref[...] = step_grad
    rows[...] = jnp.zeros((8, HEADS), F32)
    rows[0:1, :] = -jnp.exp(decay_ref[...]) * jnp.sum(d_logs * steps, axis=0, keepdims=True)
    rows[1:2, :] = jnp.sum(step_grad, axis=0, keepdims=True)
    rows[2:3, :] = full_g[1:2, :]

    rows_sum = remote(rows, rows_oth, t_send.at[shard_count], t_recv.at[shard_count], other)
    rows_sum.start()
    for copy in sums + [rows_sum]:
        copy.wait()
    for i in range(shard_count):
        shards[i, :, 0:width] = taps[:, columns(i, core)] + taps_oth[i]
        shards[i, :, width:] = rows[...] + rows_oth[...]

    def shard_copy(r):
        return remote(shards.at[dp_at(r)], arrived.at[r], d_send.at[r], d_recv.at[r], ctx, dp_at(r))

    for r in range(1, shard_count):
        shard_copy(r).start()

    @pl.when(ctx < devices - 1)
    def _():
        def landed(g, _):
            for copy in spill_copies(g):
                copy.wait_recv()
            return 0

        lax.fori_loop(0, GROUPS, landed, 0)
        last[8:16, :] += spill_in[...]

    ig_ref[ROWS - 16 :, :] = last[...].astype(BF16)
    bottom = pl.ds(ROWS - 16, 16)
    last_store = pltpu.make_async_copy(ig_ref.at[bottom], ig_hbm.at[bottom], last_sem.at[0])
    last_store.start()

    summed = shards[dp]
    for r in range(1, shard_count):
        shard_copy(r).wait()
        summed = summed + arrived[r]
    flat[0:4, 0:half] = summed[0:4, 0:half]
    flat[4:8, 0:half] = summed[0:4, half:width]
    flat[8:9, 0:half] = summed[4:5, 0:half]
    flat[9:10, 0:half] = summed[4:5, half:width]
    flat[10:16, 0:half] = jnp.zeros((6, half), F32)
    flat[0:8, half:] = summed[:, width:]
    flat[8:16, half:] = jnp.zeros((8, 128), F32)
    packed[...] = flat[...].astype(BF16)

    def chip_copy(r):
        return remote(packed, packed_in.at[r], c_send.at[r], c_recv.at[r], chip_at(r) * 2 + core)

    def send(r, _):
        chip_copy(r).start()
        return 0

    lax.fori_loop(1, chips, send, 0)

    close_swap.wait_send()
    last_store.wait()

    def stored(g, _):
        for copy in stores(g):
            copy.wait()
        return 0

    lax.fori_loop(0, GROUPS, stored, 0)

    def cleared(i, _):
        for copy in swaps(i) + swap_back(i):
            copy.wait_send()

        def sent(r, _):
            @pl.when(i == 0)
            def _():
                close_copy(r).wait_send()

            @pl.when(r < 4)
            def _():
                sg_copy(i, r).wait_send()
                row_copy(i, r).wait_send()
                hl_copy(i, r).wait_send()

            return 0

        lax.fori_loop(1, chips, sent, 0)
        return 0

    lax.fori_loop(0, BATCHES, cleared, 0)

    @pl.when(ctx > 0)
    def _():
        def left_here(g, _):
            for copy in spill_copies(g):
                copy.wait_send()
            return 0

        lax.fori_loop(0, GROUPS, left_here, 0)

    def take(r, _):
        chip_copy(r).wait()
        flat[...] += packed_in[r].astype(F32)
        return 0

    lax.fori_loop(1, chips, take, 0)
    total[0:4, 0:half] = flat[0:4, 0:half]
    total[0:4, half:] = flat[4:8, 0:half]
    total[4:5, 0:half] = flat[8:9, 0:half]
    total[4:5, half:] = flat[9:10, 0:half]
    total[5:8, :] = jnp.zeros((3, width), F32)
    final = remote(total, total_oth, o_send.at[0], o_recv.at[0], other)
    final.start()
    head_ref[...] = pltpu.roll(flat[0:8, half:], lax.rem(HEADS - (HEADS // shard_count) * dp, HEADS), 1)
    conv_ref[:, pl.ds(pl.multiple_of(core * width, 128), width)] = total[...]
    final.wait()
    conv_ref[:, pl.ds(pl.multiple_of((1 - core) * width, 128), width)] = total_oth[...]


def mixer_grads(mixer, halo, weight, shift, raw, bias, decay, gain, dy):
    chips = lax.axis_size("ctx") // 2
    shards = lax.axis_size("dp")
    width = CONV // shards // 2
    V = pltpu.VMEM
    dma = pltpu.SemaphoreType.DMA
    blocks = PAIRS * STATE // BLOCK_ROWS
    plane = V((ROWS, HEADS), F32)
    row = V((8, HEADS), F32)
    tall = V((GROUP_PAIRS + 2, ROWS + 8, 128), F32)
    group16 = V((GROUPS, ROWS, STATE), BF16)
    group32 = V((GROUPS, ROWS, ROWS), F32)
    inner = V((ROWS, INNER), BF16)
    whole = V((blocks, BLOCK_ROWS, 128), BF16)
    part = V((blocks // 2, BLOCK_ROWS, 128), BF16)
    sent = V((BATCHES, 4, 4, 2, BLOCK_ROWS, 128), BF16)
    edge = V((8, CONV), F32)
    memory = pl.BlockSpec(memory_space=pltpu.VMEM)
    remote_memory = pl.BlockSpec(memory_space=pl.ANY)
    return pl.pallas_call(
        mixer_kernel,
        out_shape=[
            jax.ShapeDtypeStruct((ROWS, CONV), BF16), jax.ShapeDtypeStruct((ROWS, HEADS), F32),
            jax.ShapeDtypeStruct((8, 2 * width), F32), jax.ShapeDtypeStruct((8, HEADS), F32),
        ],
        in_specs=[remote_memory] + [memory] * 7 + [remote_memory],
        out_specs=[remote_memory] + [memory] * 3,
        scratch_shapes=[
            V((ROWS, CONV), BF16), inner, V((ROWS, CONV), BF16), V((ROWS, CONV), F32), plane, plane, plane, row, row, row, V((chips, 8, HEADS), F32),
            V((HALF, 128), F32), V((HALF, 128), F32),
            V((BATCHES, 2, chips, 128), F32), V((BATCHES, 2, 8, 128), F32), tall, tall,
            inner, group16, group16, group32, inner, group32, plane, plane, whole, whole, part, part,
            sent, sent, sent, sent, V((BATCHES, 4, 2, BLOCK_ROWS, 128), BF16), sent, whole, whole, part, part, plane,
            inner, inner, V((ROWS, INNER), F32), V((GROUP_LANES, 128), BF16),
            V((ROWS, GROUP_LANES), BF16), V((ROWS, GROUP_LANES), BF16), V((8, GROUP_LANES), F32), plane, plane, row,
            V((16, CONV), F32), edge, edge, edge, row,
            V((shards, 8, width), F32), row, V((shards, 8, width + 128), F32), V((shards, 8, width + 128), F32),
            V((16, width // 2 + 128), F32), V((16, width // 2 + 128), BF16),
            V((chips, 16, width // 2 + 128), BF16), V((8, width), F32), V((8, width), F32),
            dma((1,)), dma((1,)), dma((chips,)), dma((chips,)),
        ]
        + [dma((BATCHES,))] * 4 + [dma((BATCHES, 4))] * 6 + [dma((BATCHES,))] * 4
        + [dma((GROUPS, 3))] * 2 + [dma((shards + 1,))] * 2 + [dma((shards,))] * 2 + [dma((chips,))] * 2 + [dma((1,))] * 2
        + [dma((GROUPS, 4)), dma((GROUPS, 3)), dma((1,))],
        compiler_params=pltpu.CompilerParams(
            collective_id=0, has_side_effects=True, vmem_limit_bytes=VMEM
        ),
        name="mixer_grads",
    )(mixer, halo, weight, shift, raw, bias, decay, gain, dy)


def finish_kernel(factor, ig_ref, step_ref, conv_ref, head_ref, ig_out, step_out, conv_out, head_out, gain_out):
    ig_out[...] = ig_ref[...]

    @pl.when(pl.program_id(0) == 0)
    def _():
        step_out[...] = step_ref[...]
        conv_out[...] = conv_ref[0 : KERNEL + 1, :] * factor
        head_out[...] = head_ref[0:2, 0 : head_out.shape[1]] * factor
        gain_out[...] = head_ref[2:3, 0 : gain_out.shape[1]] * factor


def finish(factor, input_grad, step_grad, conv, head):
    heads = HEADS // lax.axis_size("dp")
    block = pl.BlockSpec((ROWS // FINISH_PARTS, CONV), lambda i: (i, 0))

    def full(shape):
        return pl.BlockSpec(shape, lambda i: (0,) * len(shape))

    return pl.pallas_call(
        functools.partial(finish_kernel, factor),
        grid=(FINISH_PARTS,),
        in_specs=[block, full(step_grad.shape), full(conv.shape), full(head.shape)],
        out_specs=[block, full(step_grad.shape), full((KERNEL + 1, conv.shape[1])), full((2, heads)), full((1, heads))],
        out_shape=[
            jax.ShapeDtypeStruct((ROWS, CONV), BF16), jax.ShapeDtypeStruct((ROWS, HEADS), F32),
            jax.ShapeDtypeStruct((KERNEL + 1, conv.shape[1]), F32),
            jax.ShapeDtypeStruct((2, heads), F32), jax.ShapeDtypeStruct((1, heads), F32),
        ],
        compiler_params=pltpu.CompilerParams(vmem_limit_bytes=VMEM),
        name="finish",
    )(input_grad, step_grad, conv, head)


def passed_along(value, axis, steps):
    count = lax.axis_size(axis)
    initial, last = (max(0, -steps), min(count, count - steps))
    return lax.ppermute(value, axis, [(source, source + steps) for source in range(initial, last)])


def local(mixer_input, step_raw, out_grad, conv_weight, conv_bias, step_bias, decay_log, skip_gain):
    mixer, raw, dy = mixer_input[0], step_raw[0], out_grad[0]
    halo = passed_along(mixer[ROWS - 8 :], "ctx", 1)
    input_grad, step_grad, conv, head = mixer_grads(
        mixer, halo, conv_weight, conv_bias[None], raw, step_bias[None], decay_log[None], skip_gain[None], dy
    )
    factor = 1.0 / math.sqrt(lax.axis_size("dp") * ROWS * lax.axis_size("ctx"))
    input_grad, step_grad, conv, head, gain = finish(factor, input_grad, step_grad, conv, head)
    return input_grad[None], step_grad[None], conv, head, gain[0]


def solution(mesh):
    spread = P("dp", "ctx", None)
    in_specs = (spread, spread, spread, P(), P(), P(), P(), P())
    out_specs = (spread, spread, P(None, "dp"), P(None, "dp"), P("dp"))
    return jax.shard_map(local, mesh=mesh, in_specs=in_specs, out_specs=out_specs, check_vma=False)
```
